32 devices in a mesh: section: 2 (over x), fsdp: 16 (over z, y, core).
Axes of the slice: x: 2, y: 2, z: 4, core: 2. Of those that a mesh axis runs over, the one named last changes fastest.
Arguments:
- block_input: bfloat16 [2, 4096, 1024], P(None, 'fsdp'), may hold values from -6 to 6
- output_grad: bfloat16 [2, 4096, 1024], P(None, 'fsdp'), may hold values from -6 to 6
- document_ids: int32 [2, 4096], P(None, 'fsdp'), may hold values from 0 to 63, never falling along the last dimension, each value on 1 to 128 neighbouring positions
- memory_keys: bfloat16 [2, 16384, 1024], P(None, 'fsdp'), may hold values from -6 to 6
- memory_values: bfloat16 [2, 16384, 1024], P(None, 'fsdp'), may hold values from -6 to 6
- memory_index: int32 [2, 64, 128], P(None, 'fsdp'), may hold values from 0 to 1023
- memory_reset: int32 [2, 64], P(None, 'fsdp'), may hold values 0 or 1
- query_weight: bfloat16 [2, 1024, 1024], P('section', 'fsdp'), may hold values from -0.1875 to 0.1875
- key_weight: bfloat16 [2, 1024, 1024], P('section', 'fsdp'), may hold values from -0.1875 to 0.1875
- value_weight: bfloat16 [2, 1024, 1024], P('section', 'fsdp'), may hold values from -0.1875 to 0.1875
- output_weight: bfloat16 [2, 1024, 1024], P('section', 'fsdp'), may hold values from -1 to 1
- gate_weight: bfloat16 [2, 1024, 2816], P('section', 'fsdp'), may hold values from -0.1875 to 0.1875
- up_weight: bfloat16 [2, 1024, 2816], P('section', 'fsdp'), may hold values from -0.1875 to 0.1875
- down_weight: bfloat16 [2, 2816, 1024], P('section', 'fsdp'), may hold values from -0.109375 to 0.109375
- attend_gain: bfloat16 [2, 1024], P('section', 'fsdp'), may hold values from 0.099609375 to 1.8984375
- feed_gain: bfloat16 [2, 1024], P('section', 'fsdp'), may hold values from 0.099609375 to 1.8984375
Outputs:
- section_output: bfloat16 [2, 2, 4096, 1024], P('section', None, 'fsdp')
- input_grad: bfloat16 [2, 2, 4096, 1024], P('section', None, 'fsdp')
- grad_query: bfloat16 [2, 1024, 1024], P('section', 'fsdp')
- grad_key: bfloat16 [2, 1024, 1024], P('section', 'fsdp')
- grad_value: bfloat16 [2, 1024, 1024], P('section', 'fsdp')
- grad_output: bfloat16 [2, 1024, 1024], P('section', 'fsdp')
- grad_gate: bfloat16 [2, 1024, 2816], P('section', 'fsdp')
- grad_up: bfloat16 [2, 1024, 2816], P('section', 'fsdp')
- grad_down: bfloat16 [2, 2816, 1024], P('section', 'fsdp')
- grad_attend: bfloat16 [2, 1024], P('section', 'fsdp')
- grad_feed: bfloat16 [2, 1024], P('section', 'fsdp')
The draws below stay inside these ranges and needn't reach their ends.
Inputs may be any that keep to these rules, and one draw needn't show every extreme that they name: `memory_index`: indices into the sequence's own 1024 cache rows. `document_ids`: never falling along a micro-batch's tokens.
All inputs are finite; a program needn't handle non-finite values. No bound on the sum of `memory_reset` on one device may be relied on, other than what follows from the above.
Results may differ from the reference program's by a relative error of at most 0.02.
Values may be sent and summed in bfloat16 or wider, within the bound.
A program may use at most 256 MiB of HBM per device.

```python
import math
import jax
import jax.numpy as jnp
import numpy as np
from jax import lax

D = 1024
HEADS = 8
HD = 128
FF = 2816
TOK_DEV = 256
MICRO = 2
CACHE = 1024
MQB = 64
MEMK = 128
NBLK = 4
TOKENS_MB = 4096
LAYERS = 2
N_FSDP = 16


def with_ends(values, own_key, low, high):
    dims = values.shape
    index_at = [jax.random.randint(jax.random.fold_in(own_key, axis), (), 0, dims[axis]) for axis in range(len(dims))]
    values = values.at[tuple(index_at)].set(low)
    longest = dims.index(max(dims))
    index_at[longest] = (index_at[longest] + 1) % dims[longest]
    return values.at[tuple(index_at)].set(high)


def level_of(rng, extent, split, smallest, high):
    factor_of = 1.0
    for axis_at, shards_of in split:
        heights = jax.random.uniform(jax.random.fold_in(jax.random.fold_in(rng, 6), axis_at), (shards_of,), jnp.float32, smallest / len(split), high / len(split))
        factor_of = factor_of * jnp.repeat(jnp.exp(heights), extent[axis_at] // shards_of).reshape((-1,) + (1,) * (len(extent) - 1 - axis_at))
    return factor_of


def split_up(number_of, total, bound, lean):
    weights = [(1 << 20) // math.isqrt(standing ** lean) + 1 for standing in range(2, number_of + 1)]
    spare, counts = total - bound - (number_of - 1), [1] * (number_of - 1)
    while spare > 0:
        free = [i for i in range(number_of - 1) if counts[i] < bound]
        whole, left = sum([weights[i] for i in free]), spare
        for i in free:
            extra = min(bound - counts[i], max(1, left * weights[i] // whole), spare)
            counts[i] = counts[i] + extra
            spare = spare - extra
    return np.array([bound] + counts)


def uneven(stream_key, amount, total, reach, lean):
    if amount == 2:
        one = jax.random.randint(stream_key, (), max(1, total - reach), min(reach, total - 1) + 1)
        return jnp.stack([one, total - one])
    sizes = jnp.asarray(split_up(amount, total, reach, lean), jnp.int32)
    pairs = (amount - 1) // 2
    source_of, sink = sizes[1:1 + 2 * pairs:2], sizes[2:2 + 2 * pairs:2]
    margin = jnp.minimum(source_of - 1, reach - sink)
    passed = jax.random.randint(jax.random.fold_in(stream_key, 1), (pairs,), 0, 1 << 20) % (margin + 1)
    sizes = sizes.at[1:1 + 2 * pairs:2].set(source_of - passed).at[2:2 + 2 * pairs:2].set(sink + passed)
    return sizes[jax.random.permutation(jax.random.fold_in(stream_key, 2), amount)]


def scatter_about(stream_key, extent, deviation, bound, cuts=(), kind=jnp.bfloat16):
    entries = jax.random.normal(stream_key, extent, jnp.float32) * deviation
    if len(cuts) > 0:
        entries = level_of(stream_key, extent, cuts, -0.22, 0.18) * entries
    return jnp.clip(entries, min=-bound, max=bound).astype(kind)


def setup_inputs(seed: int = 0) -> dict:
    key_list = jax.random.split(jax.random.key(seed), 17)
    block_input = scatter_about(key_list[0], (MICRO, TOKENS_MB, D), 1.0, 6.0, ((1, 16),))
    output_grad = scatter_about(key_list[1], (MICRO, TOKENS_MB, D), 1.0, 6.0, ((1, 16),))
    document_ids = jax.vmap(lambda own: jnp.searchsorted(jnp.cumsum(uneven(own, 4 * N_FSDP, TOKENS_MB, TOK_DEV // 2, 1)), jnp.arange(TOKENS_MB), side="right"))(jax.random.split(key_list[2], MICRO)).reshape((MICRO, TOKENS_MB)).astype(jnp.int32)
    memory_keys = scatter_about(key_list[3], (MICRO, N_FSDP * CACHE, D), 1.0, 6.0, ((1, 16),))
    memory_values = scatter_about(key_list[4], (MICRO, N_FSDP * CACHE, D), 1.0, 6.0, ((1, 16),))
    memory_index = with_ends(jax.random.randint(key_list[5], (MICRO, N_FSDP * NBLK, MEMK), 0, CACHE), jax.random.fold_in(key_list[5], 1), 0, CACHE - 1).astype(jnp.int32)
    memory_reset = with_ends((jax.random.randint(key_list[6], (MICRO, N_FSDP * NBLK), 0, 4) < 1).astype(jnp.int32), jax.random.fold_in(key_list[6], 1), 0, 1)
    query_weight = scatter_about(key_list[7], (LAYERS, D, D), D ** -0.5, 0.1875, ((0, 2), (1, 16)))
    key_weight = scatter_about(key_list[8], (LAYERS, D, D), D ** -0.5, 0.1875, ((0, 2), (1, 16)))
    value_weight = scatter_about(key_list[9], (LAYERS, D, D), D ** -0.5, 0.1875, ((0, 2), (1, 16)))
    output_weight = scatter_about(key_list[10], (LAYERS, D, D), (D // 32) ** -0.5, 1.0, ((0, 2), (1, 16)))
    gate_weight = scatter_about(key_list[11], (LAYERS, D, FF), D ** -0.5, 0.1875, ((0, 2), (1, 16)))
    up_weight = scatter_about(key_list[12], (LAYERS, D, FF), D ** -0.5, 0.1875, ((0, 2), (1, 16)))
    down_weight = scatter_about(key_list[13], (LAYERS, FF, D), FF ** -0.5, 0.109375, ((0, 2), (1, 16)))
    attend_gain = jnp.clip(1.0 + 0.18 * jax.random.normal(key_list[14], (LAYERS, D), jnp.float32), 0.099609375, 1.8984375).astype(jnp.bfloat16)
    feed_gain = jnp.clip(1.0 + 0.18 * jax.random.normal(key_list[15], (LAYERS, D), jnp.float32), 0.099609375, 1.8984375).astype(jnp.bfloat16)
    return dict(block_input=block_input, output_grad=output_grad, document_ids=document_ids, memory_keys=memory_keys, memory_values=memory_values, memory_index=memory_index, memory_reset=memory_reset, query_weight=query_weight, key_weight=key_weight, value_weight=value_weight, output_weight=output_weight, gate_weight=gate_weight, up_weight=up_weight, down_weight=down_weight, attend_gain=attend_gain, feed_gain=feed_gain)


@jax.custom_vjp
def low(v):
    return lax.optimization_barrier(v.astype(jnp.bfloat16)).astype(jnp.float32)

@jax.custom_vjp
def low_back(v):
    return v

def low_keep(v):
    return (low(v), None)

def low_pass(kept, grad):
    return (grad,)

def back_keep(v):
    return (v, None)

def back_low(kept, grad):
    return (low(grad),)
low.defvjp(low_keep, low_pass)
low_back.defvjp(back_keep, back_low)
EPS = 1e-06
MASKED = -1e+30
HIGH = lax.Precision.HIGHEST

def product(left, right):
    return jnp.dot(left, right, precision=HIGH, preferred_element_type=jnp.float32)

def normalize(rows, gain):
    return rows * lax.rsqrt(lax.optimization_barrier(jnp.mean(rows * rows, axis=-1, keepdims=True)) + EPS) * gain

def one_layer(params, inputs, documents, cache_keys, cache_values, picks, resets, recalls):
    query_weight, key_weight, value_weight, output_weight, gate_weight, up_weight, down_weight, attend_gain, feed_gain = params
    rows = inputs.shape[0]
    blocks = rows // MQB
    scale = HD ** (-0.5)
    normed = low(normalize(inputs, attend_gain))
    queries = low_back(low(product(normed, query_weight))).reshape(rows, HEADS, HD)
    keys = low_back(low(product(normed, key_weight))).reshape(rows, HEADS, HD)
    values = low_back(low(product(normed, value_weight))).reshape(rows, HEADS, HD)
    local = jnp.einsum('qhd,khd->hqk', queries, keys, precision=HIGH) * scale
    position = jnp.arange(rows)
    allowed = (position[None, :] <= position[:, None]) & (documents[None, :] == documents[:, None])
    if recalls:
        flat = picks.reshape(-1)
        remote_keys = jnp.take(cache_keys, flat, axis=0).reshape(blocks, MEMK, HEADS, HD)
        remote_values = jnp.take(cache_values, flat, axis=0).reshape(blocks, MEMK, HEADS, HD)
        recalled = jnp.einsum('bqhd,bkhd->hbqk', queries.reshape(blocks, MQB, HEADS, HD), remote_keys, precision=HIGH) * scale
        recalled = recalled.reshape(HEADS, rows, MEMK)
        scores = low_back(jnp.concatenate([local, recalled], axis=-1))
        live = jnp.repeat(resets == 0, MQB)
        mask = jnp.concatenate([allowed, jnp.broadcast_to(live[:, None], (rows, MEMK))], axis=-1)
    else:
        scores = low_back(local)
        mask = allowed
    scores = jnp.where(mask[None], scores, MASKED)
    top = lax.optimization_barrier(jnp.max(scores, axis=-1, keepdims=True))
    raised = jnp.exp(scores - top)
    probs = low(raised / lax.optimization_barrier(jnp.sum(raised, axis=-1, keepdims=True)))
    mixed = jnp.einsum('hqk,khd->qhd', probs[:, :, :rows], values, precision=HIGH)
    if recalls:
        memory_probs = probs[:, :, rows:].reshape(HEADS, blocks, MQB, MEMK)
        mixed = mixed + jnp.einsum('hbqk,bkhd->bqhd', memory_probs, remote_values, precision=HIGH).reshape(rows, HEADS, HD)
    mixed = low_back(low(mixed.reshape(rows, D)))
    middle = inputs + low_back(product(mixed, output_weight))
    normed_two = low(normalize(middle, feed_gain))
    gate = low_back(product(normed_two, gate_weight))
    up = low_back(product(normed_two, up_weight))
    hidden = low(jax.nn.silu(gate) * up)
    return middle + low_back(product(hidden, down_weight))

def whole(params, inputs, documents, cache_keys, cache_values, picks, resets, recalls):
    count = inputs.shape[0]
    group = math.gcd(count, max(1, 4096 // TOK_DEV))

    def single(rows_in, docs_in, keys_in, values_in, picks_in, resets_in):
        return one_layer(params, rows_in, docs_in, keys_in, values_in, picks_in, resets_in, recalls)

    def run(pack):
        return jax.vmap(single)(*pack)
    packed = tuple((z.reshape((count // group, group) + z.shape[1:]) for z in (inputs, documents, cache_keys, cache_values, picks, resets)))
    result = lax.map(jax.checkpoint(run), packed)
    return result.reshape(inputs.shape)

def reference(block_input, output_grad, document_ids, memory_keys, memory_values, memory_index, memory_reset, query_weight, key_weight, value_weight, output_weight, gate_weight, up_weight, down_weight, attend_gain, feed_gain):
    count = MICRO * N_FSDP
    inputs = block_input.astype(jnp.float32).reshape(count, TOK_DEV, D)
    cotangent = output_grad.astype(jnp.float32).reshape(count, TOK_DEV, D)
    documents = document_ids.reshape(count, TOK_DEV)
    cache_keys = memory_keys.astype(jnp.float32).reshape(count, CACHE, D)
    cache_values = memory_values.astype(jnp.float32).reshape(count, CACHE, D)
    picks = memory_index.reshape(count, NBLK, MEMK)
    resets = memory_reset.reshape(count, NBLK)
    stacked = (query_weight, key_weight, value_weight, output_weight, gate_weight, up_weight, down_weight, attend_gain, feed_gain)
    first_params = tuple((w[0].astype(jnp.float32) for w in stacked))
    second_params = tuple((w[1].astype(jnp.float32) for w in stacked))

    def first(params, rows_in):
        return whole(params, rows_in, documents, cache_keys, cache_values, picks, resets, False)

    def second(params, rows_in):
        return whole(params, rows_in, documents, cache_keys, cache_values, picks, resets, True)
    between, first_back = jax.vjp(first, first_params, inputs)
    sent = low(between)
    final, second_back = jax.vjp(second, second_params, sent)
    second_grads, between_grad = second_back(cotangent)
    returned = low(between_grad)
    first_grads, first_input_grad = first_back(returned)
    shape = (MICRO, TOKENS_MB, D)
    section_output = jnp.stack([sent.reshape(shape), final.reshape(shape)]).astype(jnp.bfloat16)
    input_grad = jnp.stack([first_input_grad.reshape(shape), returned.reshape(shape)]).astype(jnp.bfloat16)
    grads = [jnp.stack([a, b]).astype(jnp.bfloat16) for a, b in zip(first_grads, second_grads)]
    return (section_output, input_grad, grads[0], grads[1], grads[2], grads[3], grads[4], grads[5], grads[6], grads[7], grads[8])
```

```python
import functools
import math
import jax
import jax.numpy as jnp
from jax import lax
from jax.experimental import pallas as pl
from jax.experimental.pallas import tpu as pltpu
from jax.sharding import PartitionSpec as P

MESH = pl.DeviceIdType.MESH


def layout(n):
    rest=n//2
    R=min(4,rest); C=rest//R
    return R,C

def gather_kernel(n, P, *refs):
    ins=refs[:P]; outs=refs[P:2*P]; bufs=refs[2*P:3*P]
    own_sem,out_sem,s_zu,s_zd,s_yu,s_yd,s_sb,s_ex,r_main,r_sib=refs[3*P:]
    R,C=layout(n)
    sec=lax.axis_index("section"); f=lax.axis_index("fsdp")
    c=f%2; zy=f//2; y=zy%C; z=zy//C
    def dev(zz,yy,cc): return (sec,(zz*C+yy)*2+cc)
    bar=pltpu.get_barrier_semaphore()
    nb=[(z>0,(z-1,y,c)),(z<R-1,(z+1,y,c)),(y>0,(z,y-1,c)),(y<C-1,(z,y+1,c)),(c>=0,(z,y,1-c))]
    for p in range(P):
        pltpu.make_async_copy(ins[p],bufs[p].at[f],own_sem.at[p]).start()
    for cond,d in nb:
        @pl.when(cond)
        def _():
            pl.semaphore_signal(bar,1,device_id=dev(*d),device_id_type=MESH)
    pl.semaphore_wait(bar,sum(jnp.where(cond,1,0) for cond,d in nb))
    pending=[]
    def send(cond,p,zb,yb,target,ssem,rsem):
        blk=(zb*C+yb)*2+c
        k=zb*C+yb
        def mk():
            return pltpu.make_async_remote_copy(bufs[p].at[blk],bufs[p].at[blk],ssem.at[p,k],rsem.at[p,k],device_id=dev(*target),device_id_type=MESH)
        @pl.when(cond)
        def _(): mk().start()
        pending.append((cond,mk))
    def wait_main(cond,p,zb,yb):
        blk=(zb*C+yb)*2+c; k=zb*C+yb
        @pl.when(cond)
        def _():
            pltpu.make_async_remote_copy(bufs[p].at[blk],bufs[p].at[blk],s_sb.at[p,k],r_main.at[p,k],device_id=dev(z,y,1-c),device_id_type=MESH).wait_recv()
    offload = (C==2)
    T=(c>=0)
    def own(p):
        pltpu.make_async_copy(ins[p],bufs[p].at[f],own_sem.at[p]).wait()
        send(y>0,p,z,y,(z,y-1,c),s_yd,r_main)
        send(y<C-1,p,z,y,(z,y+1,c),s_yu,r_main)
        send(z>0,p,z,y,(z-1,y,c),s_zd,r_main)
        send(z<R-1,p,z,y,(z+1,y,c),s_zu,r_main)
        send(T,p,z,y,(z,y,1-c),s_sb,r_sib)
    def z_arrivals(p):
        for d in range(1,R):
            for sign in (-1,1):
                zb=z+sign*d
                ok=(zb>=0)&(zb<R)
                zbc=jnp.clip(zb,0,R-1)
                wait_main(ok,p,zbc,y)
                if sign<0:
                    send(ok&(z<R-1),p,zbc,y,(z+1,y,c),s_zu,r_main)
                else:
                    send(ok&(z>0),p,zbc,y,(z-1,y,c),s_zd,r_main)
                ydo=ok
                if offload: ydo=ok & jnp.logical_not((c==1)&(zbc==(z+1-2*(z%2))))
                send(ydo&(y>0),p,zbc,y,(z,y-1,c),s_yd,r_main)
                send(ydo&(y<C-1),p,zbc,y,(z,y+1,c),s_yu,r_main)
                send(ok,p,zbc,y,(z,y,1-c),s_sb,r_sib)
    def y_arrivals(p, near):
        for dy in range(1,C):
            for sign in (-1,1):
                yb=y+sign*dy
                oky=(yb>=0)&(yb<C)
                ybc=jnp.clip(yb,0,C-1)
                for d in ([0] if near else range(1,R)):
                    for zs in ((0,) if d==0 else (-1,1)):
                        zb=z+zs*d
                        ok=oky&(zb>=0)&(zb<R)
                        zbc=jnp.clip(zb,0,R-1)
                        wait_main(ok,p,zbc,ybc)
                        if C>2:
                            if sign<0: send(ok&(y<C-1),p,zbc,ybc,(z,y+1,c),s_yu,r_main)
                            else: send(ok&(y>0),p,zbc,ybc,(z,y-1,c),s_yd,r_main)
                        if offload and d==0:
                            send(ok&(c==1),p,zbc,ybc,(z+1-2*(z%2),y,c),s_ex,r_main)
                        send(ok,p,zbc,ybc,(z,y,1-c),s_sb,r_sib)
    def finish(p):
        def body(k,_):
            blk=k*2+1-c
            pltpu.make_async_remote_copy(bufs[p].at[blk],bufs[p].at[blk],s_sb.at[p,k],r_sib.at[p,k],device_id=dev(z,y,1-c),device_id_type=MESH).wait_recv()
            return 0
        lax.fori_loop(0,n//2,body,0)
        pltpu.make_async_copy(bufs[p],outs[p],out_sem.at[p]).start()
    LA=2
    for p in range(min(LA,P)): own(p)
    for p in range(P+2):
        if p+LA<P: own(p+LA)
        if p<P: z_arrivals(p)
        if 0<=p-1<P: y_arrivals(p-1,True)
        if 0<=p-2<P:
            y_arrivals(p-2,False)
            finish(p-2)
    for cond,mk in pending:
        @pl.when(cond)
        def _(): mk().wait_send()
    for p in range(P):
        pltpu.make_async_copy(bufs[p],outs[p],out_sem.at[p]).wait()

def gather(n, shards, cid=0):
    P=len(shards)
    R,C=layout(n)
    h=n//2
    D=pltpu.SemaphoreType.DMA
    return pl.pallas_call(functools.partial(gather_kernel,n,P),
        out_shape=[jax.ShapeDtypeStruct((n,)+s.shape,s.dtype) for s in shards],
        in_specs=[pl.BlockSpec(memory_space=pltpu.HBM)]*P,
        out_specs=[pl.BlockSpec(memory_space=pltpu.HBM)]*P,
        scratch_shapes=[pltpu.VMEM((n,)+s.shape,s.dtype) for s in shards]+[D((P,)),D((P,))]+[D((P,h))]*8,
        compiler_params=pltpu.CompilerParams(collective_id=cid,has_side_effects=True,vmem_limit_bytes=60<<20),
    )(*shards)

HEADS=8; HD=128; MQB=64; MEMK=128; EPS=1e-06; MASKED=-1e30

def nn(a,b): return jnp.dot(a,b,preferred_element_type=jnp.float32)
def nt(a,b): return lax.dot_general(a,b,(((1,),(1,)),((),())),preferred_element_type=jnp.float32)
def tn(a,b): return lax.dot_general(a,b,(((0,),(0,)),((),())),preferred_element_type=jnp.float32)

def chain_kernel(n, micro, T, D, FF, CACHE, NBLK, *refs):
    it=iter(refs)
    take=lambda k:[next(it) for _ in range(k)]
    x_hbm,og_hbm,docs,mk_hbm,mv_hbm,midx,mreset,gparts=take(8)
    wh=take(7)
    (so_hbm,ig_hbm,gsum,e_h,normed_h,mixed_h,n2_h,hidden_h,gi_h,ui_h,ai_h,dq_h,dk_h,dv_h)=take(14)
    W=take(7)
    (cur,eg,normed,q,k,v,mixed,n2,g,u,hidden,middle,p,rk,rv,grads,mxg,mg,acc,so,ig,mask,gain)=take(23)
    (w_sem,in_sem,c_sem,out_sem,xs,xr,gsems,grs)=take(8)
    Wq,Wk,Wv,Wo,Wg,Wu,Wd=W
    sec=lax.axis_index("section"); f=lax.axis_index("fsdp")
    scale=HD**-0.5
    B16=jnp.bfloat16
    bar=pltpu.get_barrier_semaphore()
    pl.semaphore_signal(bar,1,device_id=(1-sec,f),device_id_type=MESH)
    def load_cur(): return pltpu.make_async_copy(x_hbm,cur,in_sem.at[0])
    def load_eg(): return pltpu.make_async_copy(og_hbm,eg,in_sem.at[0])
    @pl.when(sec==0)
    def _(): load_cur().start()
    def load_cache(m,kv):
        src=(mk_hbm,mv_hbm)[kv]
        return [pltpu.make_async_copy(src.at[m,pl.ds(i*(CACHE//2),CACHE//2)],grads.at[2*kv+i],c_sem.at[2*kv+i]) for i in range(2)]
    @pl.when(sec==1)
    def _():
        for kv in range(2):
            for cp in load_cache(0,kv): cp.start()
        load_eg().start()
    for i in range(7): pltpu.make_async_copy(wh[i],W[i],w_sem.at[i]).start()
    def wait_w(t,*ids):
        @pl.when(t==0)
        def _():
            for i in ids: pltpu.make_async_copy(wh[i],W[i],w_sem.at[i]).wait()
    gain[...]=jnp.sum(gparts[...].astype(jnp.float32),axis=0)[0:8]
    gsum[...]=jnp.zeros_like(gsum)
    ri=lax.broadcasted_iota(jnp.int32,(T,T),0); ci=lax.broadcasted_iota(jnp.int32,(T,T),1)
    for m in range(micro):
        row=jnp.broadcast_to(docs[m:m+1,:].astype(jnp.float32),(T,T))
        mask[m]=jnp.where((row==row.T)&(ci<=ri),1.0,0.0)
    @pl.when(sec==0)
    def _():
        def z(i,_):
            o=pl.ds(pl.multiple_of(i*MEMK,MEMK),MEMK)
            for m in range(micro):
                rk[m,o,:]=jnp.zeros((MEMK,D),B16); rv[m,o,:]=jnp.zeros((MEMK,D),B16)
            return 0
        lax.fori_loop(0,NBLK,z,0)
        load_cur().wait()
    @pl.when(sec==1)
    def _():
        for m in range(micro):
            for kv in range(2):
                for cp in load_cache(m,kv): cp.wait()
                dst=(rk,rv)[kv]
                def body(b,_,m=m,kv=kv,dst=dst):
                    idx=midx[m,pl.ds(b,1),:]
                    col=jnp.broadcast_to(idx.astype(jnp.float32),(MEMK,MEMK)).T[:,0:1].astype(jnp.int32)
                    half=CACHE//2
                    io=lax.broadcasted_iota(jnp.int32,(MEMK,half),1)
                    tot=None
                    for i in range(2):
                        hot=jnp.where(io+i*half==col,1.0,0.0).astype(B16)
                        r=nn(hot,grads[2*kv+i])
                        tot = r if tot is None else tot + r
                    dst[m,pl.ds(pl.multiple_of(b*MEMK,MEMK),MEMK),:]=tot.astype(B16)
                    return 0
                lax.fori_loop(0,NBLK,body,0)
                if m+1<micro:
                    for cp in load_cache(m+1,kv): cp.start()
        load_eg().wait()
    pl.semaphore_wait(bar,1)
    def save(j,src,dst,m):
        return pltpu.make_async_copy(src.at[m],dst.at[m],out_sem.at[j,m])
    def xcopy(kind,m):
        src,dst=((so,cur),(ig,eg))[kind]
        return pltpu.make_async_remote_copy(src.at[m],dst.at[m],xs.at[kind,m],xr.at[kind,m],device_id=(1-sec,f),device_id_type=MESH)
    RB=64
    def rows_loop(fn):
        def b(i,_):
            fn(pl.ds(pl.multiple_of(i*RB,RB),RB)); return 0
        lax.fori_loop(0,T//RB,b,0)
    def cols_loop(N,CH,fn):
        def b(i,_):
            fn(pl.ds(pl.multiple_of(i*CH,CH),CH)); return 0
        lax.fori_loop(0,N//CH,b,0)
    def normalize(x,row):
        inv=lax.rsqrt(jnp.mean(x*x,axis=-1,keepdims=True)+EPS)
        return x*inv*gain[row:row+1,:]
    def norm_back(x,c,row):
        inv=lax.rsqrt(jnp.mean(x*x,axis=-1,keepdims=True)+EPS)
        s=c*gain[row:row+1,:]
        gsum[row:row+1,:]+=jnp.sum(c*x*inv,axis=0,keepdims=True)
        return inv*s-x*(inv*inv*inv)*jnp.mean(s*x,axis=-1,keepdims=True)
    def forward(t,m):
        @pl.when(sec==1)
        def _(): xcopy(0,m).wait_recv()
        def f1(r): normed[m,r,:]=normalize(cur[m,r,:].astype(jnp.float32),0).astype(B16)
        rows_loop(f1)
        save(0,normed,normed_h,m).start()
        wait_w(t,0,1,2)
        def f2(cs):
            a=normed[m]
            q[m,:,cs]=nn(a,Wq[:,cs]).astype(B16)
            k[m,:,cs]=nn(a,Wk[:,cs]).astype(B16)
            v[m,:,cs]=nn(a,Wv[:,cs]).astype(B16)
        cols_loop(D,256,f2)
        def head(h,_):
            hs=pl.ds(pl.multiple_of(h*HD,HD),HD)
            qh=q[m,:,hs]; kh=k[m,:,hs]; vh=v[m,:,hs]
            s=jnp.where(mask[m]>0.5,nt(qh,kh)*scale,MASKED)
            sr=[]
            for b in range(NBLK):
                live=(mreset[m,b:b+1,:]==0)&(sec==1)
                x=nt(qh[b*MQB:(b+1)*MQB],rk[m,b*MEMK:(b+1)*MEMK,hs])*scale
                sr.append(jnp.where(jnp.broadcast_to(live,(MQB,MEMK)),x,MASKED))
            sr=jnp.concatenate(sr,axis=0)
            top=jnp.maximum(jnp.max(s,axis=-1,keepdims=True),jnp.max(sr,axis=-1,keepdims=True))
            es=jnp.exp(s-top); er=jnp.exp(sr-top)
            inv=1.0/(jnp.sum(es,axis=-1,keepdims=True)+jnp.sum(er,axis=-1,keepdims=True))
            ps=(es*inv).astype(B16); pr=(er*inv).astype(B16)
            p[m,h,:,0:T]=ps; p[m,h,:,T:T+MEMK]=pr
            mr=jnp.concatenate([nn(pr[b*MQB:(b+1)*MQB],rv[m,b*MEMK:(b+1)*MEMK,hs]) for b in range(NBLK)],axis=0)
            mixed[m,:,hs]=(nn(ps,vh)+mr).astype(B16)
            return 0
        lax.fori_loop(0,HEADS,head,0)
        save(1,mixed,mixed_h,m).start()
        wait_w(t,3)
        def f3(cs): middle[m,:,cs]=cur[m,:,cs].astype(jnp.float32)+nn(mixed[m],Wo[:,cs])
        cols_loop(D,256,f3)
        def f4(r): n2[m,r,:]=normalize(middle[m,r,:],1).astype(B16)
        rows_loop(f4)
        save(2,n2,n2_h,m).start()
        wait_w(t,4,5)
        def f5(cs):
            a=n2[m]
            gg=nn(a,Wg[:,cs]); uu=nn(a,Wu[:,cs])
            g[m,:,cs]=gg.astype(B16); u[m,:,cs]=uu.astype(B16)
            hidden[m,:,cs]=(gg*jax.nn.sigmoid(gg)*uu).astype(B16)
        cols_loop(FF,256,f5)
        save(3,hidden,hidden_h,m).start()
        wait_w(t,6)
        def f6(cs): so[m,:,cs]=(middle[m,:,cs]+nn(hidden[m],Wd[:,cs])).astype(B16)
        cols_loop(D,256,f6)
        @pl.when(sec==0)
        def _(): xcopy(0,m).start()
        save(4,so,so_hbm,m).start()
    def backward(t,m):
        @pl.when(sec==0)
        def _(): xcopy(1,m).wait_recv()
        save(5,eg,e_h,m).start()
        def b1(cs):
            hg=nt(eg[m],Wd[cs,:])
            gg=g[m,:,cs].astype(jnp.float32); uu=u[m,:,cs].astype(jnp.float32)
            sg=jax.nn.sigmoid(gg)
            u[m,:,cs]=(hg*gg*sg).astype(B16)
            g[m,:,cs]=(hg*uu*sg*(1.0+gg*(1.0-sg))).astype(B16)
        cols_loop(FF,256,b1)
        save(6,g,gi_h,m).start(); save(7,u,ui_h,m).start()
        def b2(cs): acc[:,cs]=nt(g[m],Wg[cs,:])+nt(u[m],Wu[cs,:])
        cols_loop(D,256,b2)
        def b3(r):
            t_=eg[m,r,:].astype(jnp.float32)+norm_back(middle[m,r,:],acc[r,:],1)
            mg[r,:]=t_; grads[0,pl.ds(m*T+r.start,RB),:]=t_.astype(B16)
        rows_loop(b3)
        ms=pl.ds(pl.multiple_of(m*T,T),T)
        def gsave(j,i,dst): return pltpu.make_async_copy(grads.at[i,ms],dst.at[m],out_sem.at[j,m])
        gsave(8,0,ai_h).start()
        def b4(cs): mxg[:,cs]=nt(grads[0,ms,:],Wo[cs,:]).astype(B16)
        cols_loop(D,256,b4)
        def head(h,_):
            hs=pl.ds(pl.multiple_of(h*HD,HD),HD)
            qh=q[m,:,hs]; kh=k[m,:,hs]; vh=v[m,:,hs]; mh=mxg[:,hs]
            ps=p[m,h,:,0:T]; pr=p[m,h,:,T:T+MEMK]
            grads[3,ms,hs]=tn(ps,mh).astype(B16)
            pg=nt(mh,vh)
            rg=jnp.concatenate([nt(mh[b*MQB:(b+1)*MQB],rv[m,b*MEMK:(b+1)*MEMK,hs]) for b in range(NBLK)],axis=0)
            pf=ps.astype(jnp.float32); rf=pr.astype(jnp.float32)
            w=jnp.sum(pf*pg,axis=-1,keepdims=True)+jnp.sum(rf*rg,axis=-1,keepdims=True)
            ds=(pf*(pg-w)).astype(B16); dr=(rf*(rg-w)).astype(B16)
            qr=jnp.concatenate([nn(dr[b*MQB:(b+1)*MQB],rk[m,b*MEMK:(b+1)*MEMK,hs]) for b in range(NBLK)],axis=0)
            grads[1,ms,hs]=((nn(ds,kh)+qr)*scale).astype(B16)
            grads[2,ms,hs]=(tn(ds,qh)*scale).astype(B16)
            return 0
        lax.fori_loop(0,HEADS,head,0)
        gsave(9,1,dq_h).start(); gsave(10,2,dk_h).start(); gsave(11,3,dv_h).start()
        def b5(cs): acc[:,cs]=nt(grads[1,ms,:],Wq[cs,:])+nt(grads[2,ms,:],Wk[cs,:])+nt(grads[3,ms,:],Wv[cs,:])
        cols_loop(D,256,b5)
        def b6(r): ig[m,r,:]=(mg[r,:]+norm_back(cur[m,r,:].astype(jnp.float32),acc[r,:],0)).astype(B16)
        rows_loop(b6)
        @pl.when(sec==1)
        def _(): xcopy(1,m).start()
        save(12,ig,ig_hbm,m).start()
    def tick(t,_):
        first=sec==0
        is_f=jnp.where(first,t<micro,t%2==0)
        m=jnp.where(first,lax.rem(t,micro),t//2)
        @pl.when(is_f)
        def _(): forward(t,m)
        @pl.when(jnp.logical_not(is_f))
        def _(): backward(t,m)
        return 0
    lax.fori_loop(0,2*micro,tick,0)
    for m in range(micro):
        @pl.when(sec==0)
        def _(): xcopy(0,m).wait_send()
        @pl.when(sec==1)
        def _(): xcopy(1,m).wait_send()
        for j,(s,d) in enumerate([(normed,normed_h),(mixed,mixed_h),(n2,n2_h),(hidden,hidden_h),(so,so_hbm),(eg,e_h),(g,gi_h),(u,ui_h)]):
            save(j,s,d,m).wait()
        for j,i,d in ((8,0,ai_h),(9,1,dq_h),(10,2,dk_h),(11,3,dv_h)):
            pltpu.make_async_copy(grads.at[i,pl.ds(m*T,T)],d.at[m],out_sem.at[j,m]).wait()
        save(12,ig,ig_hbm,m).wait()

def chain(n, x, og, docs, mk, mv, midx, mreset, gparts, weights, cid=2):
    micro,T,D=x.shape
    FF=weights[4].shape[1]
    CACHE=mk.shape[1]; NBLK=midx.shape[1]
    B=jnp.bfloat16; F=jnp.float32
    V=pltpu.VMEM
    act=(micro,T,D); fact=(micro,T,FF)
    S=jax.ShapeDtypeStruct
    outs=[S(act,B),S(act,B),S((8,D),F),S(act,B),S(act,B),S(act,B),S(act,B),S(fact,B),S(fact,B),S(fact,B),S(act,B),S(act,B),S(act,B),S(act,B)]
    scratch=[V(w.shape,B) for w in weights]
    scratch+=[V(act,B)]*8+[V(fact,B)]*3+[V(act,F),V((micro,HEADS,T,T+MEMK),B),V((micro,NBLK*MEMK,D),B),V((micro,NBLK*MEMK,D),B),V((4,micro*T,D),B),V((T,D),B),V((T,D),F),V((T,D),F),V(act,B),V(act,B),V((micro,T,T),F),V((8,D),F)]
    DM=pltpu.SemaphoreType.DMA
    scratch+=[DM((7,)),DM((2,)),DM((4,)),DM((13,micro)),DM((2,micro)),DM((2,micro)),DM((1,)),DM((1,))]
    HB=pl.BlockSpec(memory_space=pltpu.HBM); VB=pl.BlockSpec(memory_space=pltpu.VMEM)
    reset=jnp.broadcast_to(mreset[:,:,None],(micro,NBLK,MEMK))
    return pl.pallas_call(functools.partial(chain_kernel,n,micro,T,D,FF,CACHE,NBLK),
        out_shape=outs,
        in_specs=[HB,HB,VB,HB,HB,VB,VB,VB]+[HB]*7,
        out_specs=[HB,HB,VB]+[HB]*11,
        scratch_shapes=scratch,
        compiler_params=pltpu.CompilerParams(collective_id=cid,has_side_effects=True,vmem_limit_bytes=64<<20),
    )(x,og,docs,mk,mv,midx,reset,gparts,*weights)


COLS=1024
def plan(n, lhs_shapes, rhs_shapes, weights):
    pieces=[]
    for w,(l,r) in enumerate(weights):
        rows=lhs_shapes[l][1]//n; N=rhs_shapes[r][1]
        step=512 if rows>64*16//n else 1024
        for c0 in range(0,N,step):
            pieces.append((w,rows,c0,min(step,N-c0)))
    return pieces

def reduce_kernel(n, tok, lhs_shapes, rhs_shapes, weights, pieces, vec_rows, SLOTS, *refs):
    NP=len(pieces); NL=len(lhs_shapes); NR=len(rhs_shapes); NW=len(weights)
    R,C=layout(n); H=n//2
    it=iter(refs)
    take=lambda k:[next(it) for _ in range(k)]
    lhs=take(NL); rhs=take(NR); vec=next(it)
    outs=take(NW); vec_out=next(it)
    ring=next(it); tbuf=take(NL)
    keep=take(NP); sibr=take(NP); yr=take(NP); xr=take(NP); zu=take(NP); zd=take(NP); fin=take(NP)
    shapes=sorted({(p[1],p[3]) for p in pieces})
    stage_of=dict(zip(shapes,take(len(shapes))))
    vecb=next(it); vecr=next(it)
    (ld_sem,sib_s,sib_r,y_s,y_r,x_s,x_r,zu_s,zu_r,zd_s,zd_r,v_s,v_r,o_s)=take(14)
    sec=lax.axis_index("section"); f=lax.axis_index("fsdp")
    c=f%2; zy=f//2; y=zy%C; z=zy//C
    offload=(C==2 and R%2==0)
    zx=z+1-2*(z%2)
    def dev(zz,yy,cc): return (sec,(zz*C+yy)*2+cc)
    def rcopy(src,dst,ss,rs,d):
        return pltpu.make_async_remote_copy(src,dst,ss,rs,device_id=dev(*d),device_id_type=MESH)
    LOGN=n.bit_length()-1
    nb=[]
    nb.append((c>=0,dev(z,y,1-c)))
    for k in range(1,C): nb.append((c>=0,dev(z,lax.rem(y+k,C),c)))
    nb.append((z>0,dev(z-1,y,c))); nb.append((z<R-1,dev(z+1,y,c)))
    for k in range(1,R.bit_length()-1): nb.append((c>=0,(sec,f^(2*C<<k))))
    bar=pltpu.get_barrier_semaphore()
    loads=[]
    def parts(ref,shape):
        return [(ref,c0,min(COLS,shape[1]-c0)) for c0 in range(0,shape[1],COLS)]
    load_id={}
    def need(kind,i):
        key=(kind,i)
        if key in load_id: return
        ref=lhs[i] if kind=="l" else rhs[i]
        sh=lhs_shapes[i] if kind=="l" else rhs_shapes[i]
        ids=[]
        for pr in parts(ref,sh):
            ids.append(len(loads)); loads.append(pr)
        load_id[key]=ids
    for l,r in weights:
        need("l",l); need("r",r)
    issued=[0]; freed=set()
    def load_copy(k):
        ref,c0,w=loads[k]
        return pltpu.make_async_copy(ref.at[:,pl.ds(c0,w)],ring.at[k%SLOTS,:,pl.ds(0,w)],ld_sem.at[k%SLOTS])
    def pump():
        while issued[0]<len(loads) and (issued[0]<SLOTS or (issued[0]-SLOTS) in freed):
            load_copy(issued[0]).start(); issued[0]+=1
    pump()
    for cond,d in nb:
        @pl.when(cond)
        def _(): pl.semaphore_signal(bar,1,device_id=d,device_id_type=MESH)
    waited=set()
    def wait_load(k):
        if k not in waited:
            load_copy(k).wait(); waited.add(k)
    transposed=set()
    def ensure_lhs(l):
        if l in transposed: return
        transposed.add(l)
        for j,k in enumerate(load_id[("l",l)]):
            wait_load(k)
            w=loads[k][2]
            CH=256
            def body(i,_,k=k,j=j):
                o=pl.multiple_of(i*CH,CH)
                tbuf[l][pl.ds(pl.multiple_of(j*COLS+o,CH),CH),:]=ring[k%SLOTS,:,pl.ds(o,CH)].T
                return 0
            lax.fori_loop(0,w//CH,body,0)
            freed.add(k)
        pump()
    last_use={}
    for i,(w,rows,c0,nc) in enumerate(pieces):
        l,r=weights[w]
        last_use[load_id[("r",r)][c0//COLS]]=i
    sends=[]
    stage_use={}
    def compute(i):
        w,rows,c0,nc=pieces[i]
        l,r=weights[w]
        ensure_lhs(l)
        k=load_id[("r",r)][c0//COLS]
        wait_load(k)
        lc=c0%COLS
        st=stage_of[(rows,nc)]
        u=stage_use.get((rows,nc),0); stage_use[(rows,nc)]=u+1
        slot=u%2
        if u>=2: sib_waits[(rows,nc)].pop(0)()
        T4=tbuf[l].reshape(H,2,rows,tok)
        CH=256
        for which,dst in ((1-c,st.at[slot]),(c,keep[i])):
            def body(j,_,which=which,dst=dst):
                o=pl.multiple_of(j*CH,CH)
                a=T4[:,which].reshape(H*rows,tok)
                b=ring[k%SLOTS,:,pl.ds(pl.multiple_of(lc+o,CH),CH)]
                res=jnp.dot(a,b,preferred_element_type=jnp.float32).astype(jnp.bfloat16)
                dst[:,:,pl.ds(o,CH)]=res.reshape(H,rows,CH)
                return 0
            lax.fori_loop(0,nc//CH,body,0)
            if dst is not keep[i]:
                cp=rcopy(st.at[slot],sibr[i],sib_s.at[i],sib_r.at[i],(z,y,1-c))
                cp.start()
                sib_waits.setdefault((rows,nc),[]).append(cp.wait_send)
        if last_use[k]==i:
            freed.add(k); pump()
    sib_waits={}
    def add_into(dst,src,rows):
        def body(j,_):
            o=pl.multiple_of(j*16,16)
            dst[pl.ds(o,16),:]=dst[pl.ds(o,16),:]+src[pl.ds(o,16),:]
            return 0
        lax.fori_loop(0,rows//16,body,0)
    def send(cond,cp):
        if cond is None: cp().start()
        else:
            @pl.when(cond)
            def _(): cp().start()
        sends.append((cond,cp))
    def sib_add(i):
        w,rows,c0,nc=pieces[i]
        rcopy(sibr[i],sibr[i],sib_s.at[i],sib_r.at[i],(z,y,1-c)).wait_recv()
        def body(k,_):
            add_into(keep[i].at[k],sibr[i].at[k],rows)
            return 0
        lax.fori_loop(0,H,body,0)
        if offload:
            send(c==1,lambda: rcopy(keep[i].at[zx*C+1-y],xr[i],x_s.at[i],x_r.at[i],(zx,y,c)))
        for kz in range(R-1,-1,-1):
            zt=lax.rem(z+kz,R)
            for ky in range(1,C):
                yt=lax.rem(y+ky,C)
                slot=C-1-ky
                cp=lambda zt=zt,yt=yt,slot=slot: rcopy(keep[i].at[zt*C+yt],yr[i].at[slot,zt],y_s.at[i,slot,zt],y_r.at[i,slot,zt],(z,yt,c))
                if offload and kz==0:
                    continue
                send((jnp.logical_not((c==1)&(zt==zx))) if offload else None,cp)
    def x_add(i):
        w,rows,c0,nc=pieces[i]
        if not offload: return
        @pl.when(c==1)
        def _():
            rcopy(xr[i],xr[i],x_s.at[i],x_r.at[i],(zx,y,c)).wait_recv()
            add_into(keep[i].at[z*C+1-y],xr[i],rows)
        send(None,lambda: rcopy(keep[i].at[z*C+1-y],yr[i].at[0,z],y_s.at[i,0,z],y_r.at[i,0,z],(z,1-y,c)))
    def y_add(i):
        w,rows,c0,nc=pieces[i]
        for kz in range(R-1,-1,-1):
            zt=lax.rem(z+kz,R)
            for slot in range(C-1):
                def go(zt=zt,slot=slot):
                    rcopy(yr[i].at[slot,zt],yr[i].at[slot,zt],y_s.at[i,slot,zt],y_r.at[i,slot,zt],(z,y,1-c)).wait_recv()
                    add_into(keep[i].at[zt*C+y],yr[i].at[slot,zt],rows)
                if offload and kz!=0:
                    pl.when(jnp.logical_not((c==1)&(zt==zx)))(go)
                else: go()
    def z_step(i,s):
        w,rows,c0,nc=pieces[i]
        def line(zs,up):
            rb,rr,ss=(zu,zu_r,zu_s) if up else (zd,zd_r,zd_s)
            first=(zs==0) if up else (zs==R-1)
            targets=range(R-1,zs,-1) if up else range(0,zs)
            nxt=zs+1 if up else zs-1
            cps=[]
            for t in targets:
                k=abs(t-zs)
                cps.append((k,lambda t=t,k=k: rcopy(keep[i].at[t*C+y],rb[i].at[k-1],ss.at[i,k-1],rr.at[i,k-1],(nxt,y,c)),t))
            def go():
                for k,cp,t in cps:
                    if not first:
                        rcopy(rb[i].at[k],rb[i].at[k],ss.at[i,k],rr.at[i,k],(zs,y,1-c)).wait_recv()
                        add_into(keep[i].at[t*C+y],rb[i].at[k],rows)
                    cp().start()
            pl.when(z==zs)(go)
            for k,cp,t in cps: sends.append((z==zs,cp))
        line(s,True)
        line(R-1-s,False)
    def final(i):
        w,rows,c0,nc=pieces[i]
        blk=z*C+y
        @pl.when(z>0)
        def _():
            rcopy(zu[i].at[0],zu[i].at[0],zu_s.at[i,0],zu_r.at[i,0],(z,y,1-c)).wait_recv()
        @pl.when(z<R-1)
        def _():
            rcopy(zd[i].at[0],zd[i].at[0],zd_s.at[i,0],zd_r.at[i,0],(z,y,1-c)).wait_recv()
        def body(j,_):
            o=pl.ds(pl.multiple_of(j*16,16),16)
            a=keep[i][blk,o,:].astype(jnp.float32)
            a=a+jnp.where(z>0,zu[i][0,o,:].astype(jnp.float32),0.0)+jnp.where(z<R-1,zd[i][0,o,:].astype(jnp.float32),0.0)
            fin[i][o,:]=a.astype(jnp.bfloat16)
            return 0
        lax.fori_loop(0,rows//16,body,0)
        pltpu.make_async_copy(fin[i],outs[w].at[:,pl.ds(c0,nc)],o_s.at[i]).start()
    def vec_step(k):
        if k>0:
            vcopy(k-1).wait()
            vecb[k]=vecb[k-1]+vecr[k-1]
        if k<LOGN: vcopy(k).start()
        else:
            cp=pltpu.make_async_copy(vecb.at[LOGN],vec_out,o_s.at[NP]); cp.start()
    def vcopy(k):
        return pltpu.make_async_remote_copy(vecb.at[k],vecr.at[k],v_s.at[k],v_r.at[k],device_id=(sec,f^(1<<k)),device_id_type=MESH)
    cp=pltpu.make_async_copy(vec,vecb.at[0],o_s.at[NP]); cp.start(); cp.wait()
    pl.semaphore_wait(bar,sum(jnp.where(cond,1,0) for cond,d in nb))
    LAGY=3
    for t in range(NP+LAGY+R+1):
        if t<NP: compute(t)
        if 0<=t-1<NP: sib_add(t-1)
        if 0<=t-2<NP: x_add(t-2)
        if t<=LOGN: vec_step(t)
        if 0<=t-LAGY<NP: y_add(t-LAGY)
        for s in range(R):
            i=t-LAGY-s
            if 0<=i<NP: z_step(i,s)
        i=t-LAGY-R
        if 0<=i<NP: final(i)
    for q in sib_waits.values():
        for wfn in q: wfn()
    for cond,cp in sends:
        if cond is None: cp().wait_send()
        else:
            @pl.when(cond)
            def _(): cp().wait_send()
    for i in range(NP):
        w,rows,c0,nc=pieces[i]
        pltpu.make_async_copy(fin[i],outs[w].at[:,pl.ds(c0,nc)],o_s.at[i]).wait()
    pltpu.make_async_copy(vecb.at[LOGN],vec_out,o_s.at[NP]).wait()

def reduce(n, lhs, rhs, weights, vec, cid=1, SLOTS=6):
    tok=lhs[0].shape[0]
    ls=[a.shape for a in lhs]; rs=[a.shape for a in rhs]
    pieces=plan(n,ls,rs,weights)
    R,C=layout(n); H=n//2
    NP=len(pieces)
    LOGN=n.bit_length()-1
    D=pltpu.SemaphoreType.DMA
    B=jnp.bfloat16
    V=pltpu.VMEM
    shapes=sorted({(p[1],p[3]) for p in pieces})
    scratch=[V((SLOTS,tok,COLS),B)]+[V((s[1],tok),B) for s in ls]
    scratch+=[V((H,p[1],p[3]),B) for p in pieces]
    scratch+=[V((H,p[1],p[3]),B) for p in pieces]
    scratch+=[V((C-1,R,p[1],p[3]),B) for p in pieces]
    scratch+=[V((p[1],p[3]) if C==2 else (16,128),B) for p in pieces]
    scratch+=[V((R-1,p[1],p[3]),B) for p in pieces]*2
    scratch+=[V((p[1],p[3]),B) for p in pieces]
    scratch+=[V((2,H)+s,B) for s in shapes]
    scratch+=[V((LOGN+1,)+vec.shape,vec.dtype),V((LOGN,)+vec.shape,vec.dtype)]
    scratch+=[D((SLOTS,)),D((NP,)),D((NP,)),D((NP,C-1,R)),D((NP,C-1,R)),D((NP,)),D((NP,)),D((NP,R-1)),D((NP,R-1)),D((NP,R-1)),D((NP,R-1)),D((LOGN,)),D((LOGN,)),D((NP+1,))]
    HB=pl.BlockSpec(memory_space=pltpu.HBM)
    res=pl.pallas_call(functools.partial(reduce_kernel,n,tok,ls,rs,weights,pieces,vec.shape[0],SLOTS),
        out_shape=[jax.ShapeDtypeStruct((ls[l][1]//n,rs[r][1]),B) for l,r in weights]+[jax.ShapeDtypeStruct(vec.shape,vec.dtype)],
        in_specs=[HB]*(len(lhs)+len(rhs)+1),
        out_specs=[HB]*(len(weights)+1),
        scratch_shapes=scratch,
        compiler_params=pltpu.CompilerParams(collective_id=cid,has_side_effects=True,vmem_limit_bytes=63<<20),
    )(*lhs,*rhs,vec)
    return res[:-1],res[-1]


def per_device(
    block_input, output_grad, document_ids, memory_keys, memory_values, memory_index, memory_reset,
    query_weight, key_weight, value_weight, output_weight, gate_weight, up_weight, down_weight,
    attend_gain, feed_gain,
):
    n = lax.axis_size("fsdp")
    f = lax.axis_index("fsdp")
    micro, T, D = block_input.shape
    FF = gate_weight.shape[2]
    gw = attend_gain.shape[1]
    vec = jnp.zeros((16, D), jnp.bfloat16)
    vec = lax.dynamic_update_slice(vec, jnp.concatenate([attend_gain, feed_gain]), (0, f * gw))
    shards = [w[0] for w in (query_weight, key_weight, value_weight, output_weight, gate_weight, up_weight, down_weight)]
    rows = [s.shape[0] for s in shards]
    padded = [jnp.pad(s, ((0, -s.shape[0] % 16), (0, 0))) for s in shards]
    gathered = gather(n, [vec] + padded, 0)
    weights = [g[:, :r].reshape(n * r, g.shape[2]) for g, r in zip(gathered[1:], rows)]
    (so, ig, gsum, e, normed, mixed, n2, hidden, gi, ui, ai, dq, dk, dv) = chain(
        n, block_input, output_grad, document_ids, memory_keys, memory_values, memory_index, memory_reset, gathered[0], weights, 2)
    flat = lambda a: a.reshape(micro * T, a.shape[2])
    hid = flat(hidden)
    rd = rows[6]
    if rd % 16:
        hid = jnp.pad(hid.reshape(micro * T, n, rd), ((0, 0), (0, 0), (0, -rd % 16))).reshape(micro * T, -1)
    lhs = [hid, flat(n2), flat(mixed), flat(normed)]
    rhs = [flat(a) for a in (e, gi, ui, ai, dv, dk, dq)]
    order = [(0, 0), (1, 1), (1, 2), (2, 3), (3, 4), (3, 5), (3, 6)]
    sums, total = reduce(n, lhs, rhs, order, gsum, 1)
    gd, gg, gu, go, gv, gk, gq = sums
    gains = lax.dynamic_slice(total, (0, f * gw), (2, gw)).astype(jnp.bfloat16)
    return (so[None], ig[None], gq[None], gk[None], gv[None], go[None], gg[None], gu[None], gd[:rd][None], gains[0:1], gains[1:2])


def solution(mesh):
    w = P("section", "fsdp", None)
    r = P(None, "fsdp", None)
    v = P("section", "fsdp")
    return jax.shard_map(
        per_device,
        mesh=mesh,
        in_specs=(r, r, P(None, "fsdp"), r, r, r, P(None, "fsdp")) + (w,) * 7 + (v, v),
        out_specs=(P("section", None, "fsdp", None),) * 2 + (w,) * 7 + (v, v),
        check_vma=False,
    )
```

```python
import functools
import math
import jax
import jax.numpy as jnp
from jax import lax
from jax.experimental import pallas as pl
from jax.experimental.pallas import tpu as pltpu
from jax.sharding import PartitionSpec as P

MESH = pl.DeviceIdType.MESH


def layout(n):
    rest=n//2
    R=min(4,rest); C=rest//R
    return R,C

def gather_kernel(n, P, *refs):
    ins=refs[:P]; outs=refs[P:2*P]; bufs=refs[2*P:3*P]
    own_sem,out_sem,s_zu,s_zd,s_yu,s_yd,s_sb,s_ex,r_main,r_sib=refs[3*P:]
    R,C=layout(n)
    sec=lax.axis_index("section"); f=lax.axis_index("fsdp")
    c=f%2; zy=f//2; y=zy%C; z=zy//C
    def dev(zz,yy,cc): return (sec,(zz*C+yy)*2+cc)
    bar=pltpu.get_barrier_semaphore()
    nb=[(z>0,(z-1,y,c)),(z<R-1,(z+1,y,c)),(y>0,(z,y-1,c)),(y<C-1,(z,y+1,c)),(c>=0,(z,y,1-c))]
    for p in range(P):
        pltpu.make_async_copy(ins[p],bufs[p].at[f],own_sem.at[p]).start()
    for cond,d in nb:
        @pl.when(cond)
        def _():
            pl.semaphore_signal(bar,1,device_id=dev(*d),device_id_type=MESH)
    pl.semaphore_wait(bar,sum(jnp.where(cond,1,0) for cond,d in nb))
    pending=[]
    def send(cond,p,zb,yb,target,ssem,rsem):
        blk=(zb*C+yb)*2+c
        k=zb*C+yb
        def mk():
            return pltpu.make_async_remote_copy(bufs[p].at[blk],bufs[p].at[blk],ssem.at[p,k],rsem.at[p,k],device_id=dev(*target),device_id_type=MESH)
        @pl.when(cond)
        def _(): mk().start()
        pending.append((cond,mk))
    def wait_main(cond,p,zb,yb):
        blk=(zb*C+yb)*2+c; k=zb*C+yb
        @pl.when(cond)
        def _():
            pltpu.make_async_remote_copy(bufs[p].at[blk],bufs[p].at[blk],s_sb.at[p,k],r_main.at[p,k],device_id=dev(z,y,1-c),device_id_type=MESH).wait_recv()
    offload = (C==2)
    T=(c>=0)
    def own(p):
        pltpu.make_async_copy(ins[p],bufs[p].at[f],own_sem.at[p]).wait()
        send(y>0,p,z,y,(z,y-1,c),s_yd,r_main)
        send(y<C-1,p,z,y,(z,y+1,c),s_yu,r_main)
        send(z>0,p,z,y,(z-1,y,c),s_zd,r_main)
        send(z<R-1,p,z,y,(z+1,y,c),s_zu,r_main)
        send(T,p,z,y,(z,y,1-c),s_sb,r_sib)
    def z_arrivals(p):
        for d in range(1,R):
            for sign in (-1,1):
                zb=z+sign*d
                ok=(zb>=0)&(zb<R)
                zbc=jnp.clip(zb,0,R-1)
                wait_main(ok,p,zbc,y)
                if sign<0:
                    send(ok&(z<R-1),p,zbc,y,(z+1,y,c),s_zu,r_main)
                else:
                    send(ok&(z>0),p,zbc,y,(z-1,y,c),s_zd,r_main)
                ydo=ok
                if offload: ydo=ok & jnp.logical_not((c==1)&(zbc==(z+1-2*(z%2))))
                send(ydo&(y>0),p,zbc,y,(z,y-1,c),s_yd,r_main)
                send(ydo&(y<C-1),p,zbc,y,(z,y+1,c),s_yu,r_main)
                send(ok,p,zbc,y,(z,y,1-c),s_sb,r_sib)
    def y_arrivals(p, near):
        for dy in range(1,C):
            for sign in (-1,1):
                yb=y+sign*dy
                oky=(yb>=0)&(yb<C)
                ybc=jnp.clip(yb,0,C-1)
                for d in ([0] if near else range(1,R)):
                    for zs in ((0,) if d==0 else (-1,1)):
                        zb=z+zs*d
                        ok=oky&(zb>=0)&(zb<R)
                        zbc=jnp.clip(zb,0,R-1)
                        wait_main(ok,p,zbc,ybc)
                        if C>2:
                            if sign<0: send(ok&(y<C-1),p,zbc,ybc,(z,y+1,c),s_yu,r_main)
                            else: send(ok&(y>0),p,zbc,ybc,(z,y-1,c),s_yd,r_main)
                        if offload and d==0:
                            send(ok&(c==1),p,zbc,ybc,(z+1-2*(z%2),y,c),s_ex,r_main)
                        send(ok,p,zbc,ybc,(z,y,1-c),s_sb,r_sib)
    def finish(p):
        def body(k,_):
            blk=k*2+1-c
            pltpu.make_async_remote_copy(bufs[p].at[blk],bufs[p].at[blk],s_sb.at[p,k],r_sib.at[p,k],device_id=dev(z,y,1-c),device_id_type=MESH).wait_recv()
            return 0
        lax.fori_loop(0,n//2,body,0)
        pltpu.make_async_copy(bufs[p],outs[p],out_sem.at[p]).start()
    LA=2
    for p in range(min(LA,P)): own(p)
    for p in range(P+2):
        if p+LA<P: own(p+LA)
        if p<P: z_arrivals(p)
        if 0<=p-1<P: y_arrivals(p-1,True)
        if 0<=p-2<P:
            y_arrivals(p-2,False)
            finish(p-2)
    for cond,mk in pending:
        @pl.when(cond)
        def _(): mk().wait_send()
    for p in range(P):
        pltpu.make_async_copy(bufs[p],outs[p],out_sem.at[p]).wait()

def gather(n, shards, cid=0):
    P=len(shards)
    R,C=layout(n)
    h=n//2
    D=pltpu.SemaphoreType.DMA
    return pl.pallas_call(functools.partial(gather_kernel,n,P),
        out_shape=[jax.ShapeDtypeStruct((n,)+s.shape,s.dtype) for s in shards],
        in_specs=[pl.BlockSpec(memory_space=pltpu.HBM)]*P,
        out_specs=[pl.BlockSpec(memory_space=pltpu.HBM)]*P,
        scratch_shapes=[pltpu.VMEM((n,)+s.shape,s.dtype) for s in shards]+[D((P,)),D((P,))]+[D((P,h))]*8,
        compiler_params=pltpu.CompilerParams(collective_id=cid,has_side_effects=True,vmem_limit_bytes=60<<20),
    )(*shards)

HEADS=8; HD=128; MQB=64; MEMK=128; EPS=1e-06; MASKED=-1e30
XC=256

def nn(a,b): return jnp.dot(a,b,preferred_element_type=jnp.float32)
def nt(a,b): return lax.dot_general(a,b,(((1,),(1,)),((),())),preferred_element_type=jnp.float32)
def tn(a,b): return lax.dot_general(a,b,(((0,),(0,)),((),())),preferred_element_type=jnp.float32)

def front_kernel(n, fused, micro, T, D, FF, CACHE, NBLK, *refs):
    it=iter(refs)
    take=lambda k:[next(it) for _ in range(k)]
    x_hbm,og_hbm,docs,mk_hbm,mv_hbm,midx,mreset=take(7)
    ins=take(8)
    (so_hbm,ig_hbm,gsum,e_h,normed_h,mixed_h,n2_h,hidden_h,gi_h,ui_h,ai_h,dq_h,dk_h,dv_h)=take(14)
    bufs=take(8)
    (cur,eg,normed,q,k,v,mixed,n2,g,u,hidden,middle,p,rk,rv,grads,mg,acc,so,ig,mask,gain)=take(22)
    (own_sem,in_sem,c_sem,out_sem,xs,xr,es,er)=take(8)
    ag_sems=take(8)
    B16=jnp.bfloat16
    W=[b.reshape(b.shape[0]*b.shape[1],b.shape[2]) if fused else b for b in bufs[1:]]
    Wq,Wk,Wv,Wo,Wg,Wu,Wd=W
    sec=lax.axis_index("section"); f=lax.axis_index("fsdp")
    scale=HD**-0.5
    R,C=layout(n)
    c=f%2; zy=f//2; y=zy%C; z=zy//C
    def dev(d): return (sec,(d[0]*C+d[1])*2+d[2])
    pieces=[(i,None) for i in range(7)]+[(7,j) for j in range(D//XC)]
    NP=len(pieces)
    nb=[(c>=0,(1-sec,f))]
    if fused:
        nb+=[(z>0,dev((z-1,y,c))),(z<R-1,dev((z+1,y,c))),(y>0,dev((z,y-1,c))),(y<C-1,dev((z,y+1,c))),(c>=0,dev((z,y,1-c)))]
    bar=pltpu.get_barrier_semaphore()
    for cond,d in nb:
        @pl.when(cond)
        def _(d=d): pl.semaphore_signal(bar,1,device_id=d,device_id_type=MESH)
    def own_copy(i):
        return pltpu.make_async_copy(ins[i],bufs[i].at[f] if fused else bufs[i],own_sem.at[i])
    for i in range(8): own_copy(i).start()
    def load_cur(): return pltpu.make_async_copy(x_hbm,cur,in_sem.at[0])
    def load_eg(): return pltpu.make_async_copy(og_hbm,eg,in_sem.at[0])
    HC=CACHE//2
    def load_cache(m,kv):
        src=(mk_hbm,mv_hbm)[kv]
        return [pltpu.make_async_copy(src.at[m,pl.ds(i*HC,HC)],grads.at[2*kv+i],c_sem.at[2*kv+i]) for i in range(2)]
    @pl.when(sec==0)
    def _(): load_cur().start()
    @pl.when(sec==1)
    def _():
        for kv in range(2):
            for cp in load_cache(0,kv): cp.start()
        load_eg().start()
    def save(j,src,dst,m):
        return pltpu.make_async_copy(src.at[m],dst.at[m],out_sem.at[j,m])
    def xcopy(m,j):
        cs=pl.ds(j*XC,XC)
        return pltpu.make_async_remote_copy(so.at[m,:,cs],cur.at[m,:,cs],xs.at[m,j],xr.at[m,j],device_id=(1-sec,f),device_id_type=MESH)
    def ecopy(m):
        return pltpu.make_async_remote_copy(ig.at[m],eg.at[m],es.at[m],er.at[m],device_id=(1-sec,f),device_id_type=MESH)
    RB=64
    def rows_loop(fn):
        def b(i,_):
            fn(pl.ds(pl.multiple_of(i*RB,RB),RB)); return 0
        lax.fori_loop(0,T//RB,b,0)
    def cols_loop(N,CH,fn):
        def b(i,_):
            fn(pl.ds(pl.multiple_of(i*CH,CH),CH)); return 0
        lax.fori_loop(0,N//CH,b,0,unroll=N//CH)
    def normalize(x,row):
        inv=lax.rsqrt(jnp.mean(x*x,axis=-1,keepdims=True)+EPS)
        return x*inv*gain[row:row+1,:]
    def norm_back(x,cc,row):
        inv=lax.rsqrt(jnp.mean(x*x,axis=-1,keepdims=True)+EPS)
        s=cc*gain[row:row+1,:]
        gsum[row:row+1,:]+=jnp.sum(cc*x*inv,axis=0,keepdims=True)
        return inv*s-x*(inv*inv*inv)*jnp.mean(s*x,axis=-1,keepdims=True)
    def f_norm(m):
        def f1(r): normed[m,r,:]=normalize(cur[m,r,:].astype(jnp.float32),0).astype(B16)
        rows_loop(f1)
        save(0,normed,normed_h,m).start()
    def f_proj(m,dst,w):
        def f2(cs): dst[m,:,cs]=nn(normed[m],w[:,cs]).astype(B16)
        cols_loop(D,256,f2)
    def f_attend(m,recall):
        def head(h,_):
            hs=pl.ds(pl.multiple_of(h*HD,HD),HD)
            qh=q[m,:,hs]; kh=k[m,:,hs]; vh=v[m,:,hs]
            s=jnp.where(mask[m].astype(jnp.float32)>0.5,nt(qh,kh)*scale,MASKED)
            if not recall:
                es_=jnp.exp(s-jnp.max(s,axis=-1,keepdims=True))
                ps=(es_*(1.0/jnp.sum(es_,axis=-1,keepdims=True))).astype(B16)
                p[m,h,:,0:T]=ps
                mixed[m,:,hs]=nn(ps,vh).astype(B16)
                return 0
            sr=[]
            for b in range(NBLK):
                x=nt(qh[b*MQB:(b+1)*MQB],rk[m,b*MEMK:(b+1)*MEMK,hs])*scale
                sr.append(jnp.where(jnp.broadcast_to(mreset[m,b:b+1,:]==0,(MQB,MEMK)),x,MASKED))
            sr=jnp.concatenate(sr,axis=0)
            top=jnp.maximum(jnp.max(s,axis=-1,keepdims=True),jnp.max(sr,axis=-1,keepdims=True))
            es_=jnp.exp(s-top); er_=jnp.exp(sr-top)
            inv=1.0/(jnp.sum(es_,axis=-1,keepdims=True)+jnp.sum(er_,axis=-1,keepdims=True))
            ps=(es_*inv).astype(B16); pr=(er_*inv).astype(B16)
            p[m,h,:,0:T]=ps; p[m,h,:,T:T+MEMK]=pr
            mr=jnp.concatenate([nn(pr[b*MQB:(b+1)*MQB],rv[m,b*MEMK:(b+1)*MEMK,hs]) for b in range(NBLK)],axis=0)
            mixed[m,:,hs]=(nn(ps,vh)+mr).astype(B16)
            return 0
        lax.fori_loop(0,HEADS,head,0,unroll=HEADS)
        save(1,mixed,mixed_h,m).start()
    def f_out(m):
        def f3(cs): middle[m,:,cs]=cur[m,:,cs].astype(jnp.float32)+nn(mixed[m],Wo[:,cs])
        cols_loop(D,256,f3)
        def f4(r): n2[m,r,:]=normalize(middle[m,r,:],1).astype(B16)
        rows_loop(f4)
        save(2,n2,n2_h,m).start()
    def f_gate(m):
        def f5(cs):
            a=n2[m]
            gg=nn(a,Wg[:,cs]); uu=nn(a,Wu[:,cs])
            g[m,:,cs]=gg.astype(B16); u[m,:,cs]=uu.astype(B16)
            hidden[m,:,cs]=(gg*jax.nn.sigmoid(gg)*uu).astype(B16)
        cols_loop(FF,256,f5)
        save(3,hidden,hidden_h,m).start()
    def f_down(m,j):
        cs=pl.ds(j*XC,XC)
        so[m,:,cs]=(middle[m,:,cs]+nn(hidden[m],Wd[:,cs])).astype(B16)
    def recall(m,kv):
        for cp in load_cache(m,kv): cp.wait()
        dst=(rk,rv)[kv]
        def body(b,_):
            idx=midx[m,pl.ds(b,1),:]
            col=jnp.broadcast_to(idx.astype(jnp.float32),(MEMK,MEMK)).T[:,0:1].astype(jnp.int32)
            io=lax.broadcasted_iota(jnp.int32,(MEMK,HC),1)
            rows=nn(jnp.where(io==col,1.0,0.0).astype(B16),grads[2*kv])
            rows=rows+nn(jnp.where(io+HC==col,1.0,0.0).astype(B16),grads[2*kv+1])
            dst[m,pl.ds(pl.multiple_of(b*MEMK,MEMK),MEMK),:]=rows.astype(B16)
            return 0
        lax.fori_loop(0,NBLK,body,0)
        if m+1<micro:
            for cp in load_cache(m+1,kv): cp.start()
    def setup():
        parts=bufs[0][...]
        gain[...]=jnp.sum(parts.astype(jnp.float32),axis=0)[0:8]
    def each(fn):
        def b(m,_):
            fn(m); return 0
        return lambda: lax.fori_loop(0,micro,b,0)
    def down(j):
        def go():
            def b(m,_):
                f_down(m,j); xcopy(m,j).start(); return 0
            lax.fori_loop(0,micro,b,0)
        return go
    first={0:[each(f_norm)],1:[each(lambda m:f_proj(m,q,Wq))],2:[each(lambda m:f_proj(m,k,Wk))],
        3:[each(lambda m:f_proj(m,v,Wv)),lambda:f_attend(0,False)],
        4:[lambda:[f_attend(m,False) for m in range(1,micro)],each(f_out)],
        6:[each(f_gate)]}
    for j in range(D//XC): first[7+j]=[down(j)]
    units=[(m,kv) for m in range(micro) for kv in range(2)]
    second={i:[functools.partial(recall,*un)] for i,un in enumerate(units)}
    def arrived(i):
        if i==0: setup()
        @pl.when(sec==0)
        def _():
            for fn in first.get(i,[]): fn()
        @pl.when(sec==1)
        def _():
            for fn in second.get(i,[]): fn()
    gsum[...]=jnp.zeros_like(gsum)
    ri=lax.broadcasted_iota(jnp.int32,(T,T),0); ci=lax.broadcasted_iota(jnp.int32,(T,T),1)
    def prepare():
        for m in range(micro):
            row=jnp.broadcast_to(docs[m:m+1,:].astype(jnp.float32),(T,T))
            mask[m]=jnp.where((row==row.T)&(ci<=ri),1.0,0.0).astype(B16)
        @pl.when(sec==0)
        def _():
            def zero(i,_):
                o=pl.ds(pl.multiple_of(i*MEMK,MEMK),MEMK)
                for m in range(micro):
                    rk[m,o,:]=jnp.zeros((MEMK,D),B16); rv[m,o,:]=jnp.zeros((MEMK,D),B16)
                return 0
            lax.fori_loop(0,NBLK,zero,0)
            def zero_p(h,_):
                for m in range(micro): p[m,h,:,T:T+MEMK]=jnp.zeros((T,MEMK),B16)
                return 0
            lax.fori_loop(0,HEADS,zero_p,0)
            load_cur().wait()
        @pl.when(sec==1)
        def _(): load_eg().wait()
    pl.semaphore_wait(bar,sum(jnp.where(cond,1,0) for cond,d in nb))
    pending=[]
    if fused:
        s_zu,s_zd,s_yu,s_yd,s_sb,s_ex,r_main,r_sib=ag_sems
        def part(i,blk):
            b,j=pieces[i]
            return bufs[b].at[blk] if j is None else bufs[b].at[blk,:,pl.ds(j*XC,XC)]
        def send(cond,i,zb,yb,target,ssem,rsem):
            blk=(zb*C+yb)*2+c; kk=zb*C+yb
            def mk():
                return pltpu.make_async_remote_copy(part(i,blk),part(i,blk),ssem.at[i,kk],rsem.at[i,kk],device_id=dev(target),device_id_type=MESH)
            @pl.when(cond)
            def _(): mk().start()
            pending.append((cond,mk))
        def wait_main(cond,i,zb,yb):
            blk=(zb*C+yb)*2+c; kk=zb*C+yb
            @pl.when(cond)
            def _():
                pltpu.make_async_remote_copy(part(i,blk),part(i,blk),s_sb.at[i,kk],r_main.at[i,kk],device_id=dev((z,y,1-c)),device_id_type=MESH).wait_recv()
        offload=(C==2 and R%2==0)
        zx=z+1-2*(z%2)
        true=c>=0
        def own(i):
            b,j=pieces[i]
            if not j: own_copy(b).wait()
            send(y>0,i,z,y,(z,y-1,c),s_yd,r_main)
            send(y<C-1,i,z,y,(z,y+1,c),s_yu,r_main)
            send(z>0,i,z,y,(z-1,y,c),s_zd,r_main)
            send(z<R-1,i,z,y,(z+1,y,c),s_zu,r_main)
            send(true,i,z,y,(z,y,1-c),s_sb,r_sib)
        def z_arrivals(i):
            for d in range(1,R):
                for sign in (-1,1):
                    zb=z+sign*d
                    ok=(zb>=0)&(zb<R)
                    zbc=jnp.clip(zb,0,R-1)
                    wait_main(ok,i,zbc,y)
                    if sign<0: send(ok&(z<R-1),i,zbc,y,(z+1,y,c),s_zu,r_main)
                    else: send(ok&(z>0),i,zbc,y,(z-1,y,c),s_zd,r_main)
                    ydo=ok&jnp.logical_not((c==1)&(zbc==zx)) if offload else ok
                    send(ydo&(y>0),i,zbc,y,(z,y-1,c),s_yd,r_main)
                    send(ydo&(y<C-1),i,zbc,y,(z,y+1,c),s_yu,r_main)
                    send(ok,i,zbc,y,(z,y,1-c),s_sb,r_sib)
        def y_arrivals(i,near):
            for dy in range(1,C):
                for sign in (-1,1):
                    yb=y+sign*dy
                    oky=(yb>=0)&(yb<C)
                    ybc=jnp.clip(yb,0,C-1)
                    for d in ([0] if near else range(1,R)):
                        for zs in ((0,) if d==0 else (-1,1)):
                            zb=z+zs*d
                            ok=oky&(zb>=0)&(zb<R)
                            zbc=jnp.clip(zb,0,R-1)
                            wait_main(ok,i,zbc,ybc)
                            if C>2:
                                if sign<0: send(ok&(y<C-1),i,zbc,ybc,(z,y+1,c),s_yu,r_main)
                                else: send(ok&(y>0),i,zbc,ybc,(z,y-1,c),s_yd,r_main)
                            if offload and d==0:
                                send(ok&(c==1),i,zbc,ybc,(zx,y,c),s_ex,r_main)
                            send(ok,i,zbc,ybc,(z,y,1-c),s_sb,r_sib)
        def finish(i):
            def body(kk,_):
                blk=kk*2+1-c
                pltpu.make_async_remote_copy(part(i,blk),part(i,blk),s_sb.at[i,kk],r_sib.at[i,kk],device_id=dev((z,y,1-c)),device_id_type=MESH).wait_recv()
                return 0
            lax.fori_loop(0,n//2,body,0)
        LA=2
        for i in range(LA): own(i)
        prepare()
        for i in range(NP+2):
            if i+LA<NP: own(i+LA)
            if i<NP: z_arrivals(i)
            if 0<=i-1<NP: y_arrivals(i-1,True)
            if 0<=i-2<NP:
                y_arrivals(i-2,False)
                finish(i-2)
                arrived(i-2)
    else:
        prepare()
        for i in range(NP):
            b,j=pieces[i]
            if not j: own_copy(b).wait()
            arrived(i)
    @pl.when(sec==1)
    def _():
        def forward(m,_):
            for j in range(D//XC): xcopy(m,j).wait_recv()
            f_norm(m)
            f_proj(m,q,Wq); f_proj(m,k,Wk); f_proj(m,v,Wv)
            f_attend(m,True)
            f_out(m)
            f_gate(m)
            for j in range(D//XC): f_down(m,j)
            return 0
        lax.fori_loop(0,micro,forward,0)
    def gsave(j,i,dst,m): return pltpu.make_async_copy(grads.at[i,pl.ds(pl.multiple_of(m*T,T),T)],dst.at[m],out_sem.at[j,m])
    def backward(m,_):
        @pl.when(sec==0)
        def _(): ecopy(m).wait_recv()
        save(4,so,so_hbm,m).start()
        save(5,eg,e_h,m).start()
        def b1(cs):
            hg=nt(eg[m],Wd[cs,:])
            gg=g[m,:,cs].astype(jnp.float32); uu=u[m,:,cs].astype(jnp.float32)
            sg=jax.nn.sigmoid(gg)
            u[m,:,cs]=(hg*gg*sg).astype(B16)
            g[m,:,cs]=(hg*uu*sg*(1.0+gg*(1.0-sg))).astype(B16)
        cols_loop(FF,256,b1)
        save(6,g,gi_h,m).start(); save(7,u,ui_h,m).start()
        def b2(cs): acc[:,cs]=nt(g[m],Wg[cs,:])+nt(u[m],Wu[cs,:])
        cols_loop(D,256,b2)
        ms=pl.ds(pl.multiple_of(m*T,T),T)
        def b3(r):
            t_=eg[m,r,:].astype(jnp.float32)+norm_back(middle[m,r,:],acc[r,:],1)
            mg[r,:]=t_; grads[0,pl.ds(pl.multiple_of(m*T,T)+r.start,RB),:]=t_.astype(B16)
        rows_loop(b3)
        gsave(8,0,ai_h,m).start()
        save(0,normed,normed_h,m).wait()
        def b4(cs): normed[m,:,cs]=nt(grads[0,ms,:],Wo[cs,:]).astype(B16)
        cols_loop(D,256,b4)
        def head(h,_):
            hs=pl.ds(pl.multiple_of(h*HD,HD),HD)
            qh=q[m,:,hs]; kh=k[m,:,hs]; vh=v[m,:,hs]; mh=normed[m,:,hs]
            ps=p[m,h,:,0:T]; pr=p[m,h,:,T:T+MEMK]
            grads[3,ms,hs]=tn(ps,mh).astype(B16)
            pg=nt(mh,vh)
            rg=jnp.concatenate([nt(mh[b*MQB:(b+1)*MQB],rv[m,b*MEMK:(b+1)*MEMK,hs]) for b in range(NBLK)],axis=0)
            pf=ps.astype(jnp.float32); rf=pr.astype(jnp.float32)
            w=jnp.sum(pf*pg,axis=-1,keepdims=True)+jnp.sum(rf*rg,axis=-1,keepdims=True)
            ds=(pf*(pg-w)).astype(B16); dr=(rf*(rg-w)).astype(B16)
            qr=jnp.concatenate([nn(dr[b*MQB:(b+1)*MQB],rk[m,b*MEMK:(b+1)*MEMK,hs]) for b in range(NBLK)],axis=0)
            grads[1,ms,hs]=((nn(ds,kh)+qr)*scale).astype(B16)
            grads[2,ms,hs]=(tn(ds,qh)*scale).astype(B16)
            return 0
        lax.fori_loop(0,HEADS,head,0,unroll=HEADS)
        gsave(9,1,dq_h,m).start(); gsave(10,2,dk_h,m).start(); gsave(11,3,dv_h,m).start()
        def b5(cs): acc[:,cs]=nt(grads[1,ms,:],Wq[cs,:])+nt(grads[2,ms,:],Wk[cs,:])+nt(grads[3,ms,:],Wv[cs,:])
        cols_loop(D,256,b5)
        def b6(r): ig[m,r,:]=(mg[r,:]+norm_back(cur[m,r,:].astype(jnp.float32),acc[r,:],0)).astype(B16)
        rows_loop(b6)
        @pl.when(sec==1)
        def _(): ecopy(m).start()
        save(12,ig,ig_hbm,m).start()
        return 0
    lax.fori_loop(0,micro,backward,0)
    for cond,mk in pending:
        @pl.when(cond)
        def _(mk=mk): mk().wait_send()
    for m in range(micro):
        @pl.when(sec==0)
        def _():
            for j in range(D//XC): xcopy(m,j).wait_send()
        @pl.when(sec==1)
        def _(): ecopy(m).wait_send()
        for j,(s,d) in enumerate([(mixed,mixed_h),(n2,n2_h),(hidden,hidden_h),(so,so_hbm),(eg,e_h),(g,gi_h),(u,ui_h)],1):
            save(j,s,d,m).wait()
        for j,i,d in ((8,0,ai_h),(9,1,dq_h),(10,2,dk_h),(11,3,dv_h)):
            gsave(j,i,d,m).wait()
        save(12,ig,ig_hbm,m).wait()

def front(n, fused, x, og, docs, mk, mv, midx, mreset, vec, weights, cid=2):
    micro,T,D=x.shape
    FF=weights[4].shape[1]
    CACHE=mk.shape[1]; NBLK=midx.shape[1]
    B=jnp.bfloat16; F=jnp.float32
    V=pltpu.VMEM
    act=(micro,T,D); fact=(micro,T,FF)
    S=jax.ShapeDtypeStruct
    outs=[S(act,B),S(act,B),S((8,D),F),S(act,B),S(act,B),S(act,B),S(act,B),S(fact,B),S(fact,B),S(fact,B),S(act,B),S(act,B),S(act,B),S(act,B)]
    ws=[vec]+list(weights)
    scratch=[V((n,)+w.shape if fused else w.shape,B) for w in ws]
    scratch+=[V(act,B)]*8+[V(fact,B)]*3+[V(act,F),V((micro,HEADS,T,T+MEMK),B),V((micro,NBLK*MEMK,D),B),V((micro,NBLK*MEMK,D),B),V((4,micro*T,D),B),V((T,D),F),V((T,D),F),V(act,B),V(act,B),V((micro,T,T),B),V((8,D),F)]
    DM=pltpu.SemaphoreType.DMA
    NP=7+D//XC
    scratch+=[DM((8,)),DM((2,)),DM((4,)),DM((13,micro)),DM((micro,D//XC)),DM((micro,D//XC)),DM((micro,)),DM((micro,))]
    scratch+=[DM((NP,n//2) if fused else (1,))]*8
    HB=pl.BlockSpec(memory_space=pltpu.HBM); VB=pl.BlockSpec(memory_space=pltpu.VMEM)
    reset=jnp.broadcast_to(mreset[:,:,None],(micro,NBLK,MEMK))
    return pl.pallas_call(functools.partial(front_kernel,n,fused,micro,T,D,FF,CACHE,NBLK),
        out_shape=outs,
        in_specs=[HB,HB,VB,HB,HB,VB,VB]+[HB]*8,
        out_specs=[HB,HB,VB]+[HB]*11,
        scratch_shapes=scratch,
        compiler_params=pltpu.CompilerParams(collective_id=cid,has_side_effects=True,vmem_limit_bytes=64<<20),
    )(x,og,docs,mk,mv,midx,reset,*ws)


COLS=1024
def plan(n, lhs_shapes, rhs_shapes, weights):
    pieces=[]
    for w,(l,r) in enumerate(weights):
        rows=lhs_shapes[l][1]//n; N=rhs_shapes[r][1]
        step=512 if rows>64*16//n else 1024
        for c0 in range(0,N,step):
            pieces.append((w,rows,c0,min(step,N-c0)))
    return pieces

def reduce_kernel(n, tok, lhs_shapes, rhs_shapes, weights, pieces, vec_rows, SLOTS, *refs):
    NP=len(pieces); NL=len(lhs_shapes); NR=len(rhs_shapes); NW=len(weights)
    R,C=layout(n); H=n//2
    it=iter(refs)
    take=lambda k:[next(it) for _ in range(k)]
    lhs=take(NL); rhs=take(NR); vec=next(it)
    outs=take(NW); vec_out=next(it)
    ring=next(it); tbuf=take(NL)
    keep=take(NP); sibr=take(NP); yr=take(NP); xr=take(NP); zu=take(NP); zd=take(NP); fin=take(NP)
    shapes=sorted({(p[1],p[3]) for p in pieces})
    stage_of=dict(zip(shapes,take(len(shapes))))
    vecb=next(it); vecr=next(it)
    (ld_sem,sib_s,sib_r,y_s,y_r,x_s,x_r,zu_s,zu_r,zd_s,zd_r,v_s,v_r,o_s)=take(14)
    sec=lax.axis_index("section"); f=lax.axis_index("fsdp")
    c=f%2; zy=f//2; y=zy%C; z=zy//C
    offload=(C==2 and R%2==0)
    zx=z+1-2*(z%2)
    def dev(zz,yy,cc): return (sec,(zz*C+yy)*2+cc)
    def rcopy(src,dst,ss,rs,d):
        return pltpu.make_async_remote_copy(src,dst,ss,rs,device_id=dev(*d),device_id_type=MESH)
    LOGN=n.bit_length()-1
    nb=[]
    nb.append((c>=0,dev(z,y,1-c)))
    for k in range(1,C): nb.append((c>=0,dev(z,lax.rem(y+k,C),c)))
    nb.append((z>0,dev(z-1,y,c))); nb.append((z<R-1,dev(z+1,y,c)))
    for k in range(1,R.bit_length()-1): nb.append((c>=0,(sec,f^(2*C<<k))))
    bar=pltpu.get_barrier_semaphore()
    loads=[]
    def parts(ref,shape):
        return [(ref,c0,min(COLS,shape[1]-c0)) for c0 in range(0,shape[1],COLS)]
    load_id={}
    def need(kind,i):
        key=(kind,i)
        if key in load_id: return
        ref=lhs[i] if kind=="l" else rhs[i]
        sh=lhs_shapes[i] if kind=="l" else rhs_shapes[i]
        ids=[]
        for pr in parts(ref,sh):
            ids.append(len(loads)); loads.append(pr)
        load_id[key]=ids
    for l,r in weights:
        need("l",l); need("r",r)
    issued=[0]; freed=set()
    def load_copy(k):
        ref,c0,w=loads[k]
        return pltpu.make_async_copy(ref.at[:,pl.ds(c0,w)],ring.at[k%SLOTS,:,pl.ds(0,w)],ld_sem.at[k%SLOTS])
    def pump():
        while issued[0]<len(loads) and (issued[0]<SLOTS or (issued[0]-SLOTS) in freed):
            load_copy(issued[0]).start(); issued[0]+=1
    pump()
    for cond,d in nb:
        @pl.when(cond)
        def _(): pl.semaphore_signal(bar,1,device_id=d,device_id_type=MESH)
    waited=set()
    def wait_load(k):
        if k not in waited:
            load_copy(k).wait(); waited.add(k)
    transposed=set()
    def ensure_lhs(l):
        if l in transposed: return
        transposed.add(l)
        for j,k in enumerate(load_id[("l",l)]):
            wait_load(k)
            w=loads[k][2]
            CH=256
            def body(i,_,k=k,j=j):
                o=pl.multiple_of(i*CH,CH)
                tbuf[l][pl.ds(pl.multiple_of(j*COLS+o,CH),CH),:]=ring[k%SLOTS,:,pl.ds(o,CH)].T
                return 0
            lax.fori_loop(0,w//CH,body,0)
            freed.add(k)
        pump()
    last_use={}
    for i,(w,rows,c0,nc) in enumerate(pieces):
        l,r=weights[w]
        last_use[load_id[("r",r)][c0//COLS]]=i
    sends=[]
    stage_use={}
    def compute(i):
        w,rows,c0,nc=pieces[i]
        l,r=weights[w]
        ensure_lhs(l)
        k=load_id[("r",r)][c0//COLS]
        wait_load(k)
        lc=c0%COLS
        st=stage_of[(rows,nc)]
        u=stage_use.get((rows,nc),0); stage_use[(rows,nc)]=u+1
        slot=u%2
        if u>=2: sib_waits[(rows,nc)].pop(0)()
        T4=tbuf[l].reshape(H,2,rows,tok)
        CH=256
        for which,dst in ((1-c,st.at[slot]),(c,keep[i])):
            def body(j,_,which=which,dst=dst):
                o=pl.multiple_of(j*CH,CH)
                a=T4[:,which].reshape(H*rows,tok)
                b=ring[k%SLOTS,:,pl.ds(pl.multiple_of(lc+o,CH),CH)]
                res=jnp.dot(a,b,preferred_element_type=jnp.float32).astype(jnp.bfloat16)
                dst[:,:,pl.ds(o,CH)]=res.reshape(H,rows,CH)
                return 0
            lax.fori_loop(0,nc//CH,body,0)
            if dst is not keep[i]:
                cp=rcopy(st.at[slot],sibr[i],sib_s.at[i],sib_r.at[i],(z,y,1-c))
                cp.start()
                sib_waits.setdefault((rows,nc),[]).append(cp.wait_send)
        if last_use[k]==i:
            freed.add(k); pump()
    sib_waits={}
    def add_into(dst,src,rows):
        def body(j,_):
            o=pl.multiple_of(j*16,16)
            dst[pl.ds(o,16),:]=dst[pl.ds(o,16),:]+src[pl.ds(o,16),:]
            return 0
        lax.fori_loop(0,rows//16,body,0)
    def send(cond,cp):
        if cond is None: cp().start()
        else:
            @pl.when(cond)
            def _(): cp().start()
        sends.append((cond,cp))
    def sib_add(i):
        w,rows,c0,nc=pieces[i]
        rcopy(sibr[i],sibr[i],sib_s.at[i],sib_r.at[i],(z,y,1-c)).wait_recv()
        def body(k,_):
            add_into(keep[i].at[k],sibr[i].at[k],rows)
            return 0
        lax.fori_loop(0,H,body,0)
        if offload:
            send(c==1,lambda: rcopy(keep[i].at[zx*C+1-y],xr[i],x_s.at[i],x_r.at[i],(zx,y,c)))
        for kz in range(R-1,-1,-1):
            zt=lax.rem(z+kz,R)
            for ky in range(1,C):
                yt=lax.rem(y+ky,C)
                slot=C-1-ky
                cp=lambda zt=zt,yt=yt,slot=slot: rcopy(keep[i].at[zt*C+yt],yr[i].at[slot,zt],y_s.at[i,slot,zt],y_r.at[i,slot,zt],(z,yt,c))
                if offload and kz==0:
                    continue
                send((jnp.logical_not((c==1)&(zt==zx))) if offload else None,cp)
    def x_add(i):
        w,rows,c0,nc=pieces[i]
        if not offload: return
        @pl.when(c==1)
        def _():
            rcopy(xr[i],xr[i],x_s.at[i],x_r.at[i],(zx,y,c)).wait_recv()
            add_into(keep[i].at[z*C+1-y],xr[i],rows)
        send(None,lambda: rcopy(keep[i].at[z*C+1-y],yr[i].at[0,z],y_s.at[i,0,z],y_r.at[i,0,z],(z,1-y,c)))
    def y_add(i):
        w,rows,c0,nc=pieces[i]
        for kz in range(R-1,-1,-1):
            zt=lax.rem(z+kz,R)
            for slot in range(C-1):
                def go(zt=zt,slot=slot):
                    rcopy(yr[i].at[slot,zt],yr[i].at[slot,zt],y_s.at[i,slot,zt],y_r.at[i,slot,zt],(z,y,1-c)).wait_recv()
                    add_into(keep[i].at[zt*C+y],yr[i].at[slot,zt],rows)
                if offload and kz!=0:
                    pl.when(jnp.logical_not((c==1)&(zt==zx)))(go)
                else: go()
    def z_step(i,s):
        w,rows,c0,nc=pieces[i]
        def line(zs,up):
            rb,rr,ss=(zu,zu_r,zu_s) if up else (zd,zd_r,zd_s)
            first=(zs==0) if up else (zs==R-1)
            targets=range(R-1,zs,-1) if up else range(0,zs)
            nxt=zs+1 if up else zs-1
            cps=[]
            for t in targets:
                k=abs(t-zs)
                cps.append((k,lambda t=t,k=k: rcopy(keep[i].at[t*C+y],rb[i].at[k-1],ss.at[i,k-1],rr.at[i,k-1],(nxt,y,c)),t))
            def go():
                for k,cp,t in cps:
                    if not first:
                        rcopy(rb[i].at[k],rb[i].at[k],ss.at[i,k],rr.at[i,k],(zs,y,1-c)).wait_recv()
                        add_into(keep[i].at[t*C+y],rb[i].at[k],rows)
                    cp().start()
            pl.when(z==zs)(go)
            for k,cp,t in cps: sends.append((z==zs,cp))
        line(s,True)
        line(R-1-s,False)
    def final(i):
        w,rows,c0,nc=pieces[i]
        blk=z*C+y
        @pl.when(z>0)
        def _():
            rcopy(zu[i].at[0],zu[i].at[0],zu_s.at[i,0],zu_r.at[i,0],(z,y,1-c)).wait_recv()
        @pl.when(z<R-1)
        def _():
            rcopy(zd[i].at[0],zd[i].at[0],zd_s.at[i,0],zd_r.at[i,0],(z,y,1-c)).wait_recv()
        def body(j,_):
            o=pl.ds(pl.multiple_of(j*16,16),16)
            a=keep[i][blk,o,:].astype(jnp.float32)
            a=a+jnp.where(z>0,zu[i][0,o,:].astype(jnp.float32),0.0)+jnp.where(z<R-1,zd[i][0,o,:].astype(jnp.float32),0.0)
            fin[i][o,:]=a.astype(jnp.bfloat16)
            return 0
        lax.fori_loop(0,rows//16,body,0)
        pltpu.make_async_copy(fin[i],outs[w].at[:,pl.ds(c0,nc)],o_s.at[i]).start()
    def vec_step(k):
        if k>0:
            vcopy(k-1).wait()
            vecb[k]=vecb[k-1]+vecr[k-1]
        if k<LOGN: vcopy(k).start()
        else:
            cp=pltpu.make_async_copy(vecb.at[LOGN],vec_out,o_s.at[NP]); cp.start()
    def vcopy(k):
        return pltpu.make_async_remote_copy(vecb.at[k],vecr.at[k],v_s.at[k],v_r.at[k],device_id=(sec,f^(1<<k)),device_id_type=MESH)
    cp=pltpu.make_async_copy(vec,vecb.at[0],o_s.at[NP]); cp.start(); cp.wait()
    pl.semaphore_wait(bar,sum(jnp.where(cond,1,0) for cond,d in nb))
    LAGY=3
    for t in range(NP+LAGY+R+1):
        if t<NP: compute(t)
        if 0<=t-1<NP: sib_add(t-1)
        if 0<=t-2<NP: x_add(t-2)
        if t<=LOGN: vec_step(t)
        if 0<=t-LAGY<NP: y_add(t-LAGY)
        for s in range(R):
            i=t-LAGY-s
            if 0<=i<NP: z_step(i,s)
        i=t-LAGY-R
        if 0<=i<NP: final(i)
    for q in sib_waits.values():
        for wfn in q: wfn()
    for cond,cp in sends:
        if cond is None: cp().wait_send()
        else:
            @pl.when(cond)
            def _(): cp().wait_send()
    for i in range(NP):
        w,rows,c0,nc=pieces[i]
        pltpu.make_async_copy(fin[i],outs[w].at[:,pl.ds(c0,nc)],o_s.at[i]).wait()
    pltpu.make_async_copy(vecb.at[LOGN],vec_out,o_s.at[NP]).wait()

def reduce(n, lhs, rhs, weights, vec, cid=1, SLOTS=6):
    tok=lhs[0].shape[0]
    ls=[a.shape for a in lhs]; rs=[a.shape for a in rhs]
    pieces=plan(n,ls,rs,weights)
    R,C=layout(n); H=n//2
    NP=len(pieces)
    LOGN=n.bit_length()-1
    D=pltpu.SemaphoreType.DMA
    B=jnp.bfloat16
    V=pltpu.VMEM
    shapes=sorted({(p[1],p[3]) for p in pieces})
    scratch=[V((SLOTS,tok,COLS),B)]+[V((s[1],tok),B) for s in ls]
    scratch+=[V((H,p[1],p[3]),B) for p in pieces]
    scratch+=[V((H,p[1],p[3]),B) for p in pieces]
    scratch+=[V((C-1,R,p[1],p[3]),B) for p in pieces]
    scratch+=[V((p[1],p[3]) if C==2 else (16,128),B) for p in pieces]
    scratch+=[V((R-1,p[1],p[3]),B) for p in pieces]*2
    scratch+=[V((p[1],p[3]),B) for p in pieces]
    scratch+=[V((2,H)+s,B) for s in shapes]
    scratch+=[V((LOGN+1,)+vec.shape,vec.dtype),V((LOGN,)+vec.shape,vec.dtype)]
    scratch+=[D((SLOTS,)),D((NP,)),D((NP,)),D((NP,C-1,R)),D((NP,C-1,R)),D((NP,)),D((NP,)),D((NP,R-1)),D((NP,R-1)),D((NP,R-1)),D((NP,R-1)),D((LOGN,)),D((LOGN,)),D((NP+1,))]
    HB=pl.BlockSpec(memory_space=pltpu.HBM)
    res=pl.pallas_call(functools.partial(reduce_kernel,n,tok,ls,rs,weights,pieces,vec.shape[0],SLOTS),
        out_shape=[jax.ShapeDtypeStruct((ls[l][1]//n,rs[r][1]),B) for l,r in weights]+[jax.ShapeDtypeStruct(vec.shape,vec.dtype)],
        in_specs=[HB]*(len(lhs)+len(rhs)+1),
        out_specs=[HB]*(len(weights)+1),
        scratch_shapes=scratch,
        compiler_params=pltpu.CompilerParams(collective_id=cid,has_side_effects=True,vmem_limit_bytes=63<<20),
    )(*lhs,*rhs,vec)
    return res[:-1],res[-1]


def per_device(
    block_input, output_grad, document_ids, memory_keys, memory_values, memory_index, memory_reset,
    query_weight, key_weight, value_weight, output_weight, gate_weight, up_weight, down_weight,
    attend_gain, feed_gain,
):
    n = lax.axis_size("fsdp")
    f = lax.axis_index("fsdp")
    micro, T, D = block_input.shape
    FF = gate_weight.shape[2]
    gw = attend_gain.shape[1]
    vec = jnp.zeros((16, D), jnp.bfloat16)
    vec = lax.dynamic_update_slice(vec, jnp.concatenate([attend_gain, feed_gain]), (0, f * gw))
    shards = [w[0] for w in (query_weight, key_weight, value_weight, output_weight, gate_weight, up_weight, down_weight)]
    rows = [s.shape[0] for s in shards]
    fused = all(s % 16 == 0 for s in rows)
    if not fused:
        padded = [jnp.pad(s, ((0, -s.shape[0] % 16), (0, 0))) for s in shards]
        gathered = gather(n, [vec] + padded, 0)
        vec = jnp.sum(gathered[0], axis=0, keepdims=True)
        shards = [g[:, :r].reshape(n * r, g.shape[2]) for g, r in zip(gathered[1:], rows)]
    (so, ig, gsum, e, normed, mixed, n2, hidden, gi, ui, ai, dq, dk, dv) = front(
        n, fused, block_input, output_grad, document_ids, memory_keys, memory_values, memory_index, memory_reset, vec, shards, 2)
    flat = lambda a: a.reshape(micro * T, a.shape[2])
    hid = flat(hidden)
    rd = rows[6]
    if rd % 16:
        hid = jnp.pad(hid.reshape(micro * T, n, rd), ((0, 0), (0, 0), (0, -rd % 16))).reshape(micro * T, -1)
    lhs = [hid, flat(n2), flat(mixed), flat(normed)]
    rhs = [flat(a) for a in (e, gi, ui, ai, dv, dk, dq)]
    order = [(0, 0), (1, 1), (1, 2), (2, 3), (3, 4), (3, 5), (3, 6)]
    sums, total = reduce(n, lhs, rhs, order, gsum, 1)
    gd, gg, gu, go, gv, gk, gq = sums
    gains = lax.dynamic_slice(total, (0, f * gw), (2, gw)).astype(jnp.bfloat16)
    return (so[None], ig[None], gq[None], gk[None], gv[None], go[None], gg[None], gu[None], gd[:rd][None], gains[0:1], gains[1:2])


def solution(mesh):
    w = P("section", "fsdp", None)
    r = P(None, "fsdp", None)
    v = P("section", "fsdp")
    return jax.shard_map(
        per_device,
        mesh=mesh,
        in_specs=(r, r, P(None, "fsdp"), r, r, r, P(None, "fsdp")) + (w,) * 7 + (v, v),
        out_specs=(P("section", None, "fsdp", None),) * 2 + (w,) * 7 + (v, v),
        check_vma=False,
    )
```

```python
import functools
import math
import jax
import jax.numpy as jnp
from jax import lax
from jax.experimental import pallas as pl
from jax.experimental.pallas import tpu as pltpu
from jax.sharding import PartitionSpec as P

MESH = pl.DeviceIdType.MESH


def layout(n):
    rest=n//2
    R=min(4,rest); C=rest//R
    return R,C

def gather_kernel(n, P, *refs):
    ins=refs[:P]; outs=refs[P:2*P]; bufs=refs[2*P:3*P]
    own_sem,out_sem,s_zu,s_zd,s_yu,s_yd,s_sb,s_ex,r_main,r_sib=refs[3*P:]
    R,C=layout(n)
    sec=lax.axis_index("section"); f=lax.axis_index("fsdp")
    c=f%2; zy=f//2; y=zy%C; z=zy//C
    def dev(zz,yy,cc): return (sec,(zz*C+yy)*2+cc)
    bar=pltpu.get_barrier_semaphore()
    nb=[(z>0,(z-1,y,c)),(z<R-1,(z+1,y,c)),(y>0,(z,y-1,c)),(y<C-1,(z,y+1,c)),(c>=0,(z,y,1-c))]
    for p in range(P):
        pltpu.make_async_copy(ins[p],bufs[p].at[f],own_sem.at[p]).start()
    for cond,d in nb:
        @pl.when(cond)
        def _():
            pl.semaphore_signal(bar,1,device_id=dev(*d),device_id_type=MESH)
    pl.semaphore_wait(bar,sum(jnp.where(cond,1,0) for cond,d in nb))
    pending=[]
    def send(cond,p,zb,yb,target,ssem,rsem):
        blk=(zb*C+yb)*2+c
        k=zb*C+yb
        def mk():
            return pltpu.make_async_remote_copy(bufs[p].at[blk],bufs[p].at[blk],ssem.at[p,k],rsem.at[p,k],device_id=dev(*target),device_id_type=MESH)
        @pl.when(cond)
        def _(): mk().start()
        pending.append((cond,mk))
    def wait_main(cond,p,zb,yb):
        blk=(zb*C+yb)*2+c; k=zb*C+yb
        @pl.when(cond)
        def _():
            pltpu.make_async_remote_copy(bufs[p].at[blk],bufs[p].at[blk],s_sb.at[p,k],r_main.at[p,k],device_id=dev(z,y,1-c),device_id_type=MESH).wait_recv()
    offload = (C==2)
    T=(c>=0)
    def own(p):
        pltpu.make_async_copy(ins[p],bufs[p].at[f],own_sem.at[p]).wait()
        send(y>0,p,z,y,(z,y-1,c),s_yd,r_main)
        send(y<C-1,p,z,y,(z,y+1,c),s_yu,r_main)
        send(z>0,p,z,y,(z-1,y,c),s_zd,r_main)
        send(z<R-1,p,z,y,(z+1,y,c),s_zu,r_main)
        send(T,p,z,y,(z,y,1-c),s_sb,r_sib)
    def z_arrivals(p):
        for d in range(1,R):
            for sign in (-1,1):
                zb=z+sign*d
                ok=(zb>=0)&(zb<R)
                zbc=jnp.clip(zb,0,R-1)
                wait_main(ok,p,zbc,y)
                if sign<0:
                    send(ok&(z<R-1),p,zbc,y,(z+1,y,c),s_zu,r_main)
                else:
                    send(ok&(z>0),p,zbc,y,(z-1,y,c),s_zd,r_main)
                ydo=ok
                if offload: ydo=ok & jnp.logical_not((c==1)&(zbc==(z+1-2*(z%2))))
                send(ydo&(y>0),p,zbc,y,(z,y-1,c),s_yd,r_main)
                send(ydo&(y<C-1),p,zbc,y,(z,y+1,c),s_yu,r_main)
                send(ok,p,zbc,y,(z,y,1-c),s_sb,r_sib)
    def y_arrivals(p, near):
        for dy in range(1,C):
            for sign in (-1,1):
                yb=y+sign*dy
                oky=(yb>=0)&(yb<C)
                ybc=jnp.clip(yb,0,C-1)
                for d in ([0] if near else range(1,R)):
                    for zs in ((0,) if d==0 else (-1,1)):
                        zb=z+zs*d
                        ok=oky&(zb>=0)&(zb<R)
                        zbc=jnp.clip(zb,0,R-1)
                        wait_main(ok,p,zbc,ybc)
                        if C>2:
                            if sign<0: send(ok&(y<C-1),p,zbc,ybc,(z,y+1,c),s_yu,r_main)
                            else: send(ok&(y>0),p,zbc,ybc,(z,y-1,c),s_yd,r_main)
                        if offload and d==0:
                            send(ok&(c==1),p,zbc,ybc,(z+1-2*(z%2),y,c),s_ex,r_main)
                        send(ok,p,zbc,ybc,(z,y,1-c),s_sb,r_sib)
    def finish(p):
        def body(k,_):
            blk=k*2+1-c
            pltpu.make_async_remote_copy(bufs[p].at[blk],bufs[p].at[blk],s_sb.at[p,k],r_sib.at[p,k],device_id=dev(z,y,1-c),device_id_type=MESH).wait_recv()
            return 0
        lax.fori_loop(0,n//2,body,0)
        pltpu.make_async_copy(bufs[p],outs[p],out_sem.at[p]).start()
    LA=2
    for p in range(min(LA,P)): own(p)
    for p in range(P+2):
        if p+LA<P: own(p+LA)
        if p<P: z_arrivals(p)
        if 0<=p-1<P: y_arrivals(p-1,True)
        if 0<=p-2<P:
            y_arrivals(p-2,False)
            finish(p-2)
    for cond,mk in pending:
        @pl.when(cond)
        def _(): mk().wait_send()
    for p in range(P):
        pltpu.make_async_copy(bufs[p],outs[p],out_sem.at[p]).wait()

def gather(n, shards, cid=0):
    P=len(shards)
    R,C=layout(n)
    h=n//2
    D=pltpu.SemaphoreType.DMA
    return pl.pallas_call(functools.partial(gather_kernel,n,P),
        out_shape=[jax.ShapeDtypeStruct((n,)+s.shape,s.dtype) for s in shards],
        in_specs=[pl.BlockSpec(memory_space=pltpu.HBM)]*P,
        out_specs=[pl.BlockSpec(memory_space=pltpu.HBM)]*P,
        scratch_shapes=[pltpu.VMEM((n,)+s.shape,s.dtype) for s in shards]+[D((P,)),D((P,))]+[D((P,h))]*8,
        compiler_params=pltpu.CompilerParams(collective_id=cid,has_side_effects=True,vmem_limit_bytes=60<<20),
    )(*shards)

HEADS=8; HD=128; MQB=64; MEMK=128; EPS=1e-06; MASKED=-1e30
XC=256

def nn(a,b): return jnp.dot(a,b,preferred_element_type=jnp.float32)
def nt(a,b): return lax.dot_general(a,b,(((1,),(1,)),((),())),preferred_element_type=jnp.float32)
def tn(a,b): return lax.dot_general(a,b,(((0,),(0,)),((),())),preferred_element_type=jnp.float32)

def front_kernel(n, fused, micro, T, D, FF, CACHE, NBLK, *refs):
    it=iter(refs)
    take=lambda k:[next(it) for _ in range(k)]
    x_hbm,og_hbm,docs,mk_hbm,mv_hbm,midx,mreset,again,fgain=take(9)
    ins=take(8)
    (so_hbm,ig_hbm,gsum,e_h,normed_h,mixed_h,n2_h,hidden_h,gi_h,ui_h,ai_h,dq_h,dk_h,dv_h)=take(14)
    bufs=take(8)
    (cur,eg,normed,q,k,v,mixed,n2,g,u,hidden,middle,p,rk,rv,grads,mg,acc,so,ig,mask,gain)=take(22)
    (own_sem,in_sem,c_sem,out_sem,xs,xr,es,er)=take(8)
    ag_sems=take(8)
    B16=jnp.bfloat16
    W=[b.reshape(b.shape[0]*b.shape[1],b.shape[2]) if fused else b for b in bufs[1:]]
    Wq,Wk,Wv,Wo,Wg,Wu,Wd=W
    sec=lax.axis_index("section"); f=lax.axis_index("fsdp")
    scale=HD**-0.5
    R,C=layout(n)
    c=f%2; zy=f//2; y=zy%C; z=zy//C
    def dev(d): return (sec,(d[0]*C+d[1])*2+d[2])
    pieces=[(i,None) for i in range(7)]+[(7,j) for j in range(D//XC)]
    NP=len(pieces)
    nb=[(c>=0,(1-sec,f))]
    if fused:
        nb+=[(z>0,dev((z-1,y,c))),(z<R-1,dev((z+1,y,c))),(y>0,dev((z,y-1,c))),(y<C-1,dev((z,y+1,c))),(c>=0,dev((z,y,1-c)))]
    bar=pltpu.get_barrier_semaphore()
    for cond,d in nb:
        @pl.when(cond)
        def _(d=d): pl.semaphore_signal(bar,1,device_id=d,device_id_type=MESH)
    def own_copy(i):
        return pltpu.make_async_copy(ins[i],bufs[i].at[f] if fused else bufs[i],own_sem.at[i])
    for i in range(8):
        if i or not fused: own_copy(i).start()
    if fused:
        both=jnp.concatenate([again[...].astype(jnp.float32),fgain[...].astype(jnp.float32)],axis=1)
        bufs[0][f]=jnp.broadcast_to(both,bufs[0].shape[1:]).astype(B16)
    def load_cur(): return pltpu.make_async_copy(x_hbm,cur,in_sem.at[0])
    def load_eg(): return pltpu.make_async_copy(og_hbm,eg,in_sem.at[0])
    HC=CACHE//2
    def load_cache(m,kv):
        src=(mk_hbm,mv_hbm)[kv]
        return [pltpu.make_async_copy(src.at[m,pl.ds(i*HC,HC)],grads.at[2*kv+i],c_sem.at[2*kv+i]) for i in range(2)]
    @pl.when(sec==0)
    def _(): load_cur().start()
    @pl.when(sec==1)
    def _():
        for kv in range(2):
            for cp in load_cache(0,kv): cp.start()
        load_eg().start()
    def save(j,src,dst,m):
        return pltpu.make_async_copy(src.at[m],dst.at[m],out_sem.at[j,m])
    def xcopy(m,j):
        cs=pl.ds(j*XC,XC)
        return pltpu.make_async_remote_copy(so.at[m,:,cs],cur.at[m,:,cs],xs.at[m,j],xr.at[m,j],device_id=(1-sec,f),device_id_type=MESH)
    def ecopy(m):
        return pltpu.make_async_remote_copy(ig.at[m],eg.at[m],es.at[m],er.at[m],device_id=(1-sec,f),device_id_type=MESH)
    RB=64
    def rows_loop(fn):
        def b(i,_):
            fn(pl.ds(pl.multiple_of(i*RB,RB),RB)); return 0
        lax.fori_loop(0,T//RB,b,0)
    def cols_loop(N,CH,fn):
        def b(i,_):
            fn(pl.ds(pl.multiple_of(i*CH,CH),CH)); return 0
        lax.fori_loop(0,N//CH,b,0,unroll=N//CH)
    def normalize(x,row):
        inv=lax.rsqrt(jnp.mean(x*x,axis=-1,keepdims=True)+EPS)
        return x*inv*gain[row:row+1,:]
    def norm_back(x,cc,row):
        inv=lax.rsqrt(jnp.mean(x*x,axis=-1,keepdims=True)+EPS)
        s=cc*gain[row:row+1,:]
        gsum[row:row+1,:]+=jnp.sum(cc*x*inv,axis=0,keepdims=True)
        return inv*s-x*(inv*inv*inv)*jnp.mean(s*x,axis=-1,keepdims=True)
    def f_norm(m):
        def f1(r): normed[m,r,:]=normalize(cur[m,r,:].astype(jnp.float32),0).astype(B16)
        rows_loop(f1)
        save(0,normed,normed_h,m).start()
    def f_proj(m,dst,w):
        def f2(cs): dst[m,:,cs]=nn(normed[m],w[:,cs]).astype(B16)
        cols_loop(D,256,f2)
    G=4
    def by_block(a,other,hs,m,fn):
        return jnp.concatenate([fn(a[b*MQB:(b+1)*MQB],other[m,b*MEMK:(b+1)*MEMK,hs]) for b in range(NBLK)],axis=0)
    def halves(a): return [a[:,i:i+HD] for i in range(0,T,HD)]
    def row_sum(*parts): return jnp.sum(functools.reduce(jnp.add,parts),axis=-1,keepdims=True)
    def row_max(*parts): return jnp.max(functools.reduce(jnp.maximum,parts),axis=-1,keepdims=True)
    def f_attend(m,recall):
        for h0 in range(0,HEADS,G):
            HS=[slice(h*HD,h*HD+HD) for h in range(h0,h0+G)]
            qs=[q[m,:,hs] for hs in HS]
            s=[nt(a,k[m,:,hs]) for a,hs in zip(qs,HS)]
            if recall: x=[by_block(a,rk,hs,m,nt) for a,hs in zip(qs,HS)]
            ok=mask[m].astype(jnp.float32)>0.5
            s=[jnp.where(ok,a*scale,MASKED) for a in s]
            if recall:
                live=jnp.concatenate([jnp.broadcast_to(mreset[pl.ds(m,1),b:b+1],(MQB,MEMK)) for b in range(NBLK)],axis=0)==0
                x=[jnp.where(live,a*scale,MASKED) for a in x]
                top=[row_max(b,*halves(a)) for a,b in zip(s,x)]
                xe=[jnp.exp(b-t) for b,t in zip(x,top)]
            else: top=[row_max(*halves(a)) for a in s]
            se=[jnp.exp(a-t) for a,t in zip(s,top)]
            if recall: inv=[1.0/row_sum(b,*halves(a)) for a,b in zip(se,xe)]
            else: inv=[1.0/row_sum(*halves(a)) for a in se]
            ps=[(a*i).astype(B16) for a,i in zip(se,inv)]
            o=[nn(a,v[m,:,hs]) for a,hs in zip(ps,HS)]
            if recall:
                pr=[(a*i).astype(B16) for a,i in zip(xe,inv)]
                o=[a+by_block(b,rv,hs,m,nn) for a,b,hs in zip(o,pr,HS)]
            for j in range(G):
                p[m,h0+j,:,0:T]=ps[j]
                if recall: p[m,h0+j,:,T:T+MEMK]=pr[j]
                mixed[m,:,HS[j]]=o[j].astype(B16)
        save(1,mixed,mixed_h,m).start()
    def f_out(m):
        def f3(cs): middle[m,:,cs]=cur[m,:,cs].astype(jnp.float32)+nn(mixed[m],Wo[:,cs])
        cols_loop(D,256,f3)
        def f4(r): n2[m,r,:]=normalize(middle[m,r,:],1).astype(B16)
        rows_loop(f4)
        save(2,n2,n2_h,m).start()
    def f_gate(m):
        def f5(cs):
            a=n2[m]
            gg=nn(a,Wg[:,cs]); uu=nn(a,Wu[:,cs])
            sg=jax.nn.sigmoid(gg)
            act=gg*sg
            g[m,:,cs]=(uu*(sg*(1.0+gg*(1.0-sg)))).astype(B16); u[m,:,cs]=act.astype(B16)
            hidden[m,:,cs]=(act*uu).astype(B16)
        cols_loop(FF,256,f5)
        save(3,hidden,hidden_h,m).start()
    def f_down(m,j):
        cs=pl.ds(j*XC,XC)
        so[m,:,cs]=(middle[m,:,cs]+nn(hidden[m],Wd[:,cs])).astype(B16)
    def recall(m,kv):
        for cp in load_cache(m,kv): cp.wait()
        dst=(rk,rv)[kv]
        def body(b,_):
            idx=midx[m,pl.ds(b,1),:]
            col=jnp.broadcast_to(idx.astype(jnp.float32),(MEMK,MEMK)).T[:,0:1].astype(jnp.int32)
            io=lax.broadcasted_iota(jnp.int32,(MEMK,HC),1)
            rows=nn(jnp.where(io==col,1.0,0.0).astype(B16),grads[2*kv])
            rows=rows+nn(jnp.where(io+HC==col,1.0,0.0).astype(B16),grads[2*kv+1])
            dst[m,pl.ds(pl.multiple_of(b*MEMK,MEMK),MEMK),:]=rows.astype(B16)
            return 0
        lax.fori_loop(0,NBLK,body,0)
        if m+1<micro:
            for cp in load_cache(m+1,kv): cp.start()
    def setup():
        if not fused:
            gain[...]=bufs[0][0,0:8,:].astype(jnp.float32)
            return
        lane=lax.broadcasted_iota(jnp.int32,(8,128),1)
        for e in range(n//2):
            lo=bufs[0][2*e].astype(jnp.float32)[0:8]
            hi=bufs[0][2*e+1].astype(jnp.float32)[0:8]
            cs=pl.ds(e*128,128)
            gain[0:1,cs]=jnp.where(lane<64,lo,pltpu.roll(hi,64,1))[0:1]
            gain[1:2,cs]=jnp.where(lane<64,pltpu.roll(lo,64,1),hi)[0:1]
    def each(fn):
        def b(m,_):
            fn(m); return 0
        return lambda: lax.fori_loop(0,micro,b,0)
    def down(j):
        def go():
            def b(m,_):
                f_down(m,j); xcopy(m,j).start(); return 0
            lax.fori_loop(0,micro,b,0)
        return go
    first={0:[each(f_norm)],1:[each(lambda m:f_proj(m,q,Wq))],2:[each(lambda m:f_proj(m,k,Wk))],
        3:[each(lambda m:f_proj(m,v,Wv)),lambda:f_attend(0,False)],
        4:[lambda:[f_attend(m,False) for m in range(1,micro)],each(f_out)],
        6:[each(f_gate)]}
    for j in range(D//XC): first[7+j]=[down(j)]
    units=[(m,kv) for m in range(micro) for kv in range(2)]
    second={i:[functools.partial(recall,*un)] for i,un in enumerate(units)}
    def arrived(i):
        if i==0: setup()
        @pl.when(sec==0)
        def _():
            for fn in first.get(i,[]): fn()
        @pl.when(sec==1)
        def _():
            for fn in second.get(i,[]): fn()
    gsum[...]=jnp.zeros_like(gsum)
    ri=lax.broadcasted_iota(jnp.int32,(T,T),0); ci=lax.broadcasted_iota(jnp.int32,(T,T),1)
    def prepare():
        for m in range(micro):
            row=jnp.broadcast_to(docs[m:m+1,:].astype(jnp.float32),(T,T))
            mask[m]=jnp.where((row==row.T)&(ci<=ri),1.0,0.0).astype(B16)
        @pl.when(sec==0)
        def _(): load_cur().wait()
        @pl.when(sec==1)
        def _(): load_eg().wait()
    pl.semaphore_wait(bar,sum(jnp.where(cond,1,0) for cond,d in nb))
    pending=[]
    if fused:
        s_zu,s_zd,s_yu,s_yd,s_sb,s_ex,r_main,r_sib=ag_sems
        def part(i,blk):
            b,j=pieces[i]
            return bufs[b].at[blk] if j is None else bufs[b].at[blk,:,pl.ds(j*XC,XC)]
        def send(cond,i,zb,yb,target,ssem,rsem):
            blk=(zb*C+yb)*2+c; kk=zb*C+yb
            def mk():
                return pltpu.make_async_remote_copy(part(i,blk),part(i,blk),ssem.at[i,kk],rsem.at[i,kk],device_id=dev(target),device_id_type=MESH)
            @pl.when(cond)
            def _(): mk().start()
            pending.append((cond,mk))
        def wait_main(cond,i,zb,yb):
            blk=(zb*C+yb)*2+c; kk=zb*C+yb
            @pl.when(cond)
            def _():
                pltpu.make_async_remote_copy(part(i,blk),part(i,blk),s_sb.at[i,kk],r_main.at[i,kk],device_id=dev((z,y,1-c)),device_id_type=MESH).wait_recv()
        offload=(C==2 and R%2==0)
        zx=z+1-2*(z%2)
        true=c>=0
        def own(i):
            b,j=pieces[i]
            if not j and b: own_copy(b).wait()
            send(y>0,i,z,y,(z,y-1,c),s_yd,r_main)
            send(y<C-1,i,z,y,(z,y+1,c),s_yu,r_main)
            send(z>0,i,z,y,(z-1,y,c),s_zd,r_main)
            send(z<R-1,i,z,y,(z+1,y,c),s_zu,r_main)
            send(true,i,z,y,(z,y,1-c),s_sb,r_sib)
        def z_arrivals(i,d):
            if True:
                for sign in (-1,1):
                    zb=z+sign*d
                    ok=(zb>=0)&(zb<R)
                    zbc=jnp.clip(zb,0,R-1)
                    wait_main(ok,i,zbc,y)
                    if sign<0: send(ok&(z<R-1),i,zbc,y,(z+1,y,c),s_zu,r_main)
                    else: send(ok&(z>0),i,zbc,y,(z-1,y,c),s_zd,r_main)
                    ydo=ok&jnp.logical_not((c==1)&(zbc==zx)) if offload else ok
                    send(ydo&(y>0),i,zbc,y,(z,y-1,c),s_yd,r_main)
                    send(ydo&(y<C-1),i,zbc,y,(z,y+1,c),s_yu,r_main)
                    send(ok,i,zbc,y,(z,y,1-c),s_sb,r_sib)
        def y_arrivals(i,near):
            for dy in range(1,C):
                for sign in (-1,1):
                    yb=y+sign*dy
                    oky=(yb>=0)&(yb<C)
                    ybc=jnp.clip(yb,0,C-1)
                    for d in ([0] if near else range(1,R)):
                        for zs in ((0,) if d==0 else (-1,1)):
                            zb=z+zs*d
                            ok=oky&(zb>=0)&(zb<R)
                            zbc=jnp.clip(zb,0,R-1)
                            wait_main(ok,i,zbc,ybc)
                            if C>2:
                                if sign<0: send(ok&(y<C-1),i,zbc,ybc,(z,y+1,c),s_yu,r_main)
                                else: send(ok&(y>0),i,zbc,ybc,(z,y-1,c),s_yd,r_main)
                            if offload and d==0:
                                send(ok&(c==1),i,zbc,ybc,(zx,y,c),s_ex,r_main)
                            send(ok,i,zbc,ybc,(z,y,1-c),s_sb,r_sib)
        def finish(i):
            def body(kk,_):
                blk=kk*2+1-c
                pltpu.make_async_remote_copy(part(i,blk),part(i,blk),s_sb.at[i,kk],r_sib.at[i,kk],device_id=dev((z,y,1-c)),device_id_type=MESH).wait_recv()
                return 0
            lax.fori_loop(0,n//2,body,0)
        LA=2
        LAST=R
        for i in range(LA): own(i)
        prepare()
        for i in range(NP+LAST):
            if i+LA<NP: own(i+LA)
            for d in range(1,R):
                if 0<=i-d+1<NP: z_arrivals(i-d+1,d)
            if 0<=i-1<NP: y_arrivals(i-1,True)
            if 0<=i-LAST+1<NP:
                y_arrivals(i-LAST+1,False)
                finish(i-LAST+1)
                arrived(i-LAST+1)
    else:
        prepare()
        for i in range(NP):
            b,j=pieces[i]
            if not j: own_copy(b).wait()
            arrived(i)
    for cond,mk in pending:
        @pl.when(cond)
        def _(mk=mk): mk().wait_send()
    @pl.when(sec==1)
    def _():
        def forward(m,_):
            for j in range(D//XC): xcopy(m,j).wait_recv()
            f_norm(m)
            f_proj(m,q,Wq); f_proj(m,k,Wk); f_proj(m,v,Wv)
            f_attend(m,True)
            f_out(m)
            f_gate(m)
            for j in range(D//XC): f_down(m,j)
            return 0
        lax.fori_loop(0,micro,forward,0)
    def gsave(j,i,dst,m): return pltpu.make_async_copy(grads.at[i,pl.ds(pl.multiple_of(m*T,T),T)],dst.at[m],out_sem.at[j,m])
    def b_attend(m,ms,recall):
        for h0 in range(0,HEADS,G):
            HS=[slice(h*HD,h*HD+HD) for h in range(h0,h0+G)]
            mh=[normed[m,:,hs] for hs in HS]
            ps=[p[m,h,:,0:T] for h in range(h0,h0+G)]
            pg=[nt(a,v[m,:,hs]) for a,hs in zip(mh,HS)]
            if recall:
                pr=[p[m,h,:,T:T+MEMK].astype(jnp.float32) for h in range(h0,h0+G)]
                rg=[by_block(a,rv,hs,m,nt) for a,hs in zip(mh,HS)]
            dv=[tn(a,b) for a,b in zip(ps,mh)]
            pf=[a.astype(jnp.float32) for a in ps]
            if recall:
                w=[row_sum(c_*d_,*halves(a*b)) for a,b,c_,d_ in zip(pf,pg,pr,rg)]
                dr=[(a*(b-t)).astype(B16) for a,b,t in zip(pr,rg,w)]
            else: w=[row_sum(*halves(a*b)) for a,b in zip(pf,pg)]
            ds=[(a*(b-t)).astype(B16) for a,b,t in zip(pf,pg,w)]
            dq=[nn(a,k[m,:,hs]) for a,hs in zip(ds,HS)]
            if recall: dq=[a+by_block(b,rk,hs,m,nn) for a,b,hs in zip(dq,dr,HS)]
            dk=[tn(a,q[m,:,hs]) for a,hs in zip(ds,HS)]
            for j in range(G):
                grads[3,ms,HS[j]]=dv[j].astype(B16)
                grads[1,ms,HS[j]]=(dq[j]*scale).astype(B16)
                grads[2,ms,HS[j]]=(dk[j]*scale).astype(B16)
    def backward(m,_):
        @pl.when(sec==0)
        def _(): ecopy(m).wait_recv()
        save(4,so,so_hbm,m).start()
        save(5,eg,e_h,m).start()
        def b1(cs):
            hg=nt(eg[m],Wd[cs,:])
            u[m,:,cs]=(hg*u[m,:,cs].astype(jnp.float32)).astype(B16)
            g[m,:,cs]=(hg*g[m,:,cs].astype(jnp.float32)).astype(B16)
        cols_loop(FF,256,b1)
        save(6,g,gi_h,m).start(); save(7,u,ui_h,m).start()
        def b2(cs): acc[:,cs]=nt(g[m],Wg[cs,:])+nt(u[m],Wu[cs,:])
        cols_loop(D,256,b2)
        ms=pl.ds(pl.multiple_of(m*T,T),T)
        def b3(r):
            t_=eg[m,r,:].astype(jnp.float32)+norm_back(middle[m,r,:],acc[r,:],1)
            mg[r,:]=t_; grads[0,pl.ds(pl.multiple_of(m*T,T)+r.start,RB),:]=t_.astype(B16)
        rows_loop(b3)
        gsave(8,0,ai_h,m).start()
        save(0,normed,normed_h,m).wait()
        def b4(cs): normed[m,:,cs]=nt(grads[0,ms,:],Wo[cs,:]).astype(B16)
        cols_loop(D,256,b4)
        pl.when(sec==0)(lambda: b_attend(m,ms,False))
        pl.when(sec==1)(lambda: b_attend(m,ms,True))
        gsave(9,1,dq_h,m).start(); gsave(10,2,dk_h,m).start(); gsave(11,3,dv_h,m).start()
        def b5(cs): acc[:,cs]=nt(grads[1,ms,:],Wq[cs,:])+nt(grads[2,ms,:],Wk[cs,:])+nt(grads[3,ms,:],Wv[cs,:])
        cols_loop(D,256,b5)
        def b6(r): ig[m,r,:]=(mg[r,:]+norm_back(cur[m,r,:].astype(jnp.float32),acc[r,:],0)).astype(B16)
        rows_loop(b6)
        @pl.when(sec==1)
        def _(): ecopy(m).start()
        save(12,ig,ig_hbm,m).start()
        return 0
    lax.fori_loop(0,micro,backward,0)
    for m in range(micro):
        @pl.when(sec==0)
        def _():
            for j in range(D//XC): xcopy(m,j).wait_send()
        @pl.when(sec==1)
        def _(): ecopy(m).wait_send()
        for j,(s,d) in enumerate([(mixed,mixed_h),(n2,n2_h),(hidden,hidden_h),(so,so_hbm),(eg,e_h),(g,gi_h),(u,ui_h)],1):
            save(j,s,d,m).wait()
        for j,i,d in ((8,0,ai_h),(9,1,dq_h),(10,2,dk_h),(11,3,dv_h)):
            gsave(j,i,d,m).wait()
        save(12,ig,ig_hbm,m).wait()

def front(n, fused, x, og, docs, mk, mv, midx, mreset, again, fgain, vec, weights, cid=2):
    micro,T,D=x.shape
    FF=weights[4].shape[1]
    CACHE=mk.shape[1]; NBLK=midx.shape[1]
    B=jnp.bfloat16; F=jnp.float32
    V=pltpu.VMEM
    act=(micro,T,D); fact=(micro,T,FF)
    S=jax.ShapeDtypeStruct
    outs=[S(act,B),S(act,B),S((8,D),F),S(act,B),S(act,B),S(act,B),S(act,B),S(fact,B),S(fact,B),S(fact,B),S(act,B),S(act,B),S(act,B),S(act,B)]
    ws=[vec]+list(weights)
    scratch=[V((n,16,128),B) if fused else V(vec.shape,B)]
    scratch+=[V((n,)+w.shape if fused else w.shape,B) for w in weights]
    scratch+=[V(act,B)]*8+[V(fact,B)]*3+[V(act,F),V((micro,HEADS,T,T+MEMK),B),V((micro,NBLK*MEMK,D),B),V((micro,NBLK*MEMK,D),B),V((4,micro*T,D),B),V((T,D),F),V((T,D),F),V(act,B),V(act,B),V((micro,T,T),B),V((8,D),F)]
    DM=pltpu.SemaphoreType.DMA
    NP=7+D//XC
    scratch+=[DM((8,)),DM((2,)),DM((4,)),DM((13,micro)),DM((micro,D//XC)),DM((micro,D//XC)),DM((micro,)),DM((micro,))]
    scratch+=[DM((NP,n//2) if fused else (1,))]*8
    HB=pl.BlockSpec(memory_space=pltpu.HBM); VB=pl.BlockSpec(memory_space=pltpu.VMEM)
    return pl.pallas_call(functools.partial(front_kernel,n,fused,micro,T,D,FF,CACHE,NBLK),
        out_shape=outs,
        in_specs=[HB,HB,VB,HB,HB,VB,VB,VB,VB]+[HB]*8,
        out_specs=[HB,HB,VB]+[HB]*11,
        scratch_shapes=scratch,
        compiler_params=pltpu.CompilerParams(collective_id=cid,has_side_effects=True,vmem_limit_bytes=64<<20),
    )(x,og,docs,mk,mv,midx,mreset,again,fgain,*ws)


COLS=1024
NOFF=99
def plan(n, lhs_shapes, rhs_shapes, weights, steps):
    pieces=[]
    for w,(l,r) in enumerate(weights):
        rows=lhs_shapes[l][1]//n; N=rhs_shapes[r][1]
        c0=0
        for step in steps[w]:
            pieces.append((w,rows,c0,step)); c0+=step
        while c0<N:
            step=min(steps[w][-1],N-c0)
            pieces.append((w,rows,c0,step)); c0+=step
    return pieces

def reduce_kernel(n, tok, lhs_shapes, rhs_shapes, weights, pieces, vec_rows, SLOTS, *refs):
    NP=len(pieces); NL=len(lhs_shapes); NR=len(rhs_shapes); NW=len(weights)
    R,C=layout(n); H=n//2
    it=iter(refs)
    take=lambda k:[next(it) for _ in range(k)]
    lhs=take(NL); rhs=take(NR); vec=next(it)
    outs=take(NW); vec_out=next(it)
    ring=next(it); tbuf=take(NL)
    keep=take(NP); sibr=take(NP); yr=take(NP); xr=take(NP); zu=take(NP); zd=take(NP); fin=take(NP)
    shapes=sorted({p[1] for p in pieces})
    stage_of=dict(zip(shapes,take(len(shapes))))
    vecb=next(it); vecr=next(it)
    (ld_sem,sib_s,sib_r,y_s,y_r,x_s,x_r,zu_s,zu_r,zd_s,zd_r,v_s,v_r,o_s)=take(14)
    sec=lax.axis_index("section"); f=lax.axis_index("fsdp")
    c=f%2; zy=f//2; y=zy%C; z=zy//C
    OFF=lambda i: C==2 and R%2==0 and i<NOFF
    zx=z+1-2*(z%2)
    def dev(zz,yy,cc): return (sec,(zz*C+yy)*2+cc)
    def rcopy(src,dst,ss,rs,d):
        return pltpu.make_async_remote_copy(src,dst,ss,rs,device_id=dev(*d),device_id_type=MESH)
    LOGN=n.bit_length()-1
    nb=[]
    nb.append((c>=0,dev(z,y,1-c)))
    for k in range(1,C): nb.append((c>=0,dev(z,lax.rem(y+k,C),c)))
    nb.append((z>0,dev(z-1,y,c))); nb.append((z<R-1,dev(z+1,y,c)))
    for k in range(1,R.bit_length()-1): nb.append((c>=0,(sec,f^(2*C<<k))))
    bar=pltpu.get_barrier_semaphore()
    loads=[]
    def parts(ref,shape):
        return [(ref,c0,min(COLS,shape[1]-c0)) for c0 in range(0,shape[1],COLS)]
    load_id={}
    def need(kind,i):
        key=(kind,i)
        if key in load_id: return
        ref=lhs[i] if kind=="l" else rhs[i]
        sh=lhs_shapes[i] if kind=="l" else rhs_shapes[i]
        ids=[]
        for pr in parts(ref,sh):
            ids.append(len(loads)); loads.append(pr)
        load_id[key]=ids
    for l,r in weights:
        need("l",l); need("r",r)
    issued=[0]; freed=set()
    def load_copy(k):
        ref,c0,w=loads[k]
        return pltpu.make_async_copy(ref.at[:,pl.ds(c0,w)],ring.at[k%SLOTS,:,pl.ds(0,w)],ld_sem.at[k%SLOTS])
    def pump():
        while issued[0]<len(loads) and (issued[0]<SLOTS or (issued[0]-SLOTS) in freed):
            load_copy(issued[0]).start(); issued[0]+=1
    pump()
    for cond,d in nb:
        @pl.when(cond)
        def _(): pl.semaphore_signal(bar,1,device_id=d,device_id_type=MESH)
    waited=set()
    def wait_load(k):
        if k not in waited:
            load_copy(k).wait(); waited.add(k)
    transposed=set()
    def ensure_lhs(l):
        if l in transposed: return
        transposed.add(l)
        for j,k in enumerate(load_id[("l",l)]):
            wait_load(k)
            w=loads[k][2]
            CH=256
            def body(i,_,k=k,j=j):
                o=pl.multiple_of(i*CH,CH)
                tbuf[l][pl.ds(pl.multiple_of(j*COLS+o,CH),CH),:]=ring[k%SLOTS,:,pl.ds(o,CH)].T
                return 0
            lax.fori_loop(0,w//CH,body,0)
            freed.add(k)
        pump()
    last_use={}
    for i,(w,rows,c0,nc) in enumerate(pieces):
        l,r=weights[w]
        last_use[load_id[("r",r)][c0//COLS]]=i
    sends={}
    cur_piece=[0]
    stage_use={}
    def compute(i):
        w,rows,c0,nc=pieces[i]
        l,r=weights[w]
        ensure_lhs(l)
        k=load_id[("r",r)][c0//COLS]
        wait_load(k)
        lc=c0%COLS
        u=stage_use.get(rows,0); stage_use[rows]=u+1
        st=stage_of[rows].at[u%2,:,:,pl.ds(0,nc)]
        if u>=2: sib_waits[rows].pop(0)()
        T4=tbuf[l].reshape(H,2,rows,tok)
        CH=256
        for which,dst in ((1-c,st),(c,keep[i])):
            def body(j,_,which=which,dst=dst):
                o=pl.multiple_of(j*CH,CH)
                a=T4[:,which].reshape(H*rows,tok)
                b=ring[k%SLOTS,:,pl.ds(pl.multiple_of(lc+o,CH),CH)]
                res=jnp.dot(a,b,preferred_element_type=jnp.float32).astype(jnp.bfloat16)
                dst[:,:,pl.ds(o,CH)]=res.reshape(H,rows,CH)
                return 0
            lax.fori_loop(0,nc//CH,body,0)
            if dst is not keep[i]:
                cp=rcopy(st,sibr[i],sib_s.at[i],sib_r.at[i],(z,y,1-c))
                cp.start()
                sib_waits.setdefault(rows,[]).append(cp.wait_send)
        if last_use[k]==i:
            freed.add(k); pump()
    sib_waits={}
    def add_into(dst,src,rows):
        def body(j,_):
            o=pl.multiple_of(j*16,16)
            dst[pl.ds(o,16),:]=dst[pl.ds(o,16),:]+src[pl.ds(o,16),:]
            return 0
        lax.fori_loop(0,rows//16,body,0)
    def send(tag,cond,cp):
        if cond is None: cp().start()
        else:
            @pl.when(cond)
            def _(): cp().start()
        sends.setdefault(tag,[]).append((cond,cp))
    def sib_add(i):
        w,rows,c0,nc=pieces[i]
        rcopy(sibr[i],sibr[i],sib_s.at[i],sib_r.at[i],(z,y,1-c)).wait_recv()
        def body(k,_):
            add_into(keep[i].at[k],sibr[i].at[k],rows)
            return 0
        lax.fori_loop(0,H,body,0)
        offload=OFF(i)
        if offload:
            send((i,'y'),c==1,lambda: rcopy(keep[i].at[zx*C+1-y],xr[i],x_s.at[i],x_r.at[i],(zx,y,c)))
        for kz in range(R-1,-1,-1):
            zt=lax.rem(z+kz,R)
            for ky in range(1,C):
                yt=lax.rem(y+ky,C)
                slot=C-1-ky
                cp=lambda zt=zt,yt=yt,slot=slot: rcopy(keep[i].at[zt*C+yt],yr[i].at[slot,zt],y_s.at[i,slot,zt],y_r.at[i,slot,zt],(z,yt,c))
                if offload and kz==0:
                    continue
                send((i,'y'),(jnp.logical_not((c==1)&(zt==zx))) if offload else None,cp)
    def x_add(i):
        w,rows,c0,nc=pieces[i]
        if not OFF(i): return
        @pl.when(c==1)
        def _():
            rcopy(xr[i],xr[i],x_s.at[i],x_r.at[i],(zx,y,c)).wait_recv()
            add_into(keep[i].at[z*C+1-y],xr[i],rows)
        send((i,'y'),None,lambda: rcopy(keep[i].at[z*C+1-y],yr[i].at[0,z],y_s.at[i,0,z],y_r.at[i,0,z],(z,1-y,c)))
    def y_add(i):
        w,rows,c0,nc=pieces[i]
        offload=OFF(i)
        for kz in range(R-1,-1,-1):
            zt=lax.rem(z+kz,R)
            for slot in range(C-1):
                def go(zt=zt,slot=slot):
                    rcopy(yr[i].at[slot,zt],yr[i].at[slot,zt],y_s.at[i,slot,zt],y_r.at[i,slot,zt],(z,y,1-c)).wait_recv()
                    add_into(keep[i].at[zt*C+y],yr[i].at[slot,zt],rows)
                if offload and kz!=0:
                    pl.when(jnp.logical_not((c==1)&(zt==zx)))(go)
                else: go()
    def z_step(i,s):
        w,rows,c0,nc=pieces[i]
        def line(zs,up):
            rb,rr,ss=(zu,zu_r,zu_s) if up else (zd,zd_r,zd_s)
            first=(zs==0) if up else (zs==R-1)
            targets=range(R-1,zs,-1) if up else range(0,zs)
            nxt=zs+1 if up else zs-1
            cps=[]
            for t in targets:
                k=abs(t-zs)
                cps.append((k,lambda t=t,k=k: rcopy(keep[i].at[t*C+y],rb[i].at[k-1],ss.at[i,k-1],rr.at[i,k-1],(nxt,y,c)),t))
            def go():
                for k,cp,t in cps:
                    if not first:
                        rcopy(rb[i].at[k],rb[i].at[k],ss.at[i,k],rr.at[i,k],(zs,y,1-c)).wait_recv()
                        add_into(keep[i].at[t*C+y],rb[i].at[k],rows)
                    cp().start()
            pl.when(z==zs)(go)
            for k,cp,t in cps: sends.setdefault((i,zs if up else R-1-zs),[]).append((z==zs,cp))
        line(s,True)
        line(R-1-s,False)
    def final(i):
        w,rows,c0,nc=pieces[i]
        blk=z*C+y
        @pl.when(z>0)
        def _():
            rcopy(zu[i].at[0],zu[i].at[0],zu_s.at[i,0],zu_r.at[i,0],(z,y,1-c)).wait_recv()
        @pl.when(z<R-1)
        def _():
            rcopy(zd[i].at[0],zd[i].at[0],zd_s.at[i,0],zd_r.at[i,0],(z,y,1-c)).wait_recv()
        def body(j,_):
            o=pl.ds(pl.multiple_of(j*16,16),16)
            a=keep[i][blk,o,:].astype(jnp.float32)
            a=a+jnp.where(z>0,zu[i][0,o,:].astype(jnp.float32),0.0)+jnp.where(z<R-1,zd[i][0,o,:].astype(jnp.float32),0.0)
            fin[i][o,:]=a.astype(jnp.bfloat16)
            return 0
        lax.fori_loop(0,rows//16,body,0)
        pltpu.make_async_copy(fin[i],outs[w].at[:,pl.ds(c0,nc)],o_s.at[i]).start()
    def vec_step(k):
        if k>0:
            vcopy(k-1).wait()
            vecb[k]=vecb[k-1]+vecr[k-1]
        if k<LOGN: vcopy(k).start()
        else:
            cp=pltpu.make_async_copy(vecb.at[LOGN],vec_out,o_s.at[NP]); cp.start()
    def vcopy(k):
        return pltpu.make_async_remote_copy(vecb.at[k],vecr.at[k],v_s.at[k],v_r.at[k],device_id=(sec,f^(1<<k)),device_id_type=MESH)
    cp=pltpu.make_async_copy(vec,vecb.at[0],o_s.at[NP]); cp.start(); cp.wait()
    pl.semaphore_wait(bar,sum(jnp.where(cond,1,0) for cond,d in nb))
    def end_sends(tag):
        for cond,cp in sends.pop(tag,[]):
            if cond is None: cp().wait_send()
            else:
                @pl.when(cond)
                def _(cp=cp): cp().wait_send()
    LAGY=3
    for t in range(NP+LAGY+R+1):
        if t<NP: compute(t)
        if 0<=t-1<NP: sib_add(t-1)
        if 0<=t-2<NP: x_add(t-2)
        if t<=LOGN: vec_step(t)
        if 0<=t-LAGY<NP: y_add(t-LAGY)
        for s in range(R):
            i=t-LAGY-s
            if 0<=i<NP: z_step(i,s)
        i=t-LAGY-R
        if 0<=i<NP: final(i)
        end_sends((t-LAGY-1,'y'))
        for s in range(R): end_sends((t-LAGY-s-2,s))
    for q in sib_waits.values():
        for wfn in q: wfn()
    for tag in list(sends): end_sends(tag)
    for i in range(NP):
        w,rows,c0,nc=pieces[i]
        pltpu.make_async_copy(fin[i],outs[w].at[:,pl.ds(c0,nc)],o_s.at[i]).wait()
    pltpu.make_async_copy(vecb.at[LOGN],vec_out,o_s.at[NP]).wait()

def reduce(n, lhs, rhs, weights, vec, steps, cid=1, SLOTS=6):
    tok=lhs[0].shape[0]
    ls=[a.shape for a in lhs]; rs=[a.shape for a in rhs]
    pieces=plan(n,ls,rs,weights,steps)
    R,C=layout(n); H=n//2
    NP=len(pieces)
    LOGN=n.bit_length()-1
    D=pltpu.SemaphoreType.DMA
    B=jnp.bfloat16
    V=pltpu.VMEM
    shapes=sorted({(p[1],max(o[3] for o in pieces if o[1]==p[1])) for p in pieces})
    scratch=[V((SLOTS,tok,COLS),B)]+[V((s[1],tok),B) for s in ls]
    scratch+=[V((H,p[1],p[3]),B) for p in pieces]
    scratch+=[V((H,p[1],p[3]),B) for p in pieces]
    scratch+=[V((C-1,R,p[1],p[3]),B) for p in pieces]
    scratch+=[V((p[1],p[3]) if C==2 else (16,128),B) for p in pieces]
    scratch+=[V((R-1,p[1],p[3]),B) for p in pieces]*2
    scratch+=[V((p[1],p[3]),B) for p in pieces]
    scratch+=[V((2,H)+s,B) for s in shapes]
    scratch+=[V((LOGN+1,)+vec.shape,vec.dtype),V((LOGN,)+vec.shape,vec.dtype)]
    scratch+=[D((SLOTS,)),D((NP,)),D((NP,)),D((NP,C-1,R)),D((NP,C-1,R)),D((NP,)),D((NP,)),D((NP,R-1)),D((NP,R-1)),D((NP,R-1)),D((NP,R-1)),D((LOGN,)),D((LOGN,)),D((NP+1,))]
    HB=pl.BlockSpec(memory_space=pltpu.HBM)
    res=pl.pallas_call(functools.partial(reduce_kernel,n,tok,ls,rs,weights,pieces,vec.shape[0],SLOTS),
        out_shape=[jax.ShapeDtypeStruct((ls[l][1]//n,rs[r][1]),B) for l,r in weights]+[jax.ShapeDtypeStruct(vec.shape,vec.dtype)],
        in_specs=[HB]*(len(lhs)+len(rhs)+1),
        out_specs=[HB]*(len(weights)+1),
        scratch_shapes=scratch,
        compiler_params=pltpu.CompilerParams(collective_id=cid,has_side_effects=True,vmem_limit_bytes=63<<20),
    )(*lhs,*rhs,vec)
    return res[:-1],res[-1]


def settle_kernel(count, gw, *refs):
    ins = refs[:count]
    total = refs[count]
    outs = refs[count + 1 : 2 * count + 1]
    again, fgain = refs[2 * count + 1 : 2 * count + 3]
    held = refs[2 * count + 3 : 3 * count + 3]
    in_sem, out_sem = refs[3 * count + 3 :]
    load = [pltpu.make_async_copy(a, h, in_sem.at[i]) for i, (a, h) in enumerate(zip(ins, held))]
    store = [pltpu.make_async_copy(h, b.at[0], out_sem.at[i]) for i, (h, b) in enumerate(zip(held, outs))]
    for cp in load:
        cp.start()
    width = total.shape[1]
    f = lax.axis_index("fsdp")
    mine = pltpu.roll(total[...], lax.rem(width - f * gw, width), 1)
    again[...] = mine[0:1, 0:gw].astype(again.dtype)
    fgain[...] = mine[1:2, 0:gw].astype(fgain.dtype)
    for cp, out in zip(load, store):
        cp.wait()
        out.start()
    for cp in store:
        cp.wait()


def settle(*arrays):
    *ins, total = arrays
    gw = total.shape[1] // lax.axis_size("fsdp")
    HB = pl.BlockSpec(memory_space=pltpu.HBM)
    VB = pl.BlockSpec(memory_space=pltpu.VMEM)
    S = jax.ShapeDtypeStruct
    return pl.pallas_call(
        functools.partial(settle_kernel, len(ins), gw),
        out_shape=[S((1,) + a.shape, a.dtype) for a in ins] + [S((1, gw), jnp.bfloat16)] * 2,
        in_specs=[HB] * len(ins) + [VB],
        out_specs=[HB] * len(ins) + [VB] * 2,
        scratch_shapes=[pltpu.VMEM(a.shape, a.dtype) for a in ins] + [pltpu.SemaphoreType.DMA((len(ins),))] * 2,
        compiler_params=pltpu.CompilerParams(vmem_limit_bytes=63 << 20),
    )(*ins, total)


def per_device(
    block_input, output_grad, document_ids, memory_keys, memory_values, memory_index, memory_reset,
    query_weight, key_weight, value_weight, output_weight, gate_weight, up_weight, down_weight,
    attend_gain, feed_gain,
):
    n = lax.axis_size("fsdp")
    f = lax.axis_index("fsdp")
    micro, T, D = block_input.shape
    FF = gate_weight.shape[2]
    gw = attend_gain.shape[1]
    shards = [w[0] for w in (query_weight, key_weight, value_weight, output_weight, gate_weight, up_weight, down_weight)]
    rows = [s.shape[0] for s in shards]
    fused = 2 * gw == 128 and all(s % 16 == 0 for s in rows)
    vec = attend_gain
    if not fused:
        vec = jnp.zeros((16, D), jnp.bfloat16)
        vec = lax.dynamic_update_slice(vec, jnp.concatenate([attend_gain, feed_gain]), (0, f * gw))
        padded = [jnp.pad(s, ((0, -s.shape[0] % 16), (0, 0))) for s in shards]
        gathered = gather(n, [vec] + padded, 0)
        vec = jnp.sum(gathered[0], axis=0, keepdims=True)
        shards = [g[:, :r].reshape(n * r, g.shape[2]) for g, r in zip(gathered[1:], rows)]
    (so, ig, gsum, e, normed, mixed, n2, hidden, gi, ui, ai, dq, dk, dv) = front(
        n, fused, block_input, output_grad, document_ids, memory_keys, memory_values, memory_index, memory_reset, attend_gain, feed_gain, vec, shards, 2)
    flat = lambda a: a.reshape(micro * T, a.shape[2])
    hid = flat(hidden)
    rd = rows[6]
    if rd % 16:
        hid = jnp.pad(hid.reshape(micro * T, n, rd), ((0, 0), (0, 0), (0, -rd % 16))).reshape(micro * T, -1)
    lhs = [hid, flat(n2), flat(mixed), flat(normed)]
    rhs = [flat(a) for a in (e, gi, ui, ai, dv, dk, dq)]
    order = [(1, 1), (1, 2), (0, 0), (2, 3), (3, 4), (3, 5), (3, 6)]
    steps = [(512, 512, 1024), (1024,), (512,), (1024,), (1024,), (1024,), (512,)]
    sums, total = reduce(n, lhs, rhs, order, gsum, steps, 1)
    gg, gu, gd, go, gv, gk, gq = sums
    return settle(so, ig, gq, gk, gv, go, gg, gu, gd[:rd], total)


def solution(mesh):
    w = P("section", "fsdp", None)
    r = P(None, "fsdp", None)
    v = P("section", "fsdp")
    return jax.shard_map(
        per_device,
        mesh=mesh,
        in_specs=(r, r, P(None, "fsdp"), r, r, r, P(None, "fsdp")) + (w,) * 7 + (v, v),
        out_specs=(P("section", None, "fsdp", None),) * 2 + (w,) * 7 + (v, v),
        check_vma=False,
    )
```

```python
import functools
import math
import jax
import jax.numpy as jnp
from jax import lax
from jax.experimental import pallas as pl
from jax.experimental.pallas import tpu as pltpu
from jax.sharding import PartitionSpec as P

MESH = pl.DeviceIdType.MESH


def layout(n):
    rest=n//2
    R=min(4,rest); C=rest//R
    return R,C

def gather_kernel(n, P, *refs):
    ins=refs[:P]; outs=refs[P:2*P]; bufs=refs[2*P:3*P]
    own_sem,out_sem,s_zu,s_zd,s_yu,s_yd,s_sb,s_ex,r_main,r_sib=refs[3*P:]
    R,C=layout(n)
    sec=lax.axis_index("section"); f=lax.axis_index("fsdp")
    c=f%2; zy=f//2; y=zy%C; z=zy//C
    def dev(zz,yy,cc): return (sec,(zz*C+yy)*2+cc)
    bar=pltpu.get_barrier_semaphore()
    nb=[(z>0,(z-1,y,c)),(z<R-1,(z+1,y,c)),(y>0,(z,y-1,c)),(y<C-1,(z,y+1,c)),(c>=0,(z,y,1-c))]
    for p in range(P):
        pltpu.make_async_copy(ins[p],bufs[p].at[f],own_sem.at[p]).start()
    for cond,d in nb:
        @pl.when(cond)
        def _():
            pl.semaphore_signal(bar,1,device_id=dev(*d),device_id_type=MESH)
    pl.semaphore_wait(bar,sum(jnp.where(cond,1,0) for cond,d in nb))
    pending=[]
    def send(cond,p,zb,yb,target,ssem,rsem):
        blk=(zb*C+yb)*2+c
        k=zb*C+yb
        def mk():
            return pltpu.make_async_remote_copy(bufs[p].at[blk],bufs[p].at[blk],ssem.at[p,k],rsem.at[p,k],device_id=dev(*target),device_id_type=MESH)
        @pl.when(cond)
        def _(): mk().start()
        pending.append((cond,mk))
    def wait_main(cond,p,zb,yb):
        blk=(zb*C+yb)*2+c; k=zb*C+yb
        @pl.when(cond)
        def _():
            pltpu.make_async_remote_copy(bufs[p].at[blk],bufs[p].at[blk],s_sb.at[p,k],r_main.at[p,k],device_id=dev(z,y,1-c),device_id_type=MESH).wait_recv()
    offload = (C==2)
    T=(c>=0)
    def own(p):
        pltpu.make_async_copy(ins[p],bufs[p].at[f],own_sem.at[p]).wait()
        send(y>0,p,z,y,(z,y-1,c),s_yd,r_main)
        send(y<C-1,p,z,y,(z,y+1,c),s_yu,r_main)
        send(z>0,p,z,y,(z-1,y,c),s_zd,r_main)
        send(z<R-1,p,z,y,(z+1,y,c),s_zu,r_main)
        send(T,p,z,y,(z,y,1-c),s_sb,r_sib)
    def z_arrivals(p):
        for d in range(1,R):
            for sign in (-1,1):
                zb=z+sign*d
                ok=(zb>=0)&(zb<R)
                zbc=jnp.clip(zb,0,R-1)
                wait_main(ok,p,zbc,y)
                if sign<0:
                    send(ok&(z<R-1),p,zbc,y,(z+1,y,c),s_zu,r_main)
                else:
                    send(ok&(z>0),p,zbc,y,(z-1,y,c),s_zd,r_main)
                ydo=ok
                if offload: ydo=ok & jnp.logical_not((c==1)&(zbc==(z+1-2*(z%2))))
                send(ydo&(y>0),p,zbc,y,(z,y-1,c),s_yd,r_main)
                send(ydo&(y<C-1),p,zbc,y,(z,y+1,c),s_yu,r_main)
                send(ok,p,zbc,y,(z,y,1-c),s_sb,r_sib)
    def y_arrivals(p, near):
        for dy in range(1,C):
            for sign in (-1,1):
                yb=y+sign*dy
                oky=(yb>=0)&(yb<C)
                ybc=jnp.clip(yb,0,C-1)
                for d in ([0] if near else range(1,R)):
                    for zs in ((0,) if d==0 else (-1,1)):
                        zb=z+zs*d
                        ok=oky&(zb>=0)&(zb<R)
                        zbc=jnp.clip(zb,0,R-1)
                        wait_main(ok,p,zbc,ybc)
                        if C>2:
                            if sign<0: send(ok&(y<C-1),p,zbc,ybc,(z,y+1,c),s_yu,r_main)
                            else: send(ok&(y>0),p,zbc,ybc,(z,y-1,c),s_yd,r_main)
                        if offload and d==0:
                            send(ok&(c==1),p,zbc,ybc,(z+1-2*(z%2),y,c),s_ex,r_main)
                        send(ok,p,zbc,ybc,(z,y,1-c),s_sb,r_sib)
    def finish(p):
        def body(k,_):
            blk=k*2+1-c
            pltpu.make_async_remote_copy(bufs[p].at[blk],bufs[p].at[blk],s_sb.at[p,k],r_sib.at[p,k],device_id=dev(z,y,1-c),device_id_type=MESH).wait_recv()
            return 0
        lax.fori_loop(0,n//2,body,0)
        pltpu.make_async_copy(bufs[p],outs[p],out_sem.at[p]).start()
    LA=2
    for p in range(min(LA,P)): own(p)
    for p in range(P+2):
        if p+LA<P: own(p+LA)
        if p<P: z_arrivals(p)
        if 0<=p-1<P: y_arrivals(p-1,True)
        if 0<=p-2<P:
            y_arrivals(p-2,False)
            finish(p-2)
    for cond,mk in pending:
        @pl.when(cond)
        def _(): mk().wait_send()
    for p in range(P):
        pltpu.make_async_copy(bufs[p],outs[p],out_sem.at[p]).wait()

def gather(n, shards, cid=0):
    P=len(shards)
    R,C=layout(n)
    h=n//2
    D=pltpu.SemaphoreType.DMA
    return pl.pallas_call(functools.partial(gather_kernel,n,P),
        out_shape=[jax.ShapeDtypeStruct((n,)+s.shape,s.dtype) for s in shards],
        in_specs=[pl.BlockSpec(memory_space=pltpu.HBM)]*P,
        out_specs=[pl.BlockSpec(memory_space=pltpu.HBM)]*P,
        scratch_shapes=[pltpu.VMEM((n,)+s.shape,s.dtype) for s in shards]+[D((P,)),D((P,))]+[D((P,h))]*8,
        compiler_params=pltpu.CompilerParams(collective_id=cid,has_side_effects=True,vmem_limit_bytes=60<<20),
    )(*shards)

HEADS=8; HD=128; MQB=64; MEMK=128; EPS=1e-06; MASKED=-1e30
XC=256

def nn(a,b): return jnp.dot(a,b,preferred_element_type=jnp.float32)
def nt(a,b): return lax.dot_general(a,b,(((1,),(1,)),((),())),preferred_element_type=jnp.float32)
def tn(a,b): return lax.dot_general(a,b,(((0,),(0,)),((),())),preferred_element_type=jnp.float32)

def front_kernel(n, fused, micro, T, D, FF, CACHE, NBLK, *refs):
    it=iter(refs)
    take=lambda k:[next(it) for _ in range(k)]
    x_hbm,og_hbm,docs,mk_hbm,mv_hbm,midx,mreset,again,fgain=take(9)
    ins=take(8)
    (so_hbm,ig_hbm,gsum,e_h,normed_h,mixed_h,n2_h,hidden_h,gi_h,ui_h,ai_h,dq_h,dk_h,dv_h)=take(14)
    bufs=take(8)
    (cur,eg,normed,q,k,v,mixed,n2,g,u,hidden,middle,p,rk,rv,grads,mg,acc,so,ig,mask,gain)=take(22)
    (own_sem,in_sem,c_sem,out_sem,xs,xr,es,er)=take(8)
    ag_sems=take(8)
    B16=jnp.bfloat16
    W=[b.reshape(b.shape[0]*b.shape[1],b.shape[2]) if fused else b for b in bufs[1:]]
    Wq,Wk,Wv,Wo,Wg,Wu,Wd=W
    sec=lax.axis_index("section"); f=lax.axis_index("fsdp")
    scale=HD**-0.5
    R,C=layout(n)
    c=f%2; zy=f//2; y=zy%C; z=zy//C
    def dev(d): return (sec,(d[0]*C+d[1])*2+d[2])
    pieces=[(i,None) for i in range(7)]+[(7,j) for j in range(D//XC)]
    NP=len(pieces)
    nb=[(c>=0,(1-sec,f))]
    if fused:
        nb+=[(z>0,dev((z-1,y,c))),(z<R-1,dev((z+1,y,c))),(y>0,dev((z,y-1,c))),(y<C-1,dev((z,y+1,c))),(c>=0,dev((z,y,1-c)))]
    bar=pltpu.get_barrier_semaphore()
    for cond,d in nb:
        @pl.when(cond)
        def _(d=d): pl.semaphore_signal(bar,1,device_id=d,device_id_type=MESH)
    def own_copy(i):
        return pltpu.make_async_copy(ins[i],bufs[i].at[f] if fused else bufs[i],own_sem.at[i])
    for i in range(8):
        if i or not fused: own_copy(i).start()
    if fused:
        both=jnp.concatenate([again[...].astype(jnp.float32),fgain[...].astype(jnp.float32)],axis=1)
        bufs[0][f]=jnp.broadcast_to(both,bufs[0].shape[1:]).astype(B16)
    def load_cur(): return pltpu.make_async_copy(x_hbm,cur,in_sem.at[0])
    def load_eg(): return pltpu.make_async_copy(og_hbm,eg,in_sem.at[0])
    HC=CACHE//2
    def load_cache(m,kv):
        src=(mk_hbm,mv_hbm)[kv]
        return [pltpu.make_async_copy(src.at[m,pl.ds(i*HC,HC)],grads.at[2*kv+i],c_sem.at[2*kv+i]) for i in range(2)]
    @pl.when(sec==0)
    def _(): load_cur().start()
    @pl.when(sec==1)
    def _():
        for kv in range(2):
            for cp in load_cache(0,kv): cp.start()
        load_eg().start()
    def save(j,src,dst,m):
        return pltpu.make_async_copy(src.at[m],dst.at[m],out_sem.at[j,m])
    def xcopy(m,j):
        cs=pl.ds(j*XC,XC)
        return pltpu.make_async_remote_copy(so.at[m,:,cs],cur.at[m,:,cs],xs.at[m,j],xr.at[m,j],device_id=(1-sec,f),device_id_type=MESH)
    def ecopy(m):
        return pltpu.make_async_remote_copy(ig.at[m],eg.at[m],es.at[m],er.at[m],device_id=(1-sec,f),device_id_type=MESH)
    RB=64
    def rows_loop(fn):
        def b(i,_):
            fn(pl.ds(pl.multiple_of(i*RB,RB),RB)); return 0
        lax.fori_loop(0,T//RB,b,0,unroll=T//RB)
    def cols_loop(N,CH,fn):
        def b(i,_):
            fn(pl.ds(pl.multiple_of(i*CH,CH),CH)); return 0
        lax.fori_loop(0,N//CH,b,0,unroll=N//CH)
    def normalize(x,row):
        inv=lax.rsqrt(jnp.mean(x*x,axis=-1,keepdims=True)+EPS)
        return x*inv*gain[row:row+1,:]
    def norm_back(x,cc,row):
        inv=lax.rsqrt(jnp.mean(x*x,axis=-1,keepdims=True)+EPS)
        s=cc*gain[row:row+1,:]
        gsum[row:row+1,:]+=jnp.sum(cc*x*inv,axis=0,keepdims=True)
        return inv*s-x*(inv*inv*inv)*jnp.mean(s*x,axis=-1,keepdims=True)
    def f_norm(m):
        def f1(r): normed[m,r,:]=normalize(cur[m,r,:].astype(jnp.float32),0).astype(B16)
        rows_loop(f1)
        save(0,normed,normed_h,m).start()
    def f_proj(m,dst,w):
        def f2(cs): dst[m,:,cs]=nn(normed[m],w[:,cs]).astype(B16)
        cols_loop(D,256,f2)
    G=4
    def by_block(a,other,hs,m,fn):
        return jnp.concatenate([fn(a[b*MQB:(b+1)*MQB],other[m,b*MEMK:(b+1)*MEMK,hs]) for b in range(NBLK)],axis=0)
    def halves(a): return [a[:,i:i+HD] for i in range(0,T,HD)]
    def row_sum(*parts): return jnp.sum(functools.reduce(jnp.add,parts),axis=-1,keepdims=True)
    def row_max(*parts): return jnp.max(functools.reduce(jnp.maximum,parts),axis=-1,keepdims=True)
    def f_attend(m,recall):
        for h0 in range(0,HEADS,G):
            HS=[slice(h*HD,h*HD+HD) for h in range(h0,h0+G)]
            qs=[q[m,:,hs] for hs in HS]
            s=[nt(a,k[m,:,hs]) for a,hs in zip(qs,HS)]
            if recall: x=[by_block(a,rk,hs,m,nt) for a,hs in zip(qs,HS)]
            ok=mask[m].astype(jnp.float32)>0.5
            s=[jnp.where(ok,a*scale,MASKED) for a in s]
            if recall:
                live=jnp.concatenate([jnp.broadcast_to(mreset[pl.ds(m,1),b:b+1],(MQB,MEMK)) for b in range(NBLK)],axis=0)==0
                x=[jnp.where(live,a*scale,MASKED) for a in x]
                top=[row_max(b,*halves(a)) for a,b in zip(s,x)]
                xe=[jnp.exp(b-t) for b,t in zip(x,top)]
            else: top=[row_max(*halves(a)) for a in s]
            se=[jnp.exp(a-t) for a,t in zip(s,top)]
            if recall: inv=[1.0/row_sum(b,*halves(a)) for a,b in zip(se,xe)]
            else: inv=[1.0/row_sum(*halves(a)) for a in se]
            ps=[(a*i).astype(B16) for a,i in zip(se,inv)]
            o=[nn(a,v[m,:,hs]) for a,hs in zip(ps,HS)]
            if recall:
                pr=[(a*i).astype(B16) for a,i in zip(xe,inv)]
                o=[a+by_block(b,rv,hs,m,nn) for a,b,hs in zip(o,pr,HS)]
            for j in range(G):
                p[m,h0+j,:,0:T]=ps[j]
                if recall: p[m,h0+j,:,T:T+MEMK]=pr[j]
                mixed[m,:,HS[j]]=o[j].astype(B16)
        save(1,mixed,mixed_h,m).start()
    def f_out(m):
        def f3(cs): middle[m,:,cs]=cur[m,:,cs].astype(jnp.float32)+nn(mixed[m],Wo[:,cs])
        cols_loop(D,256,f3)
        def f4(r): n2[m,r,:]=normalize(middle[m,r,:],1).astype(B16)
        rows_loop(f4)
        save(2,n2,n2_h,m).start()
    def f_gate(m):
        def f5(cs):
            a=n2[m]
            gg=nn(a,Wg[:,cs]); uu=nn(a,Wu[:,cs])
            sg=jax.nn.sigmoid(gg)
            act=gg*sg
            g[m,:,cs]=(uu*(sg*(1.0+gg*(1.0-sg)))).astype(B16); u[m,:,cs]=act.astype(B16)
            hidden[m,:,cs]=(act*uu).astype(B16)
        cols_loop(FF,256,f5)
        save(3,hidden,hidden_h,m).start()
    def f_down(m,j):
        cs=pl.ds(j*XC,XC)
        so[m,:,cs]=(middle[m,:,cs]+nn(hidden[m],Wd[:,cs])).astype(B16)
    def recall(m,kv):
        for cp in load_cache(m,kv): cp.wait()
        dst=(rk,rv)[kv]
        def body(b,_):
            idx=midx[m,pl.ds(b,1),:]
            col=jnp.broadcast_to(idx.astype(jnp.float32),(MEMK,MEMK)).T[:,0:1].astype(jnp.int32)
            io=lax.broadcasted_iota(jnp.int32,(MEMK,HC),1)
            rows=nn(jnp.where(io==col,1.0,0.0).astype(B16),grads[2*kv])
            rows=rows+nn(jnp.where(io+HC==col,1.0,0.0).astype(B16),grads[2*kv+1])
            dst[m,pl.ds(pl.multiple_of(b*MEMK,MEMK),MEMK),:]=rows.astype(B16)
            return 0
        lax.fori_loop(0,NBLK,body,0)
        if m+1<micro:
            for cp in load_cache(m+1,kv): cp.start()
    def setup():
        if not fused:
            gain[...]=bufs[0][0,0:8,:].astype(jnp.float32)
            return
        lane=lax.broadcasted_iota(jnp.int32,(8,128),1)
        for e in range(n//2):
            lo=bufs[0][2*e].astype(jnp.float32)[0:8]
            hi=bufs[0][2*e+1].astype(jnp.float32)[0:8]
            cs=pl.ds(e*128,128)
            gain[0:1,cs]=jnp.where(lane<64,lo,pltpu.roll(hi,64,1))[0:1]
            gain[1:2,cs]=jnp.where(lane<64,pltpu.roll(lo,64,1),hi)[0:1]
    def each(fn):
        def b(m,_):
            fn(m); return 0
        return lambda: lax.fori_loop(0,micro,b,0)
    def down(j):
        def go():
            def b(m,_):
                f_down(m,j); xcopy(m,j).start(); return 0
            lax.fori_loop(0,micro,b,0)
        return go
    first={0:[each(f_norm)],1:[each(lambda m:f_proj(m,q,Wq))],2:[each(lambda m:f_proj(m,k,Wk))],
        3:[each(lambda m:f_proj(m,v,Wv)),lambda:f_attend(0,False)],
        4:[lambda:[f_attend(m,False) for m in range(1,micro)],each(f_out)],
        6:[lambda:f_gate(0)]}
    for j in range(D//XC): first[7+j]=[down(j)]
    first[7]=[lambda:[f_gate(m) for m in range(1,micro)]]+first[7]
    units=[(m,kv) for m in range(micro) for kv in range(2)]
    second={i:[functools.partial(recall,*un)] for i,un in enumerate(units)}
    def arrived(i):
        if i==0: setup()
        @pl.when(sec==0)
        def _():
            for fn in first.get(i,[]): fn()
        @pl.when(sec==1)
        def _():
            for fn in second.get(i,[]): fn()
    gsum[...]=jnp.zeros_like(gsum)
    ri=lax.broadcasted_iota(jnp.int32,(T,T),0); ci=lax.broadcasted_iota(jnp.int32,(T,T),1)
    def prepare():
        for m in range(micro):
            row=jnp.broadcast_to(docs[m:m+1,:].astype(jnp.float32),(T,T))
            mask[m]=jnp.where((row==row.T)&(ci<=ri),1.0,0.0).astype(B16)
        @pl.when(sec==0)
        def _(): load_cur().wait()
        @pl.when(sec==1)
        def _(): load_eg().wait()
    pl.semaphore_wait(bar,sum(jnp.where(cond,1,0) for cond,d in nb))
    pending=[]
    if fused:
        s_zu,s_zd,s_yu,s_yd,s_sb,s_ex,r_main,r_sib=ag_sems
        def part(i,blk):
            b,j=pieces[i]
            return bufs[b].at[blk] if j is None else bufs[b].at[blk,:,pl.ds(j*XC,XC)]
        def send(cond,i,zb,yb,target,ssem,rsem):
            blk=(zb*C+yb)*2+c; kk=zb*C+yb
            def mk():
                return pltpu.make_async_remote_copy(part(i,blk),part(i,blk),ssem.at[i,kk],rsem.at[i,kk],device_id=dev(target),device_id_type=MESH)
            @pl.when(cond)
            def _(): mk().start()
            pending.append((cond,mk))
        def wait_main(cond,i,zb,yb):
            blk=(zb*C+yb)*2+c; kk=zb*C+yb
            @pl.when(cond)
            def _():
                pltpu.make_async_remote_copy(part(i,blk),part(i,blk),s_sb.at[i,kk],r_main.at[i,kk],device_id=dev((z,y,1-c)),device_id_type=MESH).wait_recv()
        OFF=lambda i: C==2 and R%2==0
        zx=z+1-2*(z%2)
        true=c>=0
        def own(i):
            b,j=pieces[i]
            if not j and b: own_copy(b).wait()
            send(y>0,i,z,y,(z,y-1,c),s_yd,r_main)
            send(y<C-1,i,z,y,(z,y+1,c),s_yu,r_main)
            send(z>0,i,z,y,(z-1,y,c),s_zd,r_main)
            send(z<R-1,i,z,y,(z+1,y,c),s_zu,r_main)
            send(true,i,z,y,(z,y,1-c),s_sb,r_sib)
        def z_arrivals(i,d):
            if True:
                for sign in (-1,1):
                    zb=z+sign*d
                    ok=(zb>=0)&(zb<R)
                    zbc=jnp.clip(zb,0,R-1)
                    wait_main(ok,i,zbc,y)
                    if sign<0: send(ok&(z<R-1),i,zbc,y,(z+1,y,c),s_zu,r_main)
                    else: send(ok&(z>0),i,zbc,y,(z-1,y,c),s_zd,r_main)
                    ydo=ok&jnp.logical_not((c==1)&(zbc==zx)) if OFF(i) else ok
                    send(ydo&(y>0),i,zbc,y,(z,y-1,c),s_yd,r_main)
                    send(ydo&(y<C-1),i,zbc,y,(z,y+1,c),s_yu,r_main)
                    send(ok,i,zbc,y,(z,y,1-c),s_sb,r_sib)
        def y_arrivals(i,near):
            for dy in range(1,C):
                for sign in (-1,1):
                    yb=y+sign*dy
                    oky=(yb>=0)&(yb<C)
                    ybc=jnp.clip(yb,0,C-1)
                    for d in ([0] if near else range(1,R)):
                        for zs in ((0,) if d==0 else (-1,1)):
                            zb=z+zs*d
                            ok=oky&(zb>=0)&(zb<R)
                            zbc=jnp.clip(zb,0,R-1)
                            wait_main(ok,i,zbc,ybc)
                            if C>2:
                                if sign<0: send(ok&(y<C-1),i,zbc,ybc,(z,y+1,c),s_yu,r_main)
                                else: send(ok&(y>0),i,zbc,ybc,(z,y-1,c),s_yd,r_main)
                            if OFF(i) and d==0:
                                send(ok&(c==1),i,zbc,ybc,(zx,y,c),s_ex,r_main)
                            send(ok,i,zbc,ybc,(z,y,1-c),s_sb,r_sib)
        def finish(i):
            def body(kk,_):
                blk=kk*2+1-c
                pltpu.make_async_remote_copy(part(i,blk),part(i,blk),s_sb.at[i,kk],r_sib.at[i,kk],device_id=dev((z,y,1-c)),device_id_type=MESH).wait_recv()
                return 0
            lax.fori_loop(0,n//2,body,0)
        LA=2
        LAST=R
        for i in range(LA): own(i)
        prepare()
        for i in range(NP+LAST):
            if i+LA<NP: own(i+LA)
            for d in range(1,R):
                if 0<=i-d+1<NP: z_arrivals(i-d+1,d)
            if 0<=i-1<NP: y_arrivals(i-1,True)
            if 0<=i-LAST+1<NP:
                y_arrivals(i-LAST+1,False)
                finish(i-LAST+1)
                arrived(i-LAST+1)
    else:
        prepare()
        for i in range(NP):
            b,j=pieces[i]
            if not j: own_copy(b).wait()
            arrived(i)
    for cond,mk in pending:
        @pl.when(cond)
        def _(mk=mk): mk().wait_send()
    @pl.when(sec==1)
    def _():
        def forward(m,_):
            for j in range(D//XC): xcopy(m,j).wait_recv()
            f_norm(m)
            f_proj(m,q,Wq); f_proj(m,k,Wk); f_proj(m,v,Wv)
            f_attend(m,True)
            f_out(m)
            f_gate(m)
            for j in range(D//XC): f_down(m,j)
            return 0
        lax.fori_loop(0,micro,forward,0)
    def gsave(j,i,dst,m): return pltpu.make_async_copy(grads.at[i,pl.ds(pl.multiple_of(m*T,T),T)],dst.at[m],out_sem.at[j,m])
    def b_attend(m,ms,recall):
        for h0 in range(0,HEADS,G):
            HS=[slice(h*HD,h*HD+HD) for h in range(h0,h0+G)]
            mh=[normed[m,:,hs] for hs in HS]
            ps=[p[m,h,:,0:T] for h in range(h0,h0+G)]
            pg=[nt(a,v[m,:,hs]) for a,hs in zip(mh,HS)]
            if recall:
                pr=[p[m,h,:,T:T+MEMK].astype(jnp.float32) for h in range(h0,h0+G)]
                rg=[by_block(a,rv,hs,m,nt) for a,hs in zip(mh,HS)]
            dv=[tn(a,b) for a,b in zip(ps,mh)]
            pf=[a.astype(jnp.float32) for a in ps]
            if recall:
                w=[row_sum(c_*d_,*halves(a*b)) for a,b,c_,d_ in zip(pf,pg,pr,rg)]
                dr=[(a*(b-t)).astype(B16) for a,b,t in zip(pr,rg,w)]
            else: w=[row_sum(*halves(a*b)) for a,b in zip(pf,pg)]
            ds=[(a*(b-t)).astype(B16) for a,b,t in zip(pf,pg,w)]
            dq=[nn(a,k[m,:,hs]) for a,hs in zip(ds,HS)]
            if recall: dq=[a+by_block(b,rk,hs,m,nn) for a,b,hs in zip(dq,dr,HS)]
            dk=[tn(a,q[m,:,hs]) for a,hs in zip(ds,HS)]
            for j in range(G):
                grads[3,ms,HS[j]]=dv[j].astype(B16)
                grads[1,ms,HS[j]]=(dq[j]*scale).astype(B16)
                grads[2,ms,HS[j]]=(dk[j]*scale).astype(B16)
    def backward(m,_):
        @pl.when(sec==0)
        def _(): ecopy(m).wait_recv()
        save(4,so,so_hbm,m).start()
        save(5,eg,e_h,m).start()
        def b1(cs):
            hg=nt(eg[m],Wd[cs,:])
            u[m,:,cs]=(hg*u[m,:,cs].astype(jnp.float32)).astype(B16)
            g[m,:,cs]=(hg*g[m,:,cs].astype(jnp.float32)).astype(B16)
        cols_loop(FF,256,b1)
        save(6,g,gi_h,m).start(); save(7,u,ui_h,m).start()
        def b2(cs): acc[:,cs]=nt(g[m],Wg[cs,:])+nt(u[m],Wu[cs,:])
        cols_loop(D,256,b2)
        ms=pl.ds(pl.multiple_of(m*T,T),T)
        def b3(r):
            t_=eg[m,r,:].astype(jnp.float32)+norm_back(middle[m,r,:],acc[r,:],1)
            mg[r,:]=t_; grads[0,pl.ds(pl.multiple_of(m*T,T)+r.start,RB),:]=t_.astype(B16)
        rows_loop(b3)
        gsave(8,0,ai_h,m).start()
        save(0,normed,normed_h,m).wait()
        def b4(cs): normed[m,:,cs]=nt(grads[0,ms,:],Wo[cs,:]).astype(B16)
        cols_loop(D,256,b4)
        pl.when(sec==0)(lambda: b_attend(m,ms,False))
        pl.when(sec==1)(lambda: b_attend(m,ms,True))
        gsave(9,1,dq_h,m).start(); gsave(10,2,dk_h,m).start(); gsave(11,3,dv_h,m).start()
        def b5(cs): acc[:,cs]=nt(grads[1,ms,:],Wq[cs,:])+nt(grads[2,ms,:],Wk[cs,:])+nt(grads[3,ms,:],Wv[cs,:])
        cols_loop(D,256,b5)
        def b6(r): ig[m,r,:]=(mg[r,:]+norm_back(cur[m,r,:].astype(jnp.float32),acc[r,:],0)).astype(B16)
        rows_loop(b6)
        @pl.when(sec==1)
        def _(): ecopy(m).start()
        save(12,ig,ig_hbm,m).start()
        return 0
    lax.fori_loop(0,micro,backward,0)
    for m in range(micro):
        @pl.when(sec==0)
        def _():
            for j in range(D//XC): xcopy(m,j).wait_send()
        @pl.when(sec==1)
        def _(): ecopy(m).wait_send()
        for j,(s,d) in enumerate([(mixed,mixed_h),(n2,n2_h),(hidden,hidden_h),(so,so_hbm),(eg,e_h),(g,gi_h),(u,ui_h)],1):
            save(j,s,d,m).wait()
        for j,i,d in ((8,0,ai_h),(9,1,dq_h),(10,2,dk_h),(11,3,dv_h)):
            gsave(j,i,d,m).wait()
        save(12,ig,ig_hbm,m).wait()

def front(n, fused, x, og, docs, mk, mv, midx, mreset, again, fgain, vec, weights, cid=2):
    micro,T,D=x.shape
    FF=weights[4].shape[1]
    CACHE=mk.shape[1]; NBLK=midx.shape[1]
    B=jnp.bfloat16; F=jnp.float32
    V=pltpu.VMEM
    act=(micro,T,D); fact=(micro,T,FF)
    S=jax.ShapeDtypeStruct
    outs=[S(act,B),S(act,B),S((8,D),F),S(act,B),S(act,B),S(act,B),S(act,B),S(fact,B),S(fact,B),S(fact,B),S(act,B),S(act,B),S(act,B),S(act,B)]
    ws=[vec]+list(weights)
    scratch=[V((n,16,128),B) if fused else V(vec.shape,B)]
    scratch+=[V((n,)+w.shape if fused else w.shape,B) for w in weights]
    scratch+=[V(act,B)]*8+[V(fact,B)]*3+[V(act,F),V((micro,HEADS,T,T+MEMK),B),V((micro,NBLK*MEMK,D),B),V((micro,NBLK*MEMK,D),B),V((4,micro*T,D),B),V((T,D),F),V((T,D),F),V(act,B),V(act,B),V((micro,T,T),B),V((8,D),F)]
    DM=pltpu.SemaphoreType.DMA
    NP=7+D//XC
    scratch+=[DM((8,)),DM((2,)),DM((4,)),DM((13,micro)),DM((micro,D//XC)),DM((micro,D//XC)),DM((micro,)),DM((micro,))]
    scratch+=[DM((NP,n//2) if fused else (1,))]*8
    HB=pl.BlockSpec(memory_space=pltpu.HBM); VB=pl.BlockSpec(memory_space=pltpu.VMEM)
    return pl.pallas_call(functools.partial(front_kernel,n,fused,micro,T,D,FF,CACHE,NBLK),
        out_shape=outs,
        in_specs=[HB,HB,VB,HB,HB,VB,VB,VB,VB]+[HB]*8,
        out_specs=[HB,HB,VB]+[HB]*11,
        scratch_shapes=scratch,
        compiler_params=pltpu.CompilerParams(collective_id=cid,has_side_effects=True,vmem_limit_bytes=64<<20),
    )(x,og,docs,mk,mv,midx,mreset,again,fgain,*ws)


COLS=1024
NDIRECT=2
def plan(n, lhs_shapes, rhs_shapes, weights, steps):
    pieces=[]
    for w,(l,r) in enumerate(weights):
        rows=lhs_shapes[l][1]//n; N=rhs_shapes[r][1]
        c0=0
        for step in steps[w]:
            pieces.append((w,rows,c0,step)); c0+=step
        while c0<N:
            step=min(steps[w][-1],N-c0)
            pieces.append((w,rows,c0,step)); c0+=step
    return pieces

def reduce_kernel(n, tok, lhs_shapes, rhs_shapes, weights, pieces, vec_rows, SLOTS, *refs):
    NP=len(pieces); NL=len(lhs_shapes); NR=len(rhs_shapes); NW=len(weights)
    R,C=layout(n); H=n//2
    it=iter(refs)
    take=lambda k:[next(it) for _ in range(k)]
    lhs=take(NL); rhs=take(NR); vec=next(it)
    outs=take(NW); vec_out=next(it)
    ring=next(it); tbuf=take(NL)
    keep=take(NP); sibr=take(NP); yr=take(NP); xr=take(NP); zu=take(NP); zd=take(NP); fin=take(NP)
    shapes=sorted({p[1] for p in pieces})
    stage_of=dict(zip(shapes,take(len(shapes))))
    vecb=next(it); vecr=next(it)
    (ld_sem,sib_s,sib_r,y_s,y_r,x_s,x_r,zu_s,zu_r,zd_s,zd_r,v_s,v_r,o_s)=take(14)
    sec=lax.axis_index("section"); f=lax.axis_index("fsdp")
    c=f%2; zy=f//2; y=zy%C; z=zy//C
    OFF=lambda i: C==2 and R%2==0
    zx=z+1-2*(z%2)
    def dev(zz,yy,cc): return (sec,(zz*C+yy)*2+cc)
    def rcopy(src,dst,ss,rs,d):
        return pltpu.make_async_remote_copy(src,dst,ss,rs,device_id=dev(*d),device_id_type=MESH)
    LOGN=n.bit_length()-1
    nb=[]
    nb.append((c>=0,dev(z,y,1-c)))
    for k in range(1,C): nb.append((c>=0,dev(z,lax.rem(y+k,C),c)))
    for k in range(1,R): nb.append((c>=0,dev(lax.rem(z+k,R),y,c)))
    bar=pltpu.get_barrier_semaphore()
    loads=[]
    def parts(ref,shape):
        return [(ref,c0,min(COLS,shape[1]-c0)) for c0 in range(0,shape[1],COLS)]
    load_id={}
    def need(kind,i):
        key=(kind,i)
        if key in load_id: return
        ref=lhs[i] if kind=="l" else rhs[i]
        sh=lhs_shapes[i] if kind=="l" else rhs_shapes[i]
        ids=[]
        for pr in parts(ref,sh):
            ids.append(len(loads)); loads.append(pr)
        load_id[key]=ids
    for l,r in weights:
        need("l",l); need("r",r)
    issued=[0]; freed=set()
    def load_copy(k):
        ref,c0,w=loads[k]
        return pltpu.make_async_copy(ref.at[:,pl.ds(c0,w)],ring.at[k%SLOTS,:,pl.ds(0,w)],ld_sem.at[k%SLOTS])
    def pump():
        while issued[0]<len(loads) and (issued[0]<SLOTS or (issued[0]-SLOTS) in freed):
            load_copy(issued[0]).start(); issued[0]+=1
    pump()
    for cond,d in nb:
        @pl.when(cond)
        def _(): pl.semaphore_signal(bar,1,device_id=d,device_id_type=MESH)
    waited=set()
    def wait_load(k):
        if k not in waited:
            load_copy(k).wait(); waited.add(k)
    transposed=set()
    def ensure_lhs(l):
        if l in transposed: return
        transposed.add(l)
        for j,k in enumerate(load_id[("l",l)]):
            wait_load(k)
            w=loads[k][2]
            CH=256
            def body(i,_,k=k,j=j):
                o=pl.multiple_of(i*CH,CH)
                tbuf[l][pl.ds(pl.multiple_of(j*COLS+o,CH),CH),:]=ring[k%SLOTS,:,pl.ds(o,CH)].T
                return 0
            lax.fori_loop(0,w//CH,body,0)
            freed.add(k)
        pump()
    last_use={}
    for i,(w,rows,c0,nc) in enumerate(pieces):
        l,r=weights[w]
        last_use[load_id[("r",r)][c0//COLS]]=i
    sends={}
    cur_piece=[0]
    stage_use={}
    def compute(i):
        w,rows,c0,nc=pieces[i]
        l,r=weights[w]
        ensure_lhs(l)
        k=load_id[("r",r)][c0//COLS]
        wait_load(k)
        lc=c0%COLS
        u=stage_use.get(rows,0); stage_use[rows]=u+1
        st=stage_of[rows].at[u%2,:,:,pl.ds(0,nc)]
        if u>=2: sib_waits[rows].pop(0)()
        T4=tbuf[l].reshape(H,2,rows,tok)
        CH=256
        for which,dst in ((1-c,st),(c,keep[i])):
            def body(j,_,which=which,dst=dst):
                o=pl.multiple_of(j*CH,CH)
                a=T4[:,which].reshape(H*rows,tok)
                b=ring[k%SLOTS,:,pl.ds(pl.multiple_of(lc+o,CH),CH)]
                res=jnp.dot(a,b,preferred_element_type=jnp.float32).astype(jnp.bfloat16)
                dst[:,:,pl.ds(o,CH)]=res.reshape(H,rows,CH)
                return 0
            lax.fori_loop(0,nc//CH,body,0)
            if dst is not keep[i]:
                cp=rcopy(st,sibr[i],sib_s.at[i],sib_r.at[i],(z,y,1-c))
                cp.start()
                sib_waits.setdefault(rows,[]).append(cp.wait_send)
        if last_use[k]==i:
            freed.add(k); pump()
    sib_waits={}
    def add_into(dst,src,rows):
        def body(j,_):
            o=pl.multiple_of(j*16,16)
            dst[pl.ds(o,16),:]=dst[pl.ds(o,16),:]+src[pl.ds(o,16),:]
            return 0
        lax.fori_loop(0,rows//16,body,0)
    def send(tag,cond,cp):
        if cond is None: cp().start()
        else:
            @pl.when(cond)
            def _(): cp().start()
        sends.setdefault(tag,[]).append((cond,cp))
    def sib_add(i):
        w,rows,c0,nc=pieces[i]
        rcopy(sibr[i],sibr[i],sib_s.at[i],sib_r.at[i],(z,y,1-c)).wait_recv()
        def body(k,_):
            add_into(keep[i].at[k],sibr[i].at[k],rows)
            return 0
        lax.fori_loop(0,H,body,0)
        offload=OFF(i)
        if offload:
            send((i,'y'),c==1,lambda: rcopy(keep[i].at[zx*C+1-y],xr[i],x_s.at[i],x_r.at[i],(zx,y,c)))
        for kz in range(R-1,-1,-1):
            zt=lax.rem(z+kz,R)
            for ky in range(1,C):
                yt=lax.rem(y+ky,C)
                slot=C-1-ky
                cp=lambda zt=zt,yt=yt,slot=slot: rcopy(keep[i].at[zt*C+yt],yr[i].at[slot,zt],y_s.at[i,slot,zt],y_r.at[i,slot,zt],(z,yt,c))
                if offload and kz==0:
                    continue
                send((i,'y'),(jnp.logical_not((c==1)&(zt==zx))) if offload else None,cp)
    def x_add(i):
        w,rows,c0,nc=pieces[i]
        if not OFF(i): return
        @pl.when(c==1)
        def _():
            rcopy(xr[i],xr[i],x_s.at[i],x_r.at[i],(zx,y,c)).wait_recv()
            add_into(keep[i].at[z*C+1-y],xr[i],rows)
        send((i,'y'),None,lambda: rcopy(keep[i].at[z*C+1-y],yr[i].at[0,z],y_s.at[i,0,z],y_r.at[i,0,z],(z,1-y,c)))
    def y_add(i):
        w,rows,c0,nc=pieces[i]
        offload=OFF(i)
        for kz in range(R-1,-1,-1):
            zt=lax.rem(z+kz,R)
            for slot in range(C-1):
                def go(zt=zt,slot=slot):
                    rcopy(yr[i].at[slot,zt],yr[i].at[slot,zt],y_s.at[i,slot,zt],y_r.at[i,slot,zt],(z,y,1-c)).wait_recv()
                    add_into(keep[i].at[zt*C+y],yr[i].at[slot,zt],rows)
                if offload and kz!=0:
                    pl.when(jnp.logical_not((c==1)&(zt==zx)))(go)
                else: go()
    direct=lambda i: i>=NP-NDIRECT
    def z_step(i,s):
        w,rows,c0,nc=pieces[i]
        if direct(i):
            if s: return
            for k in range(1,R):
                t=lax.rem(z+k,R)
                send((i,0),None,lambda k=k,t=t: rcopy(keep[i].at[t*C+y],zu[i].at[R-1-k],zu_s.at[i,k-1],zu_r.at[i,R-1-k],(t,y,c)))
            return
        def line(zs,up):
            rb,rr,ss=(zu,zu_r,zu_s) if up else (zd,zd_r,zd_s)
            first=(zs==0) if up else (zs==R-1)
            targets=range(R-1,zs,-1) if up else range(0,zs)
            nxt=zs+1 if up else zs-1
            cps=[]
            for t in targets:
                k=abs(t-zs)
                cps.append((k,lambda t=t,k=k: rcopy(keep[i].at[t*C+y],rb[i].at[k-1],ss.at[i,k-1],rr.at[i,k-1],(nxt,y,c)),t))
            def go():
                for k,cp,t in cps:
                    if not first:
                        rcopy(rb[i].at[k],rb[i].at[k],ss.at[i,k],rr.at[i,k],(zs,y,1-c)).wait_recv()
                        add_into(keep[i].at[t*C+y],rb[i].at[k],rows)
                    cp().start()
            pl.when(z==zs)(go)
            for k,cp,t in cps: sends.setdefault((i,zs if up else R-1-zs),[]).append((z==zs,cp))
        line(s,True)
        line(R-1-s,False)
    def final(i):
        w,rows,c0,nc=pieces[i]
        blk=z*C+y
        if direct(i):
            for k in range(R-1):
                rcopy(zu[i].at[k],zu[i].at[k],zu_s.at[i,k],zu_r.at[i,k],(z,y,1-c)).wait_recv()
            def body(j,_):
                o=pl.ds(pl.multiple_of(j*16,16),16)
                a=keep[i][blk,o,:].astype(jnp.float32)
                for k in range(R-1): a=a+zu[i][k,o,:].astype(jnp.float32)
                fin[i][o,:]=a.astype(jnp.bfloat16)
                return 0
            lax.fori_loop(0,rows//16,body,0)
            pltpu.make_async_copy(fin[i],outs[w].at[:,pl.ds(c0,nc)],o_s.at[i]).start()
            return
        @pl.when(z>0)
        def _():
            rcopy(zu[i].at[0],zu[i].at[0],zu_s.at[i,0],zu_r.at[i,0],(z,y,1-c)).wait_recv()
        @pl.when(z<R-1)
        def _():
            rcopy(zd[i].at[0],zd[i].at[0],zd_s.at[i,0],zd_r.at[i,0],(z,y,1-c)).wait_recv()
        def body(j,_):
            o=pl.ds(pl.multiple_of(j*16,16),16)
            a=keep[i][blk,o,:].astype(jnp.float32)
            a=a+jnp.where(z>0,zu[i][0,o,:].astype(jnp.float32),0.0)+jnp.where(z<R-1,zd[i][0,o,:].astype(jnp.float32),0.0)
            fin[i][o,:]=a.astype(jnp.bfloat16)
            return 0
        lax.fori_loop(0,rows//16,body,0)
        pltpu.make_async_copy(fin[i],outs[w].at[:,pl.ds(c0,nc)],o_s.at[i]).start()
    def vec_step(k):
        if k>0:
            vcopy(k-1).wait()
            vecb[k]=vecb[k-1]+vecr[k-1]
        if k<LOGN: vcopy(k).start()
        else:
            cp=pltpu.make_async_copy(vecb.at[LOGN],vec_out,o_s.at[NP]); cp.start()
    def vcopy(k):
        return pltpu.make_async_remote_copy(vecb.at[k],vecr.at[k],v_s.at[k],v_r.at[k],device_id=(sec,f^(1<<k)),device_id_type=MESH)
    cp=pltpu.make_async_copy(vec,vecb.at[0],o_s.at[NP]); cp.start(); cp.wait()
    pl.semaphore_wait(bar,sum(jnp.where(cond,1,0) for cond,d in nb))
    def end_sends(tag):
        for cond,cp in sends.pop(tag,[]):
            if cond is None: cp().wait_send()
            else:
                @pl.when(cond)
                def _(cp=cp): cp().wait_send()
    LAGY=3
    for t in range(NP+LAGY+R+1):
        if t<NP: compute(t)
        if 0<=t-1<NP: sib_add(t-1)
        if 0<=t-2<NP: x_add(t-2)
        if t<=LOGN: vec_step(t)
        if 0<=t-LAGY<NP: y_add(t-LAGY)
        for s in range(R):
            i=t-LAGY-s
            if 0<=i<NP: z_step(i,s)
        i=t-LAGY-R
        if 0<=i<NP and not direct(i): final(i)
        i=t-LAGY-1
        if 0<=i<NP and direct(i): final(i)
        end_sends((t-LAGY-1,'y'))
        for s in range(R): end_sends((t-LAGY-s-2,s))
    for q in sib_waits.values():
        for wfn in q: wfn()
    for tag in list(sends): end_sends(tag)
    for i in range(NP):
        w,rows,c0,nc=pieces[i]
        pltpu.make_async_copy(fin[i],outs[w].at[:,pl.ds(c0,nc)],o_s.at[i]).wait()
    pltpu.make_async_copy(vecb.at[LOGN],vec_out,o_s.at[NP]).wait()

def reduce(n, lhs, rhs, weights, vec, steps, cid=1, SLOTS=6):
    tok=lhs[0].shape[0]
    ls=[a.shape for a in lhs]; rs=[a.shape for a in rhs]
    pieces=plan(n,ls,rs,weights,steps)
    R,C=layout(n); H=n//2
    NP=len(pieces)
    LOGN=n.bit_length()-1
    D=pltpu.SemaphoreType.DMA
    B=jnp.bfloat16
    V=pltpu.VMEM
    shapes=sorted({(p[1],max(o[3] for o in pieces if o[1]==p[1])) for p in pieces})
    scratch=[V((SLOTS,tok,COLS),B)]+[V((s[1],tok),B) for s in ls]
    scratch+=[V((H,p[1],p[3]),B) for p in pieces]
    scratch+=[V((H,p[1],p[3]),B) for p in pieces]
    scratch+=[V((C-1,R,p[1],p[3]),B) for p in pieces]
    scratch+=[V((p[1],p[3]) if C==2 else (16,128),B) for p in pieces]
    scratch+=[V((R-1,p[1],p[3]),B) for p in pieces]*2
    scratch+=[V((p[1],p[3]),B) for p in pieces]
    scratch+=[V((2,H)+s,B) for s in shapes]
    scratch+=[V((LOGN+1,)+vec.shape,vec.dtype),V((LOGN,)+vec.shape,vec.dtype)]
    scratch+=[D((SLOTS,)),D((NP,)),D((NP,)),D((NP,C-1,R)),D((NP,C-1,R)),D((NP,)),D((NP,)),D((NP,R-1)),D((NP,R-1)),D((NP,R-1)),D((NP,R-1)),D((LOGN,)),D((LOGN,)),D((NP+1,))]
    HB=pl.BlockSpec(memory_space=pltpu.HBM)
    res=pl.pallas_call(functools.partial(reduce_kernel,n,tok,ls,rs,weights,pieces,vec.shape[0],SLOTS),
        out_shape=[jax.ShapeDtypeStruct((ls[l][1]//n,rs[r][1]),B) for l,r in weights]+[jax.ShapeDtypeStruct(vec.shape,vec.dtype)],
        in_specs=[HB]*(len(lhs)+len(rhs)+1),
        out_specs=[HB]*(len(weights)+1),
        scratch_shapes=scratch,
        compiler_params=pltpu.CompilerParams(collective_id=cid,has_side_effects=True,vmem_limit_bytes=63<<20),
    )(*lhs,*rhs,vec)
    return res[:-1],res[-1]


def settle_kernel(count, gw, *refs):
    ins = refs[:count]
    total = refs[count]
    outs = refs[count + 1 : 2 * count + 1]
    again, fgain = refs[2 * count + 1 : 2 * count + 3]
    held = refs[2 * count + 3 : 3 * count + 3]
    in_sem, out_sem = refs[3 * count + 3 :]
    load = [pltpu.make_async_copy(a, h, in_sem.at[i]) for i, (a, h) in enumerate(zip(ins, held))]
    store = [pltpu.make_async_copy(h, b.at[0], out_sem.at[i]) for i, (h, b) in enumerate(zip(held, outs))]
    for cp in load:
        cp.start()
    width = total.shape[1]
    f = lax.axis_index("fsdp")
    mine = pltpu.roll(total[...], lax.rem(width - f * gw, width), 1)
    again[...] = mine[0:1, 0:gw].astype(again.dtype)
    fgain[...] = mine[1:2, 0:gw].astype(fgain.dtype)
    for cp, out in zip(load, store):
        cp.wait()
        out.start()
    for cp in store:
        cp.wait()


def settle(*arrays):
    *ins, total = arrays
    gw = total.shape[1] // lax.axis_size("fsdp")
    HB = pl.BlockSpec(memory_space=pltpu.HBM)
    VB = pl.BlockSpec(memory_space=pltpu.VMEM)
    S = jax.ShapeDtypeStruct
    return pl.pallas_call(
        functools.partial(settle_kernel, len(ins), gw),
        out_shape=[S((1,) + a.shape, a.dtype) for a in ins] + [S((1, gw), jnp.bfloat16)] * 2,
        in_specs=[HB] * len(ins) + [VB],
        out_specs=[HB] * len(ins) + [VB] * 2,
        scratch_shapes=[pltpu.VMEM(a.shape, a.dtype) for a in ins] + [pltpu.SemaphoreType.DMA((len(ins),))] * 2,
        compiler_params=pltpu.CompilerParams(vmem_limit_bytes=63 << 20),
    )(*ins, total)


def per_device(
    block_input, output_grad, document_ids, memory_keys, memory_values, memory_index, memory_reset,
    query_weight, key_weight, value_weight, output_weight, gate_weight, up_weight, down_weight,
    attend_gain, feed_gain,
):
    n = lax.axis_size("fsdp")
    f = lax.axis_index("fsdp")
    micro, T, D = block_input.shape
    FF = gate_weight.shape[2]
    gw = attend_gain.shape[1]
    shards = [w[0] for w in (query_weight, key_weight, value_weight, output_weight, gate_weight, up_weight, down_weight)]
    rows = [s.shape[0] for s in shards]
    fused = 2 * gw == 128 and all(s % 16 == 0 for s in rows)
    vec = attend_gain
    if not fused:
        vec = jnp.zeros((16, D), jnp.bfloat16)
        vec = lax.dynamic_update_slice(vec, jnp.concatenate([attend_gain, feed_gain]), (0, f * gw))
        padded = [jnp.pad(s, ((0, -s.shape[0] % 16), (0, 0))) for s in shards]
        gathered = gather(n, [vec] + padded, 0)
        vec = jnp.sum(gathered[0], axis=0, keepdims=True)
        shards = [g[:, :r].reshape(n * r, g.shape[2]) for g, r in zip(gathered[1:], rows)]
    (so, ig, gsum, e, normed, mixed, n2, hidden, gi, ui, ai, dq, dk, dv) = front(
        n, fused, block_input, output_grad, document_ids, memory_keys, memory_values, memory_index, memory_reset, attend_gain, feed_gain, vec, shards, 2)
    flat = lambda a: a.reshape(micro * T, a.shape[2])
    hid = flat(hidden)
    rd = rows[6]
    if rd % 16:
        hid = jnp.pad(hid.reshape(micro * T, n, rd), ((0, 0), (0, 0), (0, -rd % 16))).reshape(micro * T, -1)
    lhs = [hid, flat(n2), flat(mixed), flat(normed)]
    rhs = [flat(a) for a in (e, gi, ui, ai, dv, dk, dq)]
    order = [(1, 1), (1, 2), (0, 0), (2, 3), (3, 4), (3, 5), (3, 6)]
    steps = [(512, 512, 1024), (1024,), (512,), (1024,), (1024,), (1024,), (512,)]
    sums, total = reduce(n, lhs, rhs, order, gsum, steps, 1)
    gg, gu, gd, go, gv, gk, gq = sums
    return settle(so, ig, gq, gk, gv, go, gg, gu, gd[:rd], total)


def solution(mesh):
    w = P("section", "fsdp", None)
    r = P(None, "fsdp", None)
    v = P("section", "fsdp")
    return jax.shard_map(
        per_device,
        mesh=mesh,
        in_specs=(r, r, P(None, "fsdp"), r, r, r, P(None, "fsdp")) + (w,) * 7 + (v, v),
        out_specs=(P("section", None, "fsdp", None),) * 2 + (w,) * 7 + (v, v),
        check_vma=False,
    )
```

```python
import functools
import math
import jax
import jax.numpy as jnp
from jax import lax
from jax.experimental import pallas as pl
from jax.experimental.pallas import tpu as pltpu
from jax.sharding import PartitionSpec as P

MESH = pl.DeviceIdType.MESH


def layout(n):
    rest=n//2
    R=min(4,rest); C=rest//R
    return R,C

def gather_kernel(n, P, *refs):
    ins=refs[:P]; outs=refs[P:2*P]; bufs=refs[2*P:3*P]
    own_sem,out_sem,s_zu,s_zd,s_yu,s_yd,s_sb,s_ex,r_main,r_sib=refs[3*P:]
    R,C=layout(n)
    sec=lax.axis_index("section"); f=lax.axis_index("fsdp")
    c=f%2; zy=f//2; y=zy%C; z=zy//C
    def dev(zz,yy,cc): return (sec,(zz*C+yy)*2+cc)
    bar=pltpu.get_barrier_semaphore()
    nb=[(z>0,(z-1,y,c)),(z<R-1,(z+1,y,c)),(y>0,(z,y-1,c)),(y<C-1,(z,y+1,c)),(c>=0,(z,y,1-c))]
    for p in range(P):
        pltpu.make_async_copy(ins[p],bufs[p].at[f],own_sem.at[p]).start()
    for cond,d in nb:
        @pl.when(cond)
        def _():
            pl.semaphore_signal(bar,1,device_id=dev(*d),device_id_type=MESH)
    pl.semaphore_wait(bar,sum(jnp.where(cond,1,0) for cond,d in nb))
    pending=[]
    def send(cond,p,zb,yb,target,ssem,rsem):
        blk=(zb*C+yb)*2+c
        k=zb*C+yb
        def mk():
            return pltpu.make_async_remote_copy(bufs[p].at[blk],bufs[p].at[blk],ssem.at[p,k],rsem.at[p,k],device_id=dev(*target),device_id_type=MESH)
        @pl.when(cond)
        def _(): mk().start()
        pending.append((cond,mk))
    def wait_main(cond,p,zb,yb):
        blk=(zb*C+yb)*2+c; k=zb*C+yb
        @pl.when(cond)
        def _():
            pltpu.make_async_remote_copy(bufs[p].at[blk],bufs[p].at[blk],s_sb.at[p,k],r_main.at[p,k],device_id=dev(z,y,1-c),device_id_type=MESH).wait_recv()
    offload = (C==2)
    T=(c>=0)
    def own(p):
        pltpu.make_async_copy(ins[p],bufs[p].at[f],own_sem.at[p]).wait()
        send(y>0,p,z,y,(z,y-1,c),s_yd,r_main)
        send(y<C-1,p,z,y,(z,y+1,c),s_yu,r_main)
        send(z>0,p,z,y,(z-1,y,c),s_zd,r_main)
        send(z<R-1,p,z,y,(z+1,y,c),s_zu,r_main)
        send(T,p,z,y,(z,y,1-c),s_sb,r_sib)
    def z_arrivals(p):
        for d in range(1,R):
            for sign in (-1,1):
                zb=z+sign*d
                ok=(zb>=0)&(zb<R)
                zbc=jnp.clip(zb,0,R-1)
                wait_main(ok,p,zbc,y)
                if sign<0:
                    send(ok&(z<R-1),p,zbc,y,(z+1,y,c),s_zu,r_main)
                else:
                    send(ok&(z>0),p,zbc,y,(z-1,y,c),s_zd,r_main)
                ydo=ok
                if offload: ydo=ok & jnp.logical_not((c==1)&(zbc==(z+1-2*(z%2))))
                send(ydo&(y>0),p,zbc,y,(z,y-1,c),s_yd,r_main)
                send(ydo&(y<C-1),p,zbc,y,(z,y+1,c),s_yu,r_main)
                send(ok,p,zbc,y,(z,y,1-c),s_sb,r_sib)
    def y_arrivals(p, near):
        for dy in range(1,C):
            for sign in (-1,1):
                yb=y+sign*dy
                oky=(yb>=0)&(yb<C)
                ybc=jnp.clip(yb,0,C-1)
                for d in ([0] if near else range(1,R)):
                    for zs in ((0,) if d==0 else (-1,1)):
                        zb=z+zs*d
                        ok=oky&(zb>=0)&(zb<R)
                        zbc=jnp.clip(zb,0,R-1)
                        wait_main(ok,p,zbc,ybc)
                        if C>2:
                            if sign<0: send(ok&(y<C-1),p,zbc,ybc,(z,y+1,c),s_yu,r_main)
                            else: send(ok&(y>0),p,zbc,ybc,(z,y-1,c),s_yd,r_main)
                        if offload and d==0:
                            send(ok&(c==1),p,zbc,ybc,(z+1-2*(z%2),y,c),s_ex,r_main)
                        send(ok,p,zbc,ybc,(z,y,1-c),s_sb,r_sib)
    def finish(p):
        def body(k,_):
            blk=k*2+1-c
            pltpu.make_async_remote_copy(bufs[p].at[blk],bufs[p].at[blk],s_sb.at[p,k],r_sib.at[p,k],device_id=dev(z,y,1-c),device_id_type=MESH).wait_recv()
            return 0
        lax.fori_loop(0,n//2,body,0)
        pltpu.make_async_copy(bufs[p],outs[p],out_sem.at[p]).start()
    LA=2
    for p in range(min(LA,P)): own(p)
    for p in range(P+2):
        if p+LA<P: own(p+LA)
        if p<P: z_arrivals(p)
        if 0<=p-1<P: y_arrivals(p-1,True)
        if 0<=p-2<P:
            y_arrivals(p-2,False)
            finish(p-2)
    for cond,mk in pending:
        @pl.when(cond)
        def _(): mk().wait_send()
    for p in range(P):
        pltpu.make_async_copy(bufs[p],outs[p],out_sem.at[p]).wait()

def gather(n, shards, cid=0):
    P=len(shards)
    R,C=layout(n)
    h=n//2
    D=pltpu.SemaphoreType.DMA
    return pl.pallas_call(functools.partial(gather_kernel,n,P),
        out_shape=[jax.ShapeDtypeStruct((n,)+s.shape,s.dtype) for s in shards],
        in_specs=[pl.BlockSpec(memory_space=pltpu.HBM)]*P,
        out_specs=[pl.BlockSpec(memory_space=pltpu.HBM)]*P,
        scratch_shapes=[pltpu.VMEM((n,)+s.shape,s.dtype) for s in shards]+[D((P,)),D((P,))]+[D((P,h))]*8,
        compiler_params=pltpu.CompilerParams(collective_id=cid,has_side_effects=True,vmem_limit_bytes=60<<20),
    )(*shards)

HEADS=8; HD=128; MQB=64; MEMK=128; EPS=1e-06; MASKED=-1e30
XC=256

def nn(a,b): return jnp.dot(a,b,preferred_element_type=jnp.float32)
def nt(a,b): return lax.dot_general(a,b,(((1,),(1,)),((),())),preferred_element_type=jnp.float32)
def tn(a,b): return lax.dot_general(a,b,(((0,),(0,)),((),())),preferred_element_type=jnp.float32)

def front_kernel(n, fused, micro, T, D, FF, CACHE, NBLK, *refs):
    it=iter(refs)
    take=lambda k:[next(it) for _ in range(k)]
    x_hbm,og_hbm,docs,mk_hbm,mv_hbm,midx,mreset,again,fgain=take(9)
    ins=take(8)
    (so_hbm,ig_hbm,gsum,e_h,normed_h,mixed_h,n2_h,hidden_h,gi_h,ui_h,ai_h,dq_h,dk_h,dv_h)=take(14)
    bufs=take(8)
    (cur,eg,normed,q,k,v,mixed,n2,g,u,hidden,middle,p,rk,rv,grads,mg,acc,so,ig,mask,gain)=take(22)
    (own_sem,in_sem,c_sem,out_sem,xs,xr,es,er)=take(8)
    ag_sems=take(8)
    B16=jnp.bfloat16
    W=[b.reshape(b.shape[0]*b.shape[1],b.shape[2]) if fused else b for b in bufs[1:]]
    Wq,Wk,Wv,Wo,Wg,Wu,Wd=W
    sec=lax.axis_index("section"); f=lax.axis_index("fsdp")
    scale=HD**-0.5
    R,C=layout(n)
    c=f%2; zy=f//2; y=zy%C; z=zy//C
    def dev(d): return (sec,(d[0]*C+d[1])*2+d[2])
    pieces=[(i,None) for i in range(7)]+[(7,j) for j in range(D//XC)]
    NP=len(pieces)
    nb=[(c>=0,(1-sec,f))]
    if fused:
        nb+=[(z>0,dev((z-1,y,c))),(z<R-1,dev((z+1,y,c))),(y>0,dev((z,y-1,c))),(y<C-1,dev((z,y+1,c))),(c>=0,dev((z,y,1-c)))]
    bar=pltpu.get_barrier_semaphore()
    for cond,d in nb:
        @pl.when(cond)
        def _(d=d): pl.semaphore_signal(bar,1,device_id=d,device_id_type=MESH)
    def own_copy(i):
        return pltpu.make_async_copy(ins[i],bufs[i].at[f] if fused else bufs[i],own_sem.at[i])
    for i in range(8):
        if i or not fused: own_copy(i).start()
    if fused:
        both=jnp.concatenate([again[...].astype(jnp.float32),fgain[...].astype(jnp.float32)],axis=1)
        bufs[0][f]=jnp.broadcast_to(both,bufs[0].shape[1:]).astype(B16)
    def load_cur(): return pltpu.make_async_copy(x_hbm,cur,in_sem.at[0])
    def load_eg(): return pltpu.make_async_copy(og_hbm,eg,in_sem.at[0])
    HC=CACHE//2
    def load_cache(m,kv):
        src=(mk_hbm,mv_hbm)[kv]
        return [pltpu.make_async_copy(src.at[m,pl.ds(i*HC,HC)],grads.at[2*kv+i],c_sem.at[2*kv+i]) for i in range(2)]
    @pl.when(sec==0)
    def _(): load_cur().start()
    @pl.when(sec==1)
    def _():
        for kv in range(2):
            for cp in load_cache(0,kv): cp.start()
        load_eg().start()
    def save(j,src,dst,m):
        return pltpu.make_async_copy(src.at[m],dst.at[m],out_sem.at[j,m])
    def xcopy(m,j):
        cs=pl.ds(j*XC,XC)
        return pltpu.make_async_remote_copy(so.at[m,:,cs],cur.at[m,:,cs],xs.at[m,j],xr.at[m,j],device_id=(1-sec,f),device_id_type=MESH)
    def ecopy(m):
        return pltpu.make_async_remote_copy(ig.at[m],eg.at[m],es.at[m],er.at[m],device_id=(1-sec,f),device_id_type=MESH)
    RB=64
    def rows_loop(fn):
        def b(i,_):
            fn(pl.ds(pl.multiple_of(i*RB,RB),RB)); return 0
        lax.fori_loop(0,T//RB,b,0,unroll=T//RB)
    def cols_loop(N,CH,fn):
        def b(i,_):
            fn(pl.ds(pl.multiple_of(i*CH,CH),CH)); return 0
        lax.fori_loop(0,N//CH,b,0,unroll=N//CH)
    def normalize(x,row):
        inv=lax.rsqrt(jnp.mean(x*x,axis=-1,keepdims=True)+EPS)
        return x*inv*gain[row:row+1,:]
    def norm_back(x,cc,row):
        inv=lax.rsqrt(jnp.mean(x*x,axis=-1,keepdims=True)+EPS)
        s=cc*gain[row:row+1,:]
        gsum[row:row+1,:]+=jnp.sum(cc*x*inv,axis=0,keepdims=True)
        return inv*s-x*(inv*inv*inv)*jnp.mean(s*x,axis=-1,keepdims=True)
    def f_norm(m):
        def f1(r): normed[m,r,:]=normalize(cur[m,r,:].astype(jnp.float32),0).astype(B16)
        rows_loop(f1)
        save(0,normed,normed_h,m).start()
    def f_proj(m,dst,w):
        def f2(cs): dst[m,:,cs]=nn(normed[m],w[:,cs]).astype(B16)
        cols_loop(D,256,f2)
    G=4
    def by_block(a,other,hs,m,fn):
        return jnp.concatenate([fn(a[b*MQB:(b+1)*MQB],other[m,b*MEMK:(b+1)*MEMK,hs]) for b in range(NBLK)],axis=0)
    def halves(a): return [a[:,i:i+HD] for i in range(0,T,HD)]
    def row_sum(*parts): return jnp.sum(functools.reduce(jnp.add,parts),axis=-1,keepdims=True)
    def row_max(*parts): return jnp.max(functools.reduce(jnp.maximum,parts),axis=-1,keepdims=True)
    def f_attend(m,recall):
        for h0 in range(0,HEADS,G):
            HS=[slice(h*HD,h*HD+HD) for h in range(h0,h0+G)]
            qs=[q[m,:,hs] for hs in HS]
            s=[nt(a,k[m,:,hs]) for a,hs in zip(qs,HS)]
            if recall: x=[by_block(a,rk,hs,m,nt) for a,hs in zip(qs,HS)]
            ok=mask[m].astype(jnp.float32)>0.5
            s=[jnp.where(ok,a*scale,MASKED) for a in s]
            if recall:
                live=jnp.concatenate([jnp.broadcast_to(mreset[pl.ds(m,1),b:b+1],(MQB,MEMK)) for b in range(NBLK)],axis=0)==0
                x=[jnp.where(live,a*scale,MASKED) for a in x]
                top=[row_max(b,*halves(a)) for a,b in zip(s,x)]
                xe=[jnp.exp(b-t) for b,t in zip(x,top)]
            else: top=[row_max(*halves(a)) for a in s]
            se=[jnp.exp(a-t) for a,t in zip(s,top)]
            if recall: inv=[1.0/row_sum(b,*halves(a)) for a,b in zip(se,xe)]
            else: inv=[1.0/row_sum(*halves(a)) for a in se]
            ps=[(a*i).astype(B16) for a,i in zip(se,inv)]
            o=[nn(a,v[m,:,hs]) for a,hs in zip(ps,HS)]
            if recall:
                pr=[(a*i).astype(B16) for a,i in zip(xe,inv)]
                o=[a+by_block(b,rv,hs,m,nn) for a,b,hs in zip(o,pr,HS)]
            for j in range(G):
                p[m,h0+j,:,0:T]=ps[j]
                if recall: p[m,h0+j,:,T:T+MEMK]=pr[j]
                mixed[m,:,HS[j]]=o[j].astype(B16)
        save(1,mixed,mixed_h,m).start()
    def f_out(m):
        def f3(cs): middle[m,:,cs]=cur[m,:,cs].astype(jnp.float32)+nn(mixed[m],Wo[:,cs])
        cols_loop(D,256,f3)
        def f4(r): n2[m,r,:]=normalize(middle[m,r,:],1).astype(B16)
        rows_loop(f4)
        save(2,n2,n2_h,m).start()
    def f_gate(m):
        def f5(cs):
            a=n2[m]
            gg=nn(a,Wg[:,cs]); uu=nn(a,Wu[:,cs])
            sg=jax.nn.sigmoid(gg)
            act=gg*sg
            g[m,:,cs]=(uu*(sg*(1.0+gg*(1.0-sg)))).astype(B16); u[m,:,cs]=act.astype(B16)
            hidden[m,:,cs]=(act*uu).astype(B16)
        cols_loop(FF,256,f5)
        save(3,hidden,hidden_h,m).start()
    def f_down(m,j):
        cs=pl.ds(j*XC,XC)
        so[m,:,cs]=(middle[m,:,cs]+nn(hidden[m],Wd[:,cs])).astype(B16)
    def recall(m,kv):
        for cp in load_cache(m,kv): cp.wait()
        dst=(rk,rv)[kv]
        def body(b,_):
            idx=midx[m,pl.ds(b,1),:]
            col=jnp.broadcast_to(idx.astype(jnp.float32),(MEMK,MEMK)).T[:,0:1].astype(jnp.int32)
            io=lax.broadcasted_iota(jnp.int32,(MEMK,HC),1)
            rows=nn(jnp.where(io==col,1.0,0.0).astype(B16),grads[2*kv])
            rows=rows+nn(jnp.where(io+HC==col,1.0,0.0).astype(B16),grads[2*kv+1])
            dst[m,pl.ds(pl.multiple_of(b*MEMK,MEMK),MEMK),:]=rows.astype(B16)
            return 0
        lax.fori_loop(0,NBLK,body,0)
        if m+1<micro:
            for cp in load_cache(m+1,kv): cp.start()
    def setup():
        if not fused:
            gain[...]=bufs[0][0,0:8,:].astype(jnp.float32)
            return
        lane=lax.broadcasted_iota(jnp.int32,(8,128),1)
        for e in range(n//2):
            lo=bufs[0][2*e].astype(jnp.float32)[0:8]
            hi=bufs[0][2*e+1].astype(jnp.float32)[0:8]
            cs=pl.ds(e*128,128)
            gain[0:1,cs]=jnp.where(lane<64,lo,pltpu.roll(hi,64,1))[0:1]
            gain[1:2,cs]=jnp.where(lane<64,pltpu.roll(lo,64,1),hi)[0:1]
    def each(fn):
        def b(m,_):
            fn(m); return 0
        return lambda: lax.fori_loop(0,micro,b,0)
    def down(j):
        def go():
            def b(m,_):
                f_down(m,j); xcopy(m,j).start(); return 0
            lax.fori_loop(0,micro,b,0)
        return go
    first={0:[each(f_norm)],1:[each(lambda m:f_proj(m,q,Wq))],2:[each(lambda m:f_proj(m,k,Wk))],
        3:[each(lambda m:f_proj(m,v,Wv)),lambda:f_attend(0,False)],
        4:[lambda:[f_attend(m,False) for m in range(1,micro)],each(f_out)],
        6:[lambda:f_gate(0)]}
    for j in range(D//XC): first[7+j]=[down(j)]
    first[7]=[lambda:[f_gate(m) for m in range(1,micro)]]+first[7]
    units=[(m,kv) for m in range(micro) for kv in range(2)]
    second={i:[functools.partial(recall,*un)] for i,un in enumerate(units)}
    def arrived(i):
        if i==0: setup()
        @pl.when(sec==0)
        def _():
            for fn in first.get(i,[]): fn()
        @pl.when(sec==1)
        def _():
            for fn in second.get(i,[]): fn()
    gsum[...]=jnp.zeros_like(gsum)
    ri=lax.broadcasted_iota(jnp.int32,(T,T),0); ci=lax.broadcasted_iota(jnp.int32,(T,T),1)
    def prepare():
        for m in range(micro):
            row=jnp.broadcast_to(docs[m:m+1,:].astype(jnp.float32),(T,T))
            mask[m]=jnp.where((row==row.T)&(ci<=ri),1.0,0.0).astype(B16)
        @pl.when(sec==0)
        def _(): load_cur().wait()
        @pl.when(sec==1)
        def _(): load_eg().wait()
    pl.semaphore_wait(bar,sum(jnp.where(cond,1,0) for cond,d in nb))
    pending=[]
    if fused:
        s_zu,s_zd,s_yu,s_yd,s_sb,s_ex,r_main,r_sib=ag_sems
        def part(i,blk):
            b,j=pieces[i]
            return bufs[b].at[blk] if j is None else bufs[b].at[blk,:,pl.ds(j*XC,XC)]
        def send(cond,i,zb,yb,target,ssem,rsem):
            blk=(zb*C+yb)*2+c; kk=zb*C+yb
            def mk():
                return pltpu.make_async_remote_copy(part(i,blk),part(i,blk),ssem.at[i,kk],rsem.at[i,kk],device_id=dev(target),device_id_type=MESH)
            @pl.when(cond)
            def _(): mk().start()
            pending.append((cond,mk))
        def wait_main(cond,i,zb,yb):
            blk=(zb*C+yb)*2+c; kk=zb*C+yb
            @pl.when(cond)
            def _():
                pltpu.make_async_remote_copy(part(i,blk),part(i,blk),s_sb.at[i,kk],r_main.at[i,kk],device_id=dev((z,y,1-c)),device_id_type=MESH).wait_recv()
        OFF=lambda i: C==2 and R%2==0
        zx=z+1-2*(z%2)
        true=c>=0
        def own(i):
            b,j=pieces[i]
            if not j and b: own_copy(b).wait()
            send(y>0,i,z,y,(z,y-1,c),s_yd,r_main)
            send(y<C-1,i,z,y,(z,y+1,c),s_yu,r_main)
            send(z>0,i,z,y,(z-1,y,c),s_zd,r_main)
            send(z<R-1,i,z,y,(z+1,y,c),s_zu,r_main)
            send(true,i,z,y,(z,y,1-c),s_sb,r_sib)
        def z_arrivals(i,d):
            if True:
                for sign in (-1,1):
                    zb=z+sign*d
                    ok=(zb>=0)&(zb<R)
                    zbc=jnp.clip(zb,0,R-1)
                    wait_main(ok,i,zbc,y)
                    if sign<0: send(ok&(z<R-1),i,zbc,y,(z+1,y,c),s_zu,r_main)
                    else: send(ok&(z>0),i,zbc,y,(z-1,y,c),s_zd,r_main)
                    ydo=ok&jnp.logical_not((c==1)&(zbc==zx)) if OFF(i) else ok
                    send(ydo&(y>0),i,zbc,y,(z,y-1,c),s_yd,r_main)
                    send(ydo&(y<C-1),i,zbc,y,(z,y+1,c),s_yu,r_main)
                    send(ok,i,zbc,y,(z,y,1-c),s_sb,r_sib)
        def y_arrivals(i,near):
            for dy in range(1,C):
                for sign in (-1,1):
                    yb=y+sign*dy
                    oky=(yb>=0)&(yb<C)
                    ybc=jnp.clip(yb,0,C-1)
                    for d in ([0] if near else range(1,R)):
                        for zs in ((0,) if d==0 else (-1,1)):
                            zb=z+zs*d
                            ok=oky&(zb>=0)&(zb<R)
                            zbc=jnp.clip(zb,0,R-1)
                            wait_main(ok,i,zbc,ybc)
                            if C>2:
                                if sign<0: send(ok&(y<C-1),i,zbc,ybc,(z,y+1,c),s_yu,r_main)
                                else: send(ok&(y>0),i,zbc,ybc,(z,y-1,c),s_yd,r_main)
                            if OFF(i) and d==0:
                                send(ok&(c==1),i,zbc,ybc,(zx,y,c),s_ex,r_main)
                            send(ok,i,zbc,ybc,(z,y,1-c),s_sb,r_sib)
        def finish(i):
            def body(kk,_):
                blk=kk*2+1-c
                pltpu.make_async_remote_copy(part(i,blk),part(i,blk),s_sb.at[i,kk],r_sib.at[i,kk],device_id=dev((z,y,1-c)),device_id_type=MESH).wait_recv()
                return 0
            lax.fori_loop(0,n//2,body,0)
        LA=2
        LAST=R
        for i in range(LA): own(i)
        prepare()
        for i in range(NP+LAST):
            if i+LA<NP: own(i+LA)
            for d in range(1,R):
                if 0<=i-d+1<NP: z_arrivals(i-d+1,d)
            if 0<=i-1<NP: y_arrivals(i-1,True)
            if 0<=i-LAST+1<NP:
                y_arrivals(i-LAST+1,False)
                finish(i-LAST+1)
                arrived(i-LAST+1)
    else:
        prepare()
        for i in range(NP):
            b,j=pieces[i]
            if not j: own_copy(b).wait()
            arrived(i)
    for cond,mk in pending:
        @pl.when(cond)
        def _(mk=mk): mk().wait_send()
    @pl.when(sec==1)
    def _():
        def forward(m,_):
            for j in range(D//XC): xcopy(m,j).wait_recv()
            f_norm(m)
            f_proj(m,q,Wq); f_proj(m,k,Wk); f_proj(m,v,Wv)
            f_attend(m,True)
            f_out(m)
            f_gate(m)
            for j in range(D//XC): f_down(m,j)
            return 0
        lax.fori_loop(0,micro,forward,0)
    def gsave(j,i,dst,m): return pltpu.make_async_copy(grads.at[i,pl.ds(pl.multiple_of(m*T,T),T)],dst.at[m],out_sem.at[j,m])
    def b_attend(m,ms,recall):
        for h0 in range(0,HEADS,G):
            HS=[slice(h*HD,h*HD+HD) for h in range(h0,h0+G)]
            mh=[normed[m,:,hs] for hs in HS]
            ps=[p[m,h,:,0:T] for h in range(h0,h0+G)]
            pg=[nt(a,v[m,:,hs]) for a,hs in zip(mh,HS)]
            if recall:
                pr=[p[m,h,:,T:T+MEMK].astype(jnp.float32) for h in range(h0,h0+G)]
                rg=[by_block(a,rv,hs,m,nt) for a,hs in zip(mh,HS)]
            dv=[tn(a,b) for a,b in zip(ps,mh)]
            pf=[a.astype(jnp.float32) for a in ps]
            if recall:
                w=[row_sum(c_*d_,*halves(a*b)) for a,b,c_,d_ in zip(pf,pg,pr,rg)]
                dr=[(a*(b-t)).astype(B16) for a,b,t in zip(pr,rg,w)]
            else: w=[row_sum(*halves(a*b)) for a,b in zip(pf,pg)]
            ds=[(a*(b-t)).astype(B16) for a,b,t in zip(pf,pg,w)]
            dq=[nn(a,k[m,:,hs]) for a,hs in zip(ds,HS)]
            if recall: dq=[a+by_block(b,rk,hs,m,nn) for a,b,hs in zip(dq,dr,HS)]
            dk=[tn(a,q[m,:,hs]) for a,hs in zip(ds,HS)]
            for j in range(G):
                grads[3,ms,HS[j]]=dv[j].astype(B16)
                grads[1,ms,HS[j]]=(dq[j]*scale).astype(B16)
                grads[2,ms,HS[j]]=(dk[j]*scale).astype(B16)
    def backward(m,_):
        @pl.when(sec==0)
        def _(): ecopy(m).wait_recv()
        save(4,so,so_hbm,m).start()
        save(5,eg,e_h,m).start()
        def b1(cs):
            hg=nt(eg[m],Wd[cs,:])
            u[m,:,cs]=(hg*u[m,:,cs].astype(jnp.float32)).astype(B16)
            g[m,:,cs]=(hg*g[m,:,cs].astype(jnp.float32)).astype(B16)
        cols_loop(FF,256,b1)
        save(6,g,gi_h,m).start(); save(7,u,ui_h,m).start()
        def b2(cs): acc[:,cs]=nt(g[m],Wg[cs,:])+nt(u[m],Wu[cs,:])
        cols_loop(D,256,b2)
        ms=pl.ds(pl.multiple_of(m*T,T),T)
        def b3(r):
            t_=eg[m,r,:].astype(jnp.float32)+norm_back(middle[m,r,:],acc[r,:],1)
            mg[r,:]=t_; grads[0,pl.ds(pl.multiple_of(m*T,T)+r.start,RB),:]=t_.astype(B16)
        rows_loop(b3)
        gsave(8,0,ai_h,m).start()
        save(0,normed,normed_h,m).wait()
        def b4(cs): normed[m,:,cs]=nt(grads[0,ms,:],Wo[cs,:]).astype(B16)
        cols_loop(D,256,b4)
        pl.when(sec==0)(lambda: b_attend(m,ms,False))
        pl.when(sec==1)(lambda: b_attend(m,ms,True))
        gsave(9,1,dq_h,m).start(); gsave(10,2,dk_h,m).start(); gsave(11,3,dv_h,m).start()
        def b5(cs): acc[:,cs]=nt(grads[1,ms,:],Wq[cs,:])+nt(grads[2,ms,:],Wk[cs,:])+nt(grads[3,ms,:],Wv[cs,:])
        cols_loop(D,256,b5)
        def b6(r): ig[m,r,:]=(mg[r,:]+norm_back(cur[m,r,:].astype(jnp.float32),acc[r,:],0)).astype(B16)
        rows_loop(b6)
        @pl.when(sec==1)
        def _(): ecopy(m).start()
        save(12,ig,ig_hbm,m).start()
        return 0
    lax.fori_loop(0,micro,backward,0)
    for m in range(micro):
        @pl.when(sec==0)
        def _():
            for j in range(D//XC): xcopy(m,j).wait_send()
        @pl.when(sec==1)
        def _(): ecopy(m).wait_send()
        for j,(s,d) in enumerate([(mixed,mixed_h),(n2,n2_h),(hidden,hidden_h),(so,so_hbm),(eg,e_h),(g,gi_h),(u,ui_h)],1):
            save(j,s,d,m).wait()
        for j,i,d in ((8,0,ai_h),(9,1,dq_h),(10,2,dk_h),(11,3,dv_h)):
            gsave(j,i,d,m).wait()
        save(12,ig,ig_hbm,m).wait()

def front(n, fused, x, og, docs, mk, mv, midx, mreset, again, fgain, vec, weights, cid=2):
    micro,T,D=x.shape
    FF=weights[4].shape[1]
    CACHE=mk.shape[1]; NBLK=midx.shape[1]
    B=jnp.bfloat16; F=jnp.float32
    V=pltpu.VMEM
    act=(micro,T,D); fact=(micro,T,FF)
    S=jax.ShapeDtypeStruct
    outs=[S(act,B),S(act,B),S((8,D),F),S(act,B),S(act,B),S(act,B),S(act,B),S(fact,B),S(fact,B),S(fact,B),S(act,B),S(act,B),S(act,B),S(act,B)]
    ws=[vec]+list(weights)
    scratch=[V((n,16,128),B) if fused else V(vec.shape,B)]
    scratch+=[V((n,)+w.shape if fused else w.shape,B) for w in weights]
    scratch+=[V(act,B)]*8+[V(fact,B)]*3+[V(act,F),V((micro,HEADS,T,T+MEMK),B),V((micro,NBLK*MEMK,D),B),V((micro,NBLK*MEMK,D),B),V((4,micro*T,D),B),V((T,D),F),V((T,D),F),V(act,B),V(act,B),V((micro,T,T),B),V((8,D),F)]
    DM=pltpu.SemaphoreType.DMA
    NP=7+D//XC
    scratch+=[DM((8,)),DM((2,)),DM((4,)),DM((13,micro)),DM((micro,D//XC)),DM((micro,D//XC)),DM((micro,)),DM((micro,))]
    scratch+=[DM((NP,n//2) if fused else (1,))]*8
    HB=pl.BlockSpec(memory_space=pltpu.HBM); VB=pl.BlockSpec(memory_space=pltpu.VMEM)
    return pl.pallas_call(functools.partial(front_kernel,n,fused,micro,T,D,FF,CACHE,NBLK),
        out_shape=outs,
        in_specs=[HB,HB,VB,HB,HB,VB,VB,VB,VB]+[HB]*8,
        out_specs=[HB,HB,VB]+[HB]*11,
        scratch_shapes=scratch,
        compiler_params=pltpu.CompilerParams(collective_id=cid,has_side_effects=True,vmem_limit_bytes=64<<20),
    )(x,og,docs,mk,mv,midx,mreset,again,fgain,*ws)


COLS=1024
NDIRECT=2
def plan(n, lhs_shapes, rhs_shapes, weights, steps):
    pieces=[]
    for w,(l,r) in enumerate(weights):
        rows=lhs_shapes[l][1]//n; N=rhs_shapes[r][1]
        c0=0
        for step in steps[w]:
            pieces.append((w,rows,c0,step)); c0+=step
        while c0<N:
            step=min(steps[w][-1],N-c0)
            pieces.append((w,rows,c0,step)); c0+=step
    return pieces

def reduce_kernel(n, tok, lhs_shapes, rhs_shapes, weights, pieces, vec_rows, SLOTS, *refs):
    NP=len(pieces); NL=len(lhs_shapes); NR=len(rhs_shapes); NW=len(weights)
    R,C=layout(n); H=n//2
    it=iter(refs)
    take=lambda k:[next(it) for _ in range(k)]
    lhs=take(NL); rhs=take(NR); vec=next(it)
    outs=take(NW); vec_out=next(it)
    ring=next(it); tbuf=take(NL)
    keep=take(NP); sibr=take(NP); yr=take(NP); xr=take(NP); zu=take(NP); zd=take(NP); fin=take(NP)
    shapes=sorted({p[1] for p in pieces})
    stage_of=dict(zip(shapes,take(len(shapes))))
    vecb=next(it); vecr=next(it)
    (ld_sem,sib_s,sib_r,y_s,y_r,x_s,x_r,zu_s,zu_r,zd_s,zd_r,v_s,v_r,o_s)=take(14)
    sec=lax.axis_index("section"); f=lax.axis_index("fsdp")
    c=f%2; zy=f//2; y=zy%C; z=zy//C
    OFF=lambda i: C==2 and R%2==0
    zx=z+1-2*(z%2)
    def dev(zz,yy,cc): return (sec,(zz*C+yy)*2+cc)
    def rcopy(src,dst,ss,rs,d):
        return pltpu.make_async_remote_copy(src,dst,ss,rs,device_id=dev(*d),device_id_type=MESH)
    LOGN=n.bit_length()-1
    nb=[]
    nb.append((c>=0,dev(z,y,1-c)))
    for k in range(1,C): nb.append((c>=0,dev(z,lax.rem(y+k,C),c)))
    for k in range(1,R): nb.append((c>=0,dev(lax.rem(z+k,R),y,c)))
    bar=pltpu.get_barrier_semaphore()
    loads=[]
    def parts(ref,shape):
        return [(ref,c0,min(COLS,shape[1]-c0)) for c0 in range(0,shape[1],COLS)]
    load_id={}
    def need(kind,i):
        key=(kind,i)
        if key in load_id: return
        ref=lhs[i] if kind=="l" else rhs[i]
        sh=lhs_shapes[i] if kind=="l" else rhs_shapes[i]
        ids=[]
        for pr in parts(ref,sh):
            ids.append(len(loads)); loads.append(pr)
        load_id[key]=ids
    for l,r in weights:
        need("l",l); need("r",r)
    issued=[0]; freed=set()
    def load_copy(k):
        ref,c0,w=loads[k]
        return pltpu.make_async_copy(ref.at[:,pl.ds(c0,w)],ring.at[k%SLOTS,:,pl.ds(0,w)],ld_sem.at[k%SLOTS])
    def pump():
        while issued[0]<len(loads) and (issued[0]<SLOTS or (issued[0]-SLOTS) in freed):
            load_copy(issued[0]).start(); issued[0]+=1
    pump()
    for cond,d in nb:
        @pl.when(cond)
        def _(): pl.semaphore_signal(bar,1,device_id=d,device_id_type=MESH)
    waited=set()
    def wait_load(k):
        if k not in waited:
            load_copy(k).wait(); waited.add(k)
    transposed=set()
    def ensure_lhs(l):
        if l in transposed: return
        transposed.add(l)
        for j,k in enumerate(load_id[("l",l)]):
            wait_load(k)
            w=loads[k][2]
            CH=256
            def body(i,_,k=k,j=j):
                o=pl.multiple_of(i*CH,CH)
                tbuf[l][pl.ds(pl.multiple_of(j*COLS+o,CH),CH),:]=ring[k%SLOTS,:,pl.ds(o,CH)].T
                return 0
            lax.fori_loop(0,w//CH,body,0)
            freed.add(k)
        pump()
    last_use={}
    for i,(w,rows,c0,nc) in enumerate(pieces):
        l,r=weights[w]
        last_use[load_id[("r",r)][c0//COLS]]=i
    sends={}
    cur_piece=[0]
    stage_use={}
    def compute(i):
        w,rows,c0,nc=pieces[i]
        l,r=weights[w]
        ensure_lhs(l)
        k=load_id[("r",r)][c0//COLS]
        wait_load(k)
        lc=c0%COLS
        u=stage_use.get(rows,0); stage_use[rows]=u+1
        st=stage_of[rows].at[u%2,:,:,pl.ds(0,nc)]
        if u>=2: sib_waits[rows].pop(0)()
        T4=tbuf[l].reshape(H,2,rows,tok)
        CH=256
        for which,dst in ((1-c,st),(c,keep[i])):
            def body(j,_,which=which,dst=dst):
                o=pl.multiple_of(j*CH,CH)
                a=T4[:,which].reshape(H*rows,tok)
                b=ring[k%SLOTS,:,pl.ds(pl.multiple_of(lc+o,CH),CH)]
                res=jnp.dot(a,b,preferred_element_type=jnp.float32).astype(jnp.bfloat16)
                dst[:,:,pl.ds(o,CH)]=res.reshape(H,rows,CH)
                return 0
            lax.fori_loop(0,nc//CH,body,0)
            if dst is not keep[i]:
                cp=rcopy(st,sibr[i],sib_s.at[i],sib_r.at[i],(z,y,1-c))
                cp.start()
                sib_waits.setdefault(rows,[]).append(cp.wait_send)
        if last_use[k]==i:
            freed.add(k); pump()
    sib_waits={}
    def add_into(dst,src,rows):
        def body(j,_):
            o=pl.multiple_of(j*16,16)
            dst[pl.ds(o,16),:]=dst[pl.ds(o,16),:]+src[pl.ds(o,16),:]
            return 0
        lax.fori_loop(0,rows//16,body,0)
    def send(tag,cond,cp):
        if cond is None: cp().start()
        else:
            @pl.when(cond)
            def _(): cp().start()
        sends.setdefault(tag,[]).append((cond,cp))
    def sib_add(i):
        w,rows,c0,nc=pieces[i]
        rcopy(sibr[i],sibr[i],sib_s.at[i],sib_r.at[i],(z,y,1-c)).wait_recv()
        def body(k,_):
            add_into(keep[i].at[k],sibr[i].at[k],rows)
            return 0
        lax.fori_loop(0,H,body,0)
        offload=OFF(i)
        if offload:
            send((i,'y'),c==1,lambda: rcopy(keep[i].at[zx*C+1-y],xr[i],x_s.at[i],x_r.at[i],(zx,y,c)))
        for kz in range(R-1,-1,-1):
            zt=lax.rem(z+kz,R)
            for ky in range(1,C):
                yt=lax.rem(y+ky,C)
                slot=C-1-ky
                cp=lambda zt=zt,yt=yt,slot=slot: rcopy(keep[i].at[zt*C+yt],yr[i].at[slot,zt],y_s.at[i,slot,zt],y_r.at[i,slot,zt],(z,yt,c))
                if offload and kz==0:
                    continue
                send((i,'y'),(jnp.logical_not((c==1)&(zt==zx))) if offload else None,cp)
    def x_add(i):
        w,rows,c0,nc=pieces[i]
        if not OFF(i): return
        @pl.when(c==1)
        def _():
            rcopy(xr[i],xr[i],x_s.at[i],x_r.at[i],(zx,y,c)).wait_recv()
            add_into(keep[i].at[z*C+1-y],xr[i],rows)
        send((i,'y'),None,lambda: rcopy(keep[i].at[z*C+1-y],yr[i].at[0,z],y_s.at[i,0,z],y_r.at[i,0,z],(z,1-y,c)))
    def y_add(i):
        w,rows,c0,nc=pieces[i]
        offload=OFF(i)
        for kz in range(R-1,-1,-1):
            zt=lax.rem(z+kz,R)
            for slot in range(C-1):
                def go(zt=zt,slot=slot):
                    rcopy(yr[i].at[slot,zt],yr[i].at[slot,zt],y_s.at[i,slot,zt],y_r.at[i,slot,zt],(z,y,1-c)).wait_recv()
                    add_into(keep[i].at[zt*C+y],yr[i].at[slot,zt],rows)
                if offload and kz!=0:
                    pl.when(jnp.logical_not((c==1)&(zt==zx)))(go)
                else: go()
    direct=lambda i: i>=NP-NDIRECT
    def z_step(i,s):
        w,rows,c0,nc=pieces[i]
        if direct(i):
            if s: return
            for k in range(1,R):
                t=lax.rem(z+k,R)
                send((i,0),None,lambda k=k,t=t: rcopy(keep[i].at[t*C+y],zu[i].at[R-1-k],zu_s.at[i,k-1],zu_r.at[i,R-1-k],(t,y,c)))
            return
        def line(zs,up):
            rb,rr,ss=(zu,zu_r,zu_s) if up else (zd,zd_r,zd_s)
            first=(zs==0) if up else (zs==R-1)
            targets=range(R-1,zs,-1) if up else range(0,zs)
            nxt=zs+1 if up else zs-1
            cps=[]
            for t in targets:
                k=abs(t-zs)
                cps.append((k,lambda t=t,k=k: rcopy(keep[i].at[t*C+y],rb[i].at[k-1],ss.at[i,k-1],rr.at[i,k-1],(nxt,y,c)),t))
            def go():
                for k,cp,t in cps:
                    if not first:
                        rcopy(rb[i].at[k],rb[i].at[k],ss.at[i,k],rr.at[i,k],(zs,y,1-c)).wait_recv()
                        add_into(keep[i].at[t*C+y],rb[i].at[k],rows)
                    cp().start()
            pl.when(z==zs)(go)
            for k,cp,t in cps: sends.setdefault((i,zs if up else R-1-zs),[]).append((z==zs,cp))
        line(s,True)
        line(R-1-s,False)
    def final(i):
        w,rows,c0,nc=pieces[i]
        blk=z*C+y
        if direct(i):
            for k in range(R-1):
                rcopy(zu[i].at[k],zu[i].at[k],zu_s.at[i,k],zu_r.at[i,k],(z,y,1-c)).wait_recv()
            def body(j,_):
                o=pl.ds(pl.multiple_of(j*16,16),16)
                a=keep[i][blk,o,:].astype(jnp.float32)
                for k in range(R-1): a=a+zu[i][k,o,:].astype(jnp.float32)
                fin[i][o,:]=a.astype(jnp.bfloat16)
                return 0
            lax.fori_loop(0,rows//16,body,0)
            pltpu.make_async_copy(fin[i],outs[w].at[:,pl.ds(c0,nc)],o_s.at[i]).start()
            return
        @pl.when(z>0)
        def _():
            rcopy(zu[i].at[0],zu[i].at[0],zu_s.at[i,0],zu_r.at[i,0],(z,y,1-c)).wait_recv()
        @pl.when(z<R-1)
        def _():
            rcopy(zd[i].at[0],zd[i].at[0],zd_s.at[i,0],zd_r.at[i,0],(z,y,1-c)).wait_recv()
        def body(j,_):
            o=pl.ds(pl.multiple_of(j*16,16),16)
            a=keep[i][blk,o,:].astype(jnp.float32)
            a=a+jnp.where(z>0,zu[i][0,o,:].astype(jnp.float32),0.0)+jnp.where(z<R-1,zd[i][0,o,:].astype(jnp.float32),0.0)
            fin[i][o,:]=a.astype(jnp.bfloat16)
            return 0
        lax.fori_loop(0,rows//16,body,0)
        pltpu.make_async_copy(fin[i],outs[w].at[:,pl.ds(c0,nc)],o_s.at[i]).start()
    def vec_step(k):
        if k==0: first_vec.wait()
        if k>0:
            vcopy(k-1).wait()
            vecb[k]=vecb[k-1]+vecr[k-1]
        if k<LOGN: vcopy(k).start()
        else:
            cp=pltpu.make_async_copy(vecb.at[LOGN],vec_out,o_s.at[NP]); cp.start()
    def vcopy(k):
        return pltpu.make_async_remote_copy(vecb.at[k],vecr.at[k],v_s.at[k],v_r.at[k],device_id=(sec,f^(1<<k)),device_id_type=MESH)
    first_vec=pltpu.make_async_copy(vec,vecb.at[0],o_s.at[NP]); first_vec.start()
    pl.semaphore_wait(bar,sum(jnp.where(cond,1,0) for cond,d in nb))
    def end_sends(tag):
        for cond,cp in sends.pop(tag,[]):
            if cond is None: cp().wait_send()
            else:
                @pl.when(cond)
                def _(cp=cp): cp().wait_send()
    LAGY=3
    for t in range(NP+LAGY+R+1):
        if 0<=t-2<NP: x_add(t-2)
        if t<NP: compute(t)
        if 0<=t-1<NP: sib_add(t-1)
        if t<=LOGN: vec_step(t)
        if 0<=t-LAGY<NP: y_add(t-LAGY)
        for s in range(R):
            i=t-LAGY-s
            if 0<=i<NP: z_step(i,s)
        i=t-LAGY-R
        if 0<=i<NP and not direct(i): final(i)
        i=t-LAGY-1
        if 0<=i<NP and direct(i): final(i)
        end_sends((t-LAGY-1,'y'))
        for s in range(R): end_sends((t-LAGY-s-2,s))
    for q in sib_waits.values():
        for wfn in q: wfn()
    for tag in list(sends): end_sends(tag)
    for i in range(NP):
        w,rows,c0,nc=pieces[i]
        pltpu.make_async_copy(fin[i],outs[w].at[:,pl.ds(c0,nc)],o_s.at[i]).wait()
    pltpu.make_async_copy(vecb.at[LOGN],vec_out,o_s.at[NP]).wait()

def reduce(n, lhs, rhs, weights, vec, steps, cid=1, SLOTS=6):
    tok=lhs[0].shape[0]
    ls=[a.shape for a in lhs]; rs=[a.shape for a in rhs]
    pieces=plan(n,ls,rs,weights,steps)
    R,C=layout(n); H=n//2
    NP=len(pieces)
    LOGN=n.bit_length()-1
    D=pltpu.SemaphoreType.DMA
    B=jnp.bfloat16
    V=pltpu.VMEM
    shapes=sorted({(p[1],max(o[3] for o in pieces if o[1]==p[1])) for p in pieces})
    scratch=[V((SLOTS,tok,COLS),B)]+[V((s[1],tok),B) for s in ls]
    scratch+=[V((H,p[1],p[3]),B) for p in pieces]
    scratch+=[V((H,p[1],p[3]),B) for p in pieces]
    scratch+=[V((C-1,R,p[1],p[3]),B) for p in pieces]
    scratch+=[V((p[1],p[3]) if C==2 else (16,128),B) for p in pieces]
    scratch+=[V((R-1,p[1],p[3]),B) for p in pieces]*2
    scratch+=[V((p[1],p[3]),B) for p in pieces]
    scratch+=[V((2,H)+s,B) for s in shapes]
    scratch+=[V((LOGN+1,)+vec.shape,vec.dtype),V((LOGN,)+vec.shape,vec.dtype)]
    scratch+=[D((SLOTS,)),D((NP,)),D((NP,)),D((NP,C-1,R)),D((NP,C-1,R)),D((NP,)),D((NP,)),D((NP,R-1)),D((NP,R-1)),D((NP,R-1)),D((NP,R-1)),D((LOGN,)),D((LOGN,)),D((NP+1,))]
    HB=pl.BlockSpec(memory_space=pltpu.HBM)
    res=pl.pallas_call(functools.partial(reduce_kernel,n,tok,ls,rs,weights,pieces,vec.shape[0],SLOTS),
        out_shape=[jax.ShapeDtypeStruct((ls[l][1]//n,rs[r][1]),B) for l,r in weights]+[jax.ShapeDtypeStruct(vec.shape,vec.dtype)],
        in_specs=[HB]*(len(lhs)+len(rhs)+1),
        out_specs=[HB]*(len(weights)+1),
        scratch_shapes=scratch,
        compiler_params=pltpu.CompilerParams(collective_id=cid,has_side_effects=True,vmem_limit_bytes=63<<20),
    )(*lhs,*rhs,vec)
    return res[:-1],res[-1]


def settle_kernel(count, gw, *refs):
    ins = refs[:count]
    total = refs[count]
    outs = refs[count + 1 : 2 * count + 1]
    again, fgain = refs[2 * count + 1 : 2 * count + 3]
    held = refs[2 * count + 3 : 3 * count + 3]
    in_sem, out_sem = refs[3 * count + 3 :]
    load = [pltpu.make_async_copy(a, h, in_sem.at[i]) for i, (a, h) in enumerate(zip(ins, held))]
    store = [pltpu.make_async_copy(h, b.at[0], out_sem.at[i]) for i, (h, b) in enumerate(zip(held, outs))]
    for cp in load:
        cp.start()
    width = total.shape[1]
    f = lax.axis_index("fsdp")
    mine = pltpu.roll(total[...], lax.rem(width - f * gw, width), 1)
    again[...] = mine[0:1, 0:gw].astype(again.dtype)
    fgain[...] = mine[1:2, 0:gw].astype(fgain.dtype)
    for cp, out in zip(load, store):
        cp.wait()
        out.start()
    for cp in store:
        cp.wait()


def settle(*arrays):
    *ins, total = arrays
    gw = total.shape[1] // lax.axis_size("fsdp")
    HB = pl.BlockSpec(memory_space=pltpu.HBM)
    VB = pl.BlockSpec(memory_space=pltpu.VMEM)
    S = jax.ShapeDtypeStruct
    return pl.pallas_call(
        functools.partial(settle_kernel, len(ins), gw),
        out_shape=[S((1,) + a.shape, a.dtype) for a in ins] + [S((1, gw), jnp.bfloat16)] * 2,
        in_specs=[HB] * len(ins) + [VB],
        out_specs=[HB] * len(ins) + [VB] * 2,
        scratch_shapes=[pltpu.VMEM(a.shape, a.dtype) for a in ins] + [pltpu.SemaphoreType.DMA((len(ins),))] * 2,
        compiler_params=pltpu.CompilerParams(vmem_limit_bytes=63 << 20),
    )(*ins, total)


def per_device(
    block_input, output_grad, document_ids, memory_keys, memory_values, memory_index, memory_reset,
    query_weight, key_weight, value_weight, output_weight, gate_weight, up_weight, down_weight,
    attend_gain, feed_gain,
):
    n = lax.axis_size("fsdp")
    f = lax.axis_index("fsdp")
    micro, T, D = block_input.shape
    FF = gate_weight.shape[2]
    gw = attend_gain.shape[1]
    shards = [w[0] for w in (query_weight, key_weight, value_weight, output_weight, gate_weight, up_weight, down_weight)]
    rows = [s.shape[0] for s in shards]
    fused = 2 * gw == 128 and all(s % 16 == 0 for s in rows)
    vec = attend_gain
    if not fused:
        vec = jnp.zeros((16, D), jnp.bfloat16)
        vec = lax.dynamic_update_slice(vec, jnp.concatenate([attend_gain, feed_gain]), (0, f * gw))
        padded = [jnp.pad(s, ((0, -s.shape[0] % 16), (0, 0))) for s in shards]
        gathered = gather(n, [vec] + padded, 0)
        vec = jnp.sum(gathered[0], axis=0, keepdims=True)
        shards = [g[:, :r].reshape(n * r, g.shape[2]) for g, r in zip(gathered[1:], rows)]
    (so, ig, gsum, e, normed, mixed, n2, hidden, gi, ui, ai, dq, dk, dv) = front(
        n, fused, block_input, output_grad, document_ids, memory_keys, memory_values, memory_index, memory_reset, attend_gain, feed_gain, vec, shards, 2)
    flat = lambda a: a.reshape(micro * T, a.shape[2])
    hid = flat(hidden)
    rd = rows[6]
    if rd % 16:
        hid = jnp.pad(hid.reshape(micro * T, n, rd), ((0, 0), (0, 0), (0, -rd % 16))).reshape(micro * T, -1)
    lhs = [hid, flat(n2), flat(mixed), flat(normed)]
    rhs = [flat(a) for a in (e, gi, ui, ai, dv, dk, dq)]
    order = [(1, 1), (1, 2), (0, 0), (2, 3), (3, 4), (3, 5), (3, 6)]
    steps = [(512, 512, 1024), (1024,), (512,), (1024,), (1024,), (1024,), (512,)]
    sums, total = reduce(n, lhs, rhs, order, gsum, steps, 1)
    gg, gu, gd, go, gv, gk, gq = sums
    return settle(so, ig, gq, gk, gv, go, gg, gu, gd[:rd], total)


def solution(mesh):
    w = P("section", "fsdp", None)
    r = P(None, "fsdp", None)
    v = P("section", "fsdp")
    return jax.shard_map(
        per_device,
        mesh=mesh,
        in_specs=(r, r, P(None, "fsdp"), r, r, r, P(None, "fsdp")) + (w,) * 7 + (v, v),
        out_specs=(P("section", None, "fsdp", None),) * 2 + (w,) * 7 + (v, v),
        check_vma=False,
    )
```
